32 devices in a mesh: expert: 4 (over y, x), fsdp: 8 (over z, core).
Axes of the slice: x: 2, y: 2, z: 4, core: 2. Of those that a mesh axis runs over, the one named last changes fastest.
Arguments:
- tokens: bfloat16 [16384, 768], P(('expert', 'fsdp')), may hold values from -6 to 6
- past_logits: float32 [16384, 8], P(('expert', 'fsdp')), may hold values from -3 to 3
- routes: int32 [16384, 2], P(('expert', 'fsdp')), may hold values from 0 to 7, all different within a row; in each aligned block of 512 rows (0 to 511, 512 to 1023, ...) at most 128 rows name the same one
- lengths: int32 [4, 4], P('expert'), may hold values from 1 to 3840, 4096 in all within a row
- projector: bfloat16 [768, 2304], P('fsdp'), may hold values from -0.21875 to 0.21875
- collector: bfloat16 [768, 768], P('fsdp'), may hold values from -1.75 to 1.75
- router: bfloat16 [768, 8], P('fsdp'), may hold values from -0.109375 to 0.109375
- blender: bfloat16 [768, 4], P('fsdp'), may hold values from -0.21875 to 0.21875
- constants: bfloat16 [768, 2], P('fsdp'), may hold values from -5 to 5
- first_gain: bfloat16 [768], P('fsdp'), may hold values from 0.5 to 1.5
- second_gain: bfloat16 [768], P('fsdp'), may hold values from 0.5 to 1.5
- carryover: float32 [8, 8], replicated, may hold values from -2 to 2
- gating: bfloat16 [4, 768, 2048], P('expert', 'fsdp'), may hold values from -0.21875 to 0.21875
- upward: bfloat16 [4, 768, 2048], P('expert', 'fsdp'), may hold values from -0.21875 to 0.21875
- downward: bfloat16 [4, 768, 2048], P('expert', 'fsdp'), may hold values from -0.25 to 0.25
- cotangent: bfloat16 [16384, 768], P(('expert', 'fsdp')), may hold values from -6 to 6
Outputs:
- layer_output: bfloat16 [16384, 768], P(('expert', 'fsdp'))
- gradient_tokens: bfloat16 [16384, 768], P(('expert', 'fsdp'))
- gradient_logits: float32 [16384, 8], P(('expert', 'fsdp'))
- gradient_projector: float32 [768, 2304], P('fsdp')
- gradient_collector: float32 [768, 768], P('fsdp')
- gradient_router: float32 [768, 8], P('fsdp')
- gradient_blender: float32 [768, 4], P('fsdp')
- gradient_constants: float32 [768, 2], P('fsdp')
- gradient_first: float32 [768], P('fsdp')
- gradient_second: float32 [768], P('fsdp')
- gradient_carryover: float32 [8, 8], replicated
- gradient_gating: float32 [4, 768, 2048], P('expert', 'fsdp')
- gradient_upward: float32 [4, 768, 2048], P('expert', 'fsdp')
- gradient_downward: float32 [4, 768, 2048], P('expert', 'fsdp')
The draws below stay inside these ranges and needn't reach their ends.
Inputs may be any that keep to these rules, and one draw needn't show every extreme that they name: `routes`: each row names two different experts: 0 to 3 are feed-forward experts, 4 the zero expert, 5 the copy expert, 6 and 7 the constant experts. Among the 512 rows of one device no expert is named more than 128 times, and in every draw some expert is named exactly 128 times among the rows of some device. Each row holds the lengths of the 4 documents packed in order into one sequence; they sum to 4096, and the longest is exactly 3840.
All inputs are finite; a program needn't handle non-finite values.
Results may differ from the reference program's by a relative error of at most 0.02.
Values may be sent and summed in bfloat16 or wider, within the bound.
No kernel may reach another device: no remote copies, remote signals or barrier semaphores. Data moves between devices by JAX's collectives and lax.ppermute only.
A program may use at most 256 MiB of HBM per device.

```python
import math
import jax
import jax.numpy as jnp
import numpy as np
from jax import lax

D = 768
H = 12
HD = 64
FF = 2048
TOK_DEV = 512
WINDOW = 1024
DOCS = 4
E = 4
NEXP = 8
CAP = 128
SEQ = 4096
SEQS = 4
TOKENS = 16384


def steps_of(own_key, shape, shards, low, top_value):
    level, own = 1.0, jax.random.fold_in(own_key, 6)
    for dim, shards_of in shards:
        draws = jnp.exp(jax.random.uniform(jax.random.fold_in(own, dim), (shards_of,), jnp.float32, low / len(shards), top_value / len(shards)))
        level = level * jnp.repeat(draws, shape[dim] // shards_of).reshape([-1 if axis == dim else 1 for axis in range(len(shape))])
    return level


def profile(number_of, total, most, lean):
    portions = [(1 << 20) // math.isqrt(grade ** lean) + 1 for grade in range(2, number_of + 1)]
    spare, given = total - most - (number_of - 1), [1] * (number_of - 1)
    while spare > 0:
        movable = [i for i in range(number_of - 1) if given[i] < most]
        whole, remaining = sum([portions[i] for i in movable]), spare
        for i in movable:
            more = min(most - given[i], max(1, remaining * portions[i] // whole), spare)
            given[i] = given[i] + more
            spare = spare - more
    return np.array([most] + given)


def ragged_sizes(rng, amount, total, most, lean):
    if amount == 2:
        one = jax.random.randint(rng, (), max(1, total - most), min(most, total - 1) + 1)
        return jnp.stack([one, total - one])
    sizes = jnp.asarray(profile(amount, total, most, lean), jnp.int32)
    pairs = (amount - 1) // 2
    source_of, receiver = sizes[1:1 + 2 * pairs:2], sizes[2:2 + 2 * pairs:2]
    room = jnp.minimum(source_of - 1, most - receiver)
    moved = jax.random.randint(jax.random.fold_in(rng, 1), (pairs,), 0, 1 << 20) % (room + 1)
    sizes = sizes.at[1:1 + 2 * pairs:2].set(source_of - moved).at[2:2 + 2 * pairs:2].set(receiver + moved)
    return sizes[jax.random.permutation(jax.random.fold_in(rng, 2), amount)]


def shared_out(stream_key, own, number, rows, number_of, top, limit, skew):
    ranking = jax.random.permutation(stream_key, number_of)
    crowded, common = load_shares(number_of, rows * top, limit, skew, True), load_shares(number_of, rows * top, limit, skew, False)
    places = jnp.arange(number_of)

    def named(sizes, turn):
        used = int((sizes > 0).sum())
        fixed = max(1, used // 4)
        shifted = fixed + (places - fixed + turn * (used - fixed)) % max(1, number_of - fixed)
        return jnp.zeros((number_of,), jnp.int32).at[ranking[jnp.where(places < fixed, places, shifted)]].set(jnp.asarray(sizes, jnp.int32))

    sizes = jnp.where(number % 4 == 0, named(crowded, number // 4), named(common, number - number // 4 - 1))
    mixed = jax.random.permutation(jax.random.fold_in(own, 3), number_of)
    donor, taker = mixed[0:number_of // 2 * 2:2], mixed[1:number_of // 2 * 2:2]
    room = jnp.minimum(sizes[donor] - 1, limit - sizes[taker]) // 2
    room = jnp.where((donor == ranking[0]) | (taker == ranking[0]) | (sizes[taker] == 0), 0, jnp.maximum(room, 0))
    shifted = jax.random.randint(jax.random.fold_in(own, 4), (number_of // 2,), 0, 1 << 20) % (room + 1)
    sizes = sizes.at[donor].add(-shifted).at[taker].add(shifted)
    labels = jnp.searchsorted(jnp.cumsum(sizes), jnp.arange(rows * top), side="right").astype(jnp.int32)
    table = labels.reshape(top, rows).T
    table = table[jax.random.permutation(jax.random.fold_in(own, 1), rows)]
    turn = jax.random.randint(jax.random.fold_in(own, 2), (rows, 1), 0, top)
    return jnp.take_along_axis(table, (jnp.arange(top)[None, :] + turn) % top, axis=1)


def load_shares(count, total, most, lean, full):
    loads = [(1 << 20) // math.isqrt(grade ** lean) + 1 for grade in range(1, count + 1)]
    largest = most if full else min(most, max(-(-total // count), total * loads[0] // sum(loads)))
    least = 1 if total - largest >= count - 1 else 0
    counts, surplus = [largest] + [least] * (count - 1), total - largest - least * (count - 1)
    while surplus > 0:
        movable = [i for i in range(1, count) if counts[i] < largest] or [i for i in range(1, count) if counts[i] < most]
        mass, left = sum([loads[i] for i in movable]), surplus
        for i in movable:
            extra = min(most - counts[i], max(1, left * loads[i] // mass), surplus)
            counts[i] = counts[i] + extra
            surplus = surplus - extra
    return np.array(counts)


def centred(rng, shape, scale, reach, pieces=(), kind=jnp.bfloat16):
    values = jax.random.normal(rng, shape, jnp.float32) * scale
    if len(pieces) > 0:
        values = steps_of(rng, shape, pieces, -0.22, 0.18) * values
    return jnp.clip(values, min=-reach, max=reach).astype(kind)


def setup_inputs(seed: int = 0) -> dict:
    keys = jax.random.split(jax.random.key(seed), 17)
    tokens = centred(keys[0], (TOKENS, D), 1.0, 6.0, ((0, 32),))
    past_logits = centred(keys[1], (TOKENS, NEXP), 0.5, 3.0, ((0, 32),), jnp.float32)
    routes_keys = jax.random.split(jax.random.fold_in(keys[2], 1), TOKENS // TOK_DEV)
    routes_turns = jax.random.permutation(jax.random.fold_in(keys[2], 3), TOKENS // TOK_DEV)
    routes = jax.vmap(lambda own, number: shared_out(jax.random.fold_in(keys[2], 2), own, number, TOK_DEV, NEXP, 2, CAP, 1))(routes_keys, routes_turns).reshape((TOKENS, 2))
    lengths = jax.vmap(lambda own: ragged_sizes(own, DOCS, SEQ, SEQ - TOK_DEV // 2, 2))(jax.random.split(keys[3], SEQS)).reshape((SEQS, DOCS)).astype(jnp.int32)
    projector = centred(keys[4], (D, 3 * D), D ** -0.5, 0.21875, ((0, 8),))
    collector = centred(keys[5], (D, D), (16 * D // WINDOW) ** -0.5, 1.75, ((0, 8),))
    router = centred(keys[6], (D, NEXP), (4 * D) ** -0.5, 0.109375, ((0, 8),))
    blender = centred(keys[7], (D, 4), D ** -0.5, 0.21875, ((0, 8),))
    constants = centred(keys[8], (D, 2), 1.0, 5.0, ((0, 8),))
    first_gain = jnp.clip(1.0 + 0.1 * jax.random.normal(keys[9], (D,), jnp.float32), 0.5, 1.5).astype(jnp.bfloat16)
    second_gain = jnp.clip(1.0 + 0.1 * jax.random.normal(keys[10], (D,), jnp.float32), 0.5, 1.5).astype(jnp.bfloat16)
    carryover = centred(keys[11], (NEXP, NEXP), NEXP ** -0.5, 2.0, (), jnp.float32)
    gating = centred(keys[12], (E, D, FF), D ** -0.5, 0.21875, ((0, 4), (1, 8)))
    upward = centred(keys[13], (E, D, FF), D ** -0.5, 0.21875, ((0, 4), (1, 8)))
    downward = centred(keys[14], (E, D, FF), (FF // 4) ** -0.5, 0.25, ((0, 4), (1, 8)))
    cotangent = centred(keys[15], (TOKENS, D), 1.0, 6.0, ((0, 32),))
    return dict(tokens=tokens, past_logits=past_logits, routes=routes, lengths=lengths, projector=projector, collector=collector, router=router, blender=blender, constants=constants, first_gain=first_gain, second_gain=second_gain, carryover=carryover, gating=gating, upward=upward, downward=downward, cotangent=cotangent)


@jax.custom_vjp
def low(v):
    return lax.optimization_barrier(v.astype(jnp.bfloat16)).astype(jnp.float32)

@jax.custom_vjp
def low_back(v):
    return v

def low_keep(v):
    return (low(v), None)

def low_pass(kept, grad):
    return (grad,)

def back_keep(v):
    return (v, None)

def back_low(kept, grad):
    return (low(grad),)
low.defvjp(low_keep, low_pass)
low_back.defvjp(back_keep, back_low)
epsilon = 1e-06
rope_base = 10000.0
masked_score = -1e+30

def matmul(left, right):
    return jnp.dot(left, right, precision=lax.Precision.HIGHEST, preferred_element_type=jnp.float32)

def norm_scale(values):
    return lax.rsqrt(lax.optimization_barrier(jnp.mean(values * values, axis=-1, keepdims=True)) + epsilon)

def softmax_rows(values):
    row_max = lax.optimization_barrier(jnp.max(values, axis=-1, keepdims=True))
    exponent = jnp.exp(values - row_max)
    return exponent / lax.optimization_barrier(jnp.sum(exponent, axis=-1, keepdims=True))

def rope_tables(positions, head_size):
    half_size = head_size // 2
    freq_index = jnp.arange(half_size).astype(jnp.float32)
    inverse = jnp.exp(freq_index * (-2.0 * math.log(rope_base) / head_size))
    angles = positions[:, None] * inverse[None, :]
    return (jnp.cos(angles)[:, None, :], jnp.sin(angles)[:, None, :])

def rotate(values, cosine_table, sine_table):
    half_size = values.shape[-1] // 2
    lower_half = values[..., :half_size]
    upper_half = values[..., half_size:]
    return jnp.concatenate([lower_half * cosine_table - upper_half * sine_table, lower_half * sine_table + upper_half * cosine_table], axis=-1)

def document_number(lengths_row, positions):
    bounds = jnp.cumsum(lengths_row)
    return lax.optimization_barrier(jnp.sum((positions[:, None] >= bounds[None, :]).astype(jnp.int32), axis=1)).astype(jnp.int32)

def attention(queries, keys_low, values_low, lengths):
    rows_block = min(512, SEQ)
    blocks_seq = SEQ // rows_block
    padding = jnp.zeros((SEQS, WINDOW, H, HD), jnp.float32)
    keys_padded = jnp.concatenate([padding, keys_low], axis=1)
    values_padded = jnp.concatenate([padding, values_low], axis=1)
    positions = jnp.arange(SEQ, dtype=jnp.int32)
    doc_table = jax.vmap(document_number, in_axes=(0, None))(lengths, positions)
    doc_padded = jnp.concatenate([jnp.full((SEQS, WINDOW), -1, jnp.int32), doc_table], axis=1)

    def one_block(block_number):
        seq_index = (block_number // blocks_seq).astype(jnp.int32)
        row_start = (block_number % blocks_seq * rows_block).astype(jnp.int32)
        query_block = lax.dynamic_slice_in_dim(lax.dynamic_index_in_dim(queries, seq_index, 0, False), row_start, rows_block, 0)
        key_block = lax.dynamic_slice_in_dim(lax.dynamic_index_in_dim(keys_padded, seq_index, 0, False), row_start, rows_block + WINDOW, 0)
        value_block = lax.dynamic_slice_in_dim(lax.dynamic_index_in_dim(values_padded, seq_index, 0, False), row_start, rows_block + WINDOW, 0)
        query_docs = lax.dynamic_slice_in_dim(lax.dynamic_index_in_dim(doc_table, seq_index, 0, False), row_start, rows_block, 0)
        key_docs = lax.dynamic_slice_in_dim(lax.dynamic_index_in_dim(doc_padded, seq_index, 0, False), row_start, rows_block + WINDOW, 0)
        query_pos = row_start + jnp.arange(rows_block, dtype=jnp.int32)
        key_pos = row_start - WINDOW + jnp.arange(rows_block + WINDOW, dtype=jnp.int32)
        distance = query_pos[:, None] - key_pos[None, :]
        allowed = (distance >= 0) & (distance < WINDOW) & (query_docs[:, None] == key_docs[None, :])
        scores = low_back(jnp.einsum('qhd,khd->hqk', query_block, key_block, precision=lax.Precision.HIGHEST))
        scores = jnp.where(allowed[None], scores, masked_score)
        probability = low(softmax_rows(scores))
        return jnp.einsum('hqk,khd->qhd', probability, value_block, precision=lax.Precision.HIGHEST)
    outputs = lax.map(jax.checkpoint(one_block), jnp.arange(SEQS * blocks_seq, dtype=jnp.int32))
    return outputs.reshape(SEQS, SEQ, H, HD)

def expert_rows(packed):
    rows_in, gating_one, upward_one, downward_one = packed
    gate_pre = low_back(matmul(rows_in, gating_one))
    up_pre = low_back(matmul(rows_in, upward_one))
    hidden = low(jax.nn.silu(gate_pre) * up_pre)
    return low(low_back(matmul(hidden, downward_one.T)))

def dispatch_slots(routes):
    blocks_all = TOKENS // TOK_DEV
    onehot = (routes[:, :, None] == jnp.arange(E, dtype=jnp.int32)[None, None, :]).astype(jnp.int32)
    per_token = lax.optimization_barrier(jnp.sum(onehot, axis=1)).reshape(blocks_all, TOK_DEV, E)
    before = (jnp.cumsum(per_token, axis=1) - per_token).reshape(TOKENS, 1, E)
    position_in = lax.optimization_barrier(jnp.sum(onehot * before, axis=2))
    block_of = (jnp.arange(TOKENS, dtype=jnp.int32) // TOK_DEV)[:, None]
    return jnp.where(routes < E, block_of * (E * CAP) + routes * CAP + position_in, blocks_all * E * CAP).astype(jnp.int32)

def forward(tokens, past_logits, projector, collector, router, blender, constants, first_gain, second_gain, carryover, gating, upward, downward, routes, lengths):
    normed = low(tokens * norm_scale(tokens) * first_gain)
    projected = low_back(matmul(normed, projector))
    shaped = projected.reshape(SEQS, SEQ, 3, H, HD)
    cosine_table, sine_table = rope_tables(jnp.arange(SEQ).astype(jnp.float32), HD)
    queries = low(rotate(shaped[:, :, 0], cosine_table, sine_table) * (1.0 / math.sqrt(HD)))
    keys_low = low(rotate(shaped[:, :, 1], cosine_table, sine_table))
    values_low = low(shaped[:, :, 2])
    attended = attention(queries, keys_low, values_low, lengths).reshape(TOKENS, D)
    attended = low(low_back(attended))
    residual = tokens + low_back(matmul(attended, collector))
    hidden_in = low(residual * norm_scale(residual) * second_gain)
    logits = matmul(hidden_in, router) + matmul(past_logits, carryover)
    gate_values = softmax_rows(jnp.take_along_axis(logits, routes, axis=1))
    slot_index = dispatch_slots(routes)
    blocks_all = TOKENS // TOK_DEV
    slot_table = jnp.full((blocks_all * E * CAP + 1,), 2 * TOKENS, jnp.int32).at[slot_index.reshape(-1)].set(jnp.arange(2 * TOKENS, dtype=jnp.int32))
    zero_row = jnp.zeros((1, D), jnp.float32)
    copies = jnp.stack([low_back(hidden_in), low_back(hidden_in)], axis=1).reshape(2 * TOKENS, D)
    copies = jnp.concatenate([copies, zero_row], axis=0)
    rows_in = copies[slot_table[:-1]].reshape(blocks_all, E, CAP, D).transpose(1, 0, 2, 3).reshape(E, blocks_all * CAP, D)
    rows_out = lax.map(jax.checkpoint(expert_rows), (rows_in, gating, upward, downward))
    rows_out = rows_out.reshape(E, blocks_all, CAP, D).transpose(1, 0, 2, 3).reshape(blocks_all * E * CAP, D)
    rows_out = jnp.concatenate([rows_out, zero_row], axis=0)
    expert_values = rows_out[slot_index]
    mixing = softmax_rows(matmul(hidden_in, blender).reshape(TOKENS, 2, 2))
    const_values = mixing[:, :, 0:1] * hidden_in[:, None, :] + mixing[:, :, 1:2] * constants.T[None, :, :]
    route_copy = (routes == E + 1).astype(jnp.float32)[:, :, None]
    route_first = (routes == E + 2).astype(jnp.float32)[:, :, None]
    route_second = (routes == E + 3).astype(jnp.float32)[:, :, None]
    values_all = expert_values + route_copy * hidden_in[:, None, :] + route_first * const_values[:, 0:1, :] + route_second * const_values[:, 1:2, :]
    return residual + lax.optimization_barrier(jnp.sum(gate_values[:, :, None] * values_all, axis=1))

def reference(tokens, past_logits, routes, lengths, projector, collector, router, blender, constants, first_gain, second_gain, carryover, gating, upward, downward, cotangent):

    def closed(*floats):
        return forward(*floats, routes, lengths)
    inputs = tuple((array_in.astype(jnp.float32) for array_in in (tokens, past_logits, projector, collector, router, blender, constants, first_gain, second_gain, carryover, gating, upward, downward)))
    result, pullback = jax.vjp(closed, *inputs)
    gradients = pullback(cotangent.astype(jnp.float32))
    return (result.astype(jnp.bfloat16), gradients[0].astype(jnp.bfloat16), gradients[1], gradients[2], gradients[3], gradients[4], gradients[5], gradients[6], gradients[7], gradients[8], gradients[9], gradients[10], gradients[11], gradients[12])
```

```python
import functools
import math

import jax
import jax.numpy as jnp
from jax import lax
from jax.experimental import pallas as pl
from jax.experimental.pallas import tpu as pltpu
from jax.sharding import PartitionSpec as P

D = 768
H = 12
HD = 64
FF = 2048
WINDOW = 1024
CAP = 128

epsilon = 1e-06
rope_base = 10000.0
masked_score = -1e30
QTILE = 256
SPAN = QTILE + WINDOW
LANES = 128
PAIRS = H * HD // LANES
FTILE = 256
NT = (((1,), (1,)), ((), ()))
TN = (((0,), (0,)), ((), ()))
F32 = jnp.float32
BF16 = jnp.bfloat16
query_scale = 1.0 / math.sqrt(HD)


def vmem(megabytes):
    return pltpu.CompilerParams(vmem_limit_bytes=megabytes << 20)


def cost(flops, moved, trans=0):
    return pl.CostEstimate(flops=int(flops), bytes_accessed=int(moved), transcendentals=int(trans))


def dot(a, b):
    return jnp.dot(a, b, preferred_element_type=F32)


def dot_nt(a, b):
    return lax.dot_general(a, b, NT, preferred_element_type=F32)


def dot_tn(a, b):
    return lax.dot_general(a, b, TN, preferred_element_type=F32)


def halves(x):
    high = x.astype(BF16)
    return high, (x - high.astype(F32)).astype(BF16)


def lanes_of(shape):
    return lax.broadcasted_iota(jnp.int32, shape, len(shape) - 1)


def norm_scale(values):
    return lax.rsqrt(jnp.mean(values * values, axis=-1, keepdims=True) + epsilon)


def rope_tables(positions):
    lane = jnp.arange(LANES, dtype=jnp.int32)
    half = HD // 2
    freq_index = (lane % half).astype(F32)
    inverse = jnp.exp(freq_index * (-2.0 * math.log(rope_base) / HD))
    angles = positions[:, None] * inverse[None, :]
    sign = jnp.where(lane % HD < half, -1.0, 1.0).astype(F32)
    return jnp.cos(angles), jnp.sin(angles) * sign[None, :]


def swapped(x):
    half = HD // 2
    lane = lanes_of(x.shape)
    return jnp.where(
        lane % HD < half, pltpu.roll(x, LANES - half, 1), pltpu.roll(x, half, 1)
    )


def rotate(x, cosine, sine):
    return x * cosine + swapped(x) * sine


def rotate_back(x, cosine, sine):
    return x * cosine - swapped(x) * sine


def project_kernel(place, *refs):
    count = place.shape[0]
    chunks = refs[:count]
    tok_ref, cos_ref, sin_ref, w_ref, normed_ref, q_ref, k_ref, v_ref = refs[count:]
    rows = chunks[0].shape[0]
    step = pl.program_id(0)

    @pl.when(step == 0)
    def _():
        for i in range(count):
            at = pl.multiple_of(place[i] * rows, rows)
            w_ref[pl.ds(at, rows), :] = chunks[i][...]

    small = w_ref[:, 3 * D :].astype(F32).T
    gain = small[LANES - 2 : LANES - 1, :]
    x = tok_ref[...].astype(F32)
    normed = (x * norm_scale(x) * gain).astype(BF16)
    normed_ref[...] = normed
    cosine, sine = cos_ref[...], sin_ref[...]
    keys = dot(normed, w_ref[:, D : 2 * D])
    for j in range(PAIRS):
        part = slice(j * LANES, (j + 1) * LANES)
        k_ref[:, part] = rotate(keys[:, part], cosine, sine).astype(BF16)
    v_ref[...] = dot(normed, w_ref[:, 2 * D : 3 * D]).astype(BF16)

    @pl.when(step == pl.num_programs(0) - 1)
    def _():
        queries = dot(normed, w_ref[:, :D])
        for j in range(PAIRS):
            part = slice(j * LANES, (j + 1) * LANES)
            q_ref[:, part] = (rotate(queries[:, part], cosine, sine) * query_scale).astype(BF16)


def project(place, chunks, tokens_all, cosine, sine, tok):
    rows, width = chunks[0].shape
    blocks = tokens_all.shape[0] // tok
    fixed = lambda s, *_: (0, 0)
    moving = lambda s, *_: (s, 0)
    span = tokens_all.shape[0]
    return pl.pallas_call(
        project_kernel,
        grid_spec=pltpu.PrefetchScalarGridSpec(
            num_scalar_prefetch=1,
            grid=(blocks,),
            in_specs=[pl.BlockSpec((rows, width), fixed)] * len(chunks)
            + [
                pl.BlockSpec((tok, D), moving),
                pl.BlockSpec((tok, LANES), moving),
                pl.BlockSpec((tok, LANES), moving),
            ],
            out_specs=[
                pl.BlockSpec((D, width), fixed),
                pl.BlockSpec((tok, D), moving),
                pl.BlockSpec((tok, D), fixed),
                pl.BlockSpec((tok, D), moving),
                pl.BlockSpec((tok, D), moving),
            ],
        ),
        out_shape=[
            jax.ShapeDtypeStruct((D, width), BF16),
            jax.ShapeDtypeStruct((span, D), BF16),
            jax.ShapeDtypeStruct((tok, D), BF16),
            jax.ShapeDtypeStruct((span, D), BF16),
            jax.ShapeDtypeStruct((span, D), BF16),
        ],
        compiler_params=vmem(56),
        cost_estimate=cost(2 * span * D * 2 * D, 20 << 20),
        name="project",
    )(place, *chunks, tokens_all, cosine, sine)


def head_mask(x, head):
    return jnp.where(lanes_of(x.shape) // HD == head, x, jnp.zeros_like(x))


def attend_kernel(q_ref, k_ref, v_ref, bias_ref, o_ref, lse_ref, vt_ref):
    vt_ref[...] = v_ref[...].T
    for t in range(q_ref.shape[0] // QTILE):
        rows = slice(t * QTILE, (t + 1) * QTILE)
        span = slice(t * QTILE, t * QTILE + SPAN)
        keys, queries = k_ref[span, :], q_ref[rows, :]
        parts = []
        for h in range(2):
            s = dot_nt(keys, head_mask(queries, h)) + bias_ref[t]
            top = jnp.max(s, axis=0, keepdims=True)
            e = jnp.exp(s - top)
            total = jnp.sum(e, axis=0, keepdims=True)
            o = dot(vt_ref[h * HD : (h + 1) * HD, span], e.astype(BF16))
            parts.append(o / total)
            lse_ref[0, h : h + 1, rows] = top + jnp.log(total)
        o_ref[rows, :] = jnp.concatenate(parts, axis=0).T.astype(BF16)


def attend(q, k, v, bias):
    tok, span = q.shape[0], k.shape[0]
    col = lambda p: (0, p)
    return pl.pallas_call(
        attend_kernel,
        grid=(PAIRS,),
        in_specs=[
            pl.BlockSpec((tok, LANES), col),
            pl.BlockSpec((span, LANES), col),
            pl.BlockSpec((span, LANES), col),
            pl.BlockSpec(bias.shape, lambda p: (0, 0, 0)),
        ],
        out_specs=[
            pl.BlockSpec((tok, LANES), col),
            pl.BlockSpec((1, 8, tok), lambda p: (p, 0, 0)),
        ],
        out_shape=[
            jax.ShapeDtypeStruct((tok, D), BF16),
            jax.ShapeDtypeStruct((PAIRS, 8, tok), F32),
        ],
        scratch_shapes=[pltpu.VMEM((LANES, span), BF16)],
        compiler_params=vmem(56),
        cost_estimate=cost(4 * tok * SPAN * D * 4, 10 << 20, tok * SPAN * H),
        name="attend",
    )(q, k, v, bias)


def attend_back_kernel(
    q_ref, k_ref, v_ref, o_ref, do_ref, lse_ref, bias_ref, cos_ref, sin_ref,
    dq_ref, dk_ref, dv_ref, kt_ref, dk_sum, dv_sum,
):
    tok = q_ref.shape[0]
    own = k_ref.shape[0] - tok
    kt_ref[...] = k_ref[...].T
    dk_sum[...] = jnp.zeros_like(dk_sum)
    dv_sum[...] = jnp.zeros_like(dv_sum)
    for t in range(tok // QTILE):
        rows = slice(t * QTILE, (t + 1) * QTILE)
        span = slice(t * QTILE, t * QTILE + SPAN)
        keys, values = k_ref[span, :], v_ref[span, :]
        queries, upstream = q_ref[rows, :], do_ref[rows, :]
        product = (upstream.astype(F32) * o_ref[rows, :].astype(F32)).T
        dq_parts = []
        for h in range(2):
            head = slice(h * HD, (h + 1) * HD)
            qh, gh = head_mask(queries, h), head_mask(upstream, h)
            s = dot_nt(keys, qh) + bias_ref[t]
            p = jnp.exp(s - lse_ref[0, h : h + 1, rows])
            dp = dot_nt(values, gh)
            delta = jnp.sum(product[head, :], axis=0, keepdims=True)
            ds = (p * (dp - delta)).astype(BF16)
            dv_sum[span, :] += dot(p.astype(BF16), gh)
            dk_sum[span, :] += dot(ds, qh)
            dq_parts.append(dot(kt_ref[head, span], ds))
        dq = jnp.concatenate(dq_parts, axis=0).T
        there = slice(own + t * QTILE, own + (t + 1) * QTILE)
        dq = rotate_back(dq, cos_ref[there, :], sin_ref[there, :]) * query_scale
        dq_ref[rows, :] = dq.astype(BF16)
    dk_ref[...] = rotate_back(dk_sum[...], cos_ref[...], sin_ref[...]).astype(BF16)
    dv_ref[...] = dv_sum[...].astype(BF16)


def attend_back(q, k, v, o, do, lse, bias, cosine, sine):
    tok, span = q.shape[0], k.shape[0]
    col = lambda p: (0, p)
    whole = lambda p: (0, 0)
    mine = pl.BlockSpec((tok, LANES), col)
    long = pl.BlockSpec((span, LANES), col)
    return pl.pallas_call(
        attend_back_kernel,
        grid=(PAIRS,),
        in_specs=[
            mine,
            long,
            long,
            mine,
            mine,
            pl.BlockSpec((1, 8, tok), lambda p: (p, 0, 0)),
            pl.BlockSpec(bias.shape, lambda p: (0, 0, 0)),
            pl.BlockSpec((span, LANES), whole),
            pl.BlockSpec((span, LANES), whole),
        ],
        out_specs=[mine, long, long],
        out_shape=[
            jax.ShapeDtypeStruct((tok, D), BF16),
            jax.ShapeDtypeStruct((span, D), BF16),
            jax.ShapeDtypeStruct((span, D), BF16),
        ],
        scratch_shapes=[
            pltpu.VMEM((LANES, span), BF16),
            pltpu.VMEM((span, LANES), F32),
            pltpu.VMEM((span, LANES), F32),
        ],
        compiler_params=vmem(56),
        cost_estimate=cost(10 * tok * SPAN * D * 4, 20 << 20, tok * SPAN * H),
        name="attend_back",
    )(q, k, v, o, do, lse, bias, cosine, sine)


def route_kernel(
    experts, att_ref, col_ref, tok_ref, cot_ref, small_ref, past_ref, routes_ref, slots_ref,
    residual_ref, hidden_ref, aux_ref, send_ref,
):
    small = small_ref[...]
    gain = small.astype(F32).T[LANES - 1 : LANES, :]
    residual = tok_ref[...].astype(F32) + dot(att_ref[...], col_ref[...])
    scale = norm_scale(residual)
    hidden = (residual * scale * gain).astype(BF16)
    residual_ref[...] = residual
    hidden_ref[...] = hidden
    mixed = dot(hidden, small)
    logits = mixed + past_ref[...]
    lane = lanes_of(logits.shape)
    routes = routes_ref[...]
    picked = [
        jnp.sum(jnp.where(lane == routes[:, k : k + 1], logits, 0.0), axis=1, keepdims=True)
        for k in range(2)
    ]
    top = jnp.maximum(picked[0], picked[1])
    raised = [jnp.exp(x - top) for x in picked]
    total = raised[0] + raised[1]
    gates = [x / total for x in raised]
    names = experts + 4
    aux = [gates[0], gates[1]]
    for c in range(2):
        pair = [mixed[:, names + 2 * c + i : names + 2 * c + i + 1] for i in range(2)]
        above = jnp.maximum(pair[0], pair[1])
        up = [jnp.exp(x - above) for x in pair]
        aux += [up[0] / (up[0] + up[1]), up[1] / (up[0] + up[1])]
    aux.append(scale)
    packed = jnp.zeros(logits.shape, F32)
    for i, value in enumerate(aux):
        packed = jnp.where(lane == i, value, packed)
    aux_ref[...] = packed
    cot = cot_ref[...].astype(F32)
    slots = slots_ref[...]
    count, tok = send_ref.shape[0], hidden.shape[0]
    where = lax.broadcasted_iota(jnp.int32, (count, tok), 0)
    hot = [(where == slots[k : k + 1, :]).astype(F32).astype(BF16) for k in range(2)]
    send_ref[:, :D] = dot(hot[0] + hot[1], hidden).astype(BF16)
    grads = dot(hot[0], (gates[0] * cot).astype(BF16)) + dot(hot[1], (gates[1] * cot).astype(BF16))
    send_ref[:, D:] = grads.astype(BF16)


def whole_specs(arrays):
    return [pl.BlockSpec(memory_space=pltpu.VMEM) for _ in arrays]


def route(experts, *args):
    tok = args[0].shape[0]
    outs = [
        jax.ShapeDtypeStruct((tok, D), F32),
        jax.ShapeDtypeStruct((tok, D), BF16),
        jax.ShapeDtypeStruct((tok, LANES), F32),
        jax.ShapeDtypeStruct((experts * CAP, 2 * D), BF16),
    ]
    return pl.pallas_call(
        functools.partial(route_kernel, experts),
        in_specs=whole_specs(args),
        out_specs=whole_specs(outs),
        out_shape=outs,
        compiler_params=vmem(56),
        cost_estimate=cost(2 * tok * D * (D + 3 * experts * CAP), 9 << 20),
        name="route",
    )(*args)


def expert_kernel(x_ref, gw_ref, uw_ref, dw_ref, out_ref, low_ref, answer, back):
    step = pl.program_id(0)

    @pl.when(step == 0)
    def _():
        answer[...] = jnp.zeros_like(answer)
        back[...] = jnp.zeros_like(back)

    rows, grads = x_ref[:, :D], x_ref[:, D:]
    gw, uw, dw = gw_ref[...], uw_ref[...], dw_ref[...]
    pre = dot(rows, gw)
    up = dot(rows, uw)
    grad = dot(grads, dw)
    sigmoid = 1.0 / (1.0 + jnp.exp(-pre))
    active = pre * sigmoid
    hidden = (active * up).astype(BF16)
    gate_low = (grad * up * sigmoid * (1.0 + pre * (1.0 - sigmoid))).astype(BF16)
    up_low = (grad * active).astype(BF16)
    low_ref[0] = gate_low
    low_ref[1] = up_low
    low_ref[2] = hidden
    answer[...] += dot_nt(hidden, dw)
    back[...] += dot_nt(gate_low, gw) + dot_nt(up_low, uw)

    @pl.when(step == pl.num_programs(0) - 1)
    def _():
        out_ref[:, :D] = answer[...].astype(BF16)
        out_ref[:, D:] = back[...].astype(BF16)


def expert_rows(x, gating, upward, downward):
    rows = x.shape[0]
    weight = pl.BlockSpec((D, FTILE), lambda j: (0, j))
    return pl.pallas_call(
        expert_kernel,
        grid=(FF // FTILE,),
        in_specs=[pl.BlockSpec((rows, 2 * D), lambda j: (0, 0)), weight, weight, weight],
        out_specs=[
            pl.BlockSpec((rows, 2 * D), lambda j: (0, 0)),
            pl.BlockSpec((3, rows, FTILE), lambda j: (0, 0, j)),
        ],
        out_shape=[
            jax.ShapeDtypeStruct((rows, 2 * D), BF16),
            jax.ShapeDtypeStruct((3, rows, FF), BF16),
        ],
        scratch_shapes=[pltpu.VMEM((rows, D), F32), pltpu.VMEM((rows, D), F32)],
        compiler_params=vmem(56),
        cost_estimate=cost(12 * rows * D * FF, 20 << 20),
        name="expert_rows",
    )(x, gating, upward, downward)


def expert_sums_kernel(x_ref, low_ref, out_ref, turned):
    step = pl.program_id(0)
    tiles = FF // FTILE

    @pl.when(step == 0)
    def _():
        turned[...] = x_ref[:, :D].T

    @pl.when(step == 2 * tiles)
    def _():
        turned[...] = x_ref[:, D:].T

    out_ref[...] = dot(turned[...], low_ref[0]).astype(BF16)


def expert_sums(x, low):
    rows = x.shape[0]
    tiles = FF // FTILE
    return pl.pallas_call(
        expert_sums_kernel,
        grid=(3 * tiles,),
        in_specs=[
            pl.BlockSpec((rows, 2 * D), lambda j: (0, 0)),
            pl.BlockSpec((1, rows, FTILE), lambda j: (j // tiles, 0, j % tiles)),
        ],
        out_specs=pl.BlockSpec((D, FTILE), lambda j: (0, j)),
        out_shape=jax.ShapeDtypeStruct((D, 3 * FF), BF16),
        scratch_shapes=[pltpu.VMEM((D, rows), BF16)],
        compiler_params=vmem(56),
        cost_estimate=cost(6 * rows * D * FF, 20 << 20),
        name="expert_sums",
    )(x, low)


def combine_kernel(
    experts, back_ref, residual_ref, hidden_ref, cot_ref, aux_ref, small_ref, col_ref, att_ref,
    past_ref, carry_ref, routes_ref, slots_ref,
    layer_ref, rgrad_ref, agrad_ref, logits_ref, colgrad_ref, smallgrad_ref, carrygrad_ref,
):
    tok = hidden_ref.shape[0]
    names = experts + 4
    slots, routes = slots_ref[...], routes_ref[...]
    count = back_ref.shape[0]
    where = lax.broadcasted_iota(jnp.int32, (tok, count), 1)
    hot = [(where == slots[:, k : k + 1]).astype(F32).astype(BF16) for k in range(2)]
    answers, returned = back_ref[:, :D], back_ref[:, D:]
    values = [dot(hot[k], answers) for k in range(2)]
    hidden_grad = dot(hot[0] + hot[1], returned)
    hidden_low, cot_low = hidden_ref[...], cot_ref[...]
    hidden, cot = hidden_low.astype(F32), cot_low.astype(F32)
    residual = residual_ref[...]
    small = small_ref[...]
    turned = small.astype(F32).T
    aux = aux_ref[...]
    gates = [aux[:, k : k + 1] for k in range(2)]
    mixing = [[aux[:, 2 + 2 * c + i : 3 + 2 * c + i] for i in range(2)] for c in range(2)]
    scale = aux[:, 6:7]
    both = jnp.sum(hidden * cot, axis=1, keepdims=True)
    against = dot(cot_low, small)
    fixed = [against[:, names + 4 + c : names + 5 + c] for c in range(2)]
    constant = [turned[names + 4 + c : names + 5 + c, :] for c in range(2)]

    def on(k, e):
        return (routes[:, k : k + 1] == e).astype(F32)

    gate_grad = []
    for k in range(2):
        total = jnp.sum(values[k] * cot, axis=1, keepdims=True) + on(k, experts + 1) * both
        for c in range(2):
            total += on(k, experts + 2 + c) * (mixing[c][0] * both + mixing[c][1] * fixed[c])
        gate_grad.append(total)
    mean = gates[0] * gate_grad[0] + gates[1] * gate_grad[1]
    chosen = [gates[k] * (gate_grad[k] - mean) for k in range(2)]
    weight = [sum(on(k, experts + 2 + c) * gates[k] for k in range(2)) for c in range(2)]
    copied = sum(on(k, experts + 1) * gates[k] for k in range(2))
    copied += weight[0] * mixing[0][0] + weight[1] * mixing[1][0]
    lane = lanes_of((tok, LANES))
    logit_grad = jnp.where(lane == routes[:, 0:1], chosen[0], 0.0)
    logit_grad += jnp.where(lane == routes[:, 1:2], chosen[1], 0.0)
    wide = logit_grad
    shares = jnp.zeros((tok, LANES), F32)
    output = residual + gates[0] * values[0] + gates[1] * values[1] + copied * hidden
    for c in range(2):
        parts = [weight[c] * both, weight[c] * fixed[c]]
        middle = mixing[c][0] * parts[0] + mixing[c][1] * parts[1]
        for i in range(2):
            wide = jnp.where(lane == names + 2 * c + i, mixing[c][i] * (parts[i] - middle), wide)
        share = weight[c] * mixing[c][1]
        shares = jnp.where(lane == names + 4 + c, share, shares)
        output += share * constant[c]
    layer_ref[...] = output.astype(BF16)
    logits_ref[...] = lax.dot_general(
        logit_grad, carry_ref[...], NT, precision=lax.Precision.HIGHEST,
        preferred_element_type=F32,
    )
    carrygrad_ref[...] = lax.dot_general(
        past_ref[...], logit_grad, TN, precision=lax.Precision.HIGHEST,
        preferred_element_type=F32,
    )
    high, low = halves(wide)
    hidden_grad += copied * cot + dot_nt(high, small) + dot_nt(low, small)
    scaled = hidden_grad * turned[LANES - 1 : LANES, :]
    residual_grad = (
        cot
        + scale * scaled
        - residual * (scale * scale * scale) * jnp.mean(scaled * residual, axis=1, keepdims=True)
    )
    rgrad_ref[...] = residual_grad
    residual_low = residual_grad.astype(BF16)
    agrad_ref[...] = dot_nt(residual_low, col_ref[...]).astype(BF16)
    colgrad_ref[...] = dot_tn(att_ref[...], residual_low).astype(BF16)
    gained = jnp.sum((hidden_grad * residual * scale).reshape(tok // 8, 8, D), axis=0)
    gained = jnp.sum(gained, axis=0, keepdims=True)
    column = lax.broadcasted_iota(jnp.int32, (LANES, D), 0)
    second = jnp.where(column == LANES - 1, gained, 0.0).T
    shares_high, shares_low = halves(shares)
    smallgrad_ref[...] = (
        second
        + dot_tn(hidden_low, high)
        + dot_tn(hidden_low, low)
        + dot_tn(cot_low, shares_high)
        + dot_tn(cot_low, shares_low)
    )


def combine(experts, *args):
    tok = args[1].shape[0]
    outs = [
        jax.ShapeDtypeStruct((tok, D), BF16),
        jax.ShapeDtypeStruct((tok, D), F32),
        jax.ShapeDtypeStruct((tok, D), BF16),
        jax.ShapeDtypeStruct((tok, LANES), F32),
        jax.ShapeDtypeStruct((D, D), BF16),
        jax.ShapeDtypeStruct((D, LANES), F32),
        jax.ShapeDtypeStruct((LANES, LANES), F32),
    ]
    return pl.pallas_call(
        functools.partial(combine_kernel, experts),
        in_specs=whole_specs(args),
        out_specs=whole_specs(outs),
        out_shape=outs,
        compiler_params=vmem(56),
        cost_estimate=cost(2 * tok * D * (2 * D + 3 * experts * CAP), 14 << 20),
        name="combine",
    )(*args)


def normed_grad_kernel(dq_ref, dk_ref, dv_ref, tok_ref, w_ref, halo_ref, own_ref, first_ref):
    step = pl.program_id(0)
    last = pl.num_programs(0) - 1

    @pl.when(step == 0)
    def _():
        first_ref[...] = jnp.zeros_like(first_ref)

    x = tok_ref[...].astype(F32)
    weight = x * norm_scale(x)

    def add(grad):
        rows = grad.shape[0]
        first_ref[...] += jnp.sum((grad * weight).reshape(rows // 8, 8, D), axis=0)

    grad = dot_nt(dk_ref[...], w_ref[:, D : 2 * D]) + dot_nt(dv_ref[...], w_ref[:, 2 * D : 3 * D])

    @pl.when(step < last)
    def _():
        halo_ref[...] = grad.astype(BF16)
        add(grad)

    @pl.when(step == last)
    def _():
        full = grad + dot_nt(dq_ref[...], w_ref[:, :D])
        own_ref[...] = full
        add(full)


def normed_grad(dq, dk, dv, tokens_all, weights):
    tok, span = dq.shape[0], dk.shape[0]
    blocks = span // tok
    fixed = lambda s: (0, 0)
    moving = lambda s: (s, 0)
    return pl.pallas_call(
        normed_grad_kernel,
        grid=(blocks,),
        in_specs=[
            pl.BlockSpec((tok, D), fixed),
            pl.BlockSpec((tok, D), moving),
            pl.BlockSpec((tok, D), moving),
            pl.BlockSpec((tok, D), moving),
            pl.BlockSpec(weights.shape, fixed),
        ],
        out_specs=[
            pl.BlockSpec((tok, D), lambda s: (jnp.minimum(s, blocks - 2), 0)),
            pl.BlockSpec((tok, D), fixed),
            pl.BlockSpec((8, D), fixed),
        ],
        out_shape=[
            jax.ShapeDtypeStruct((span - tok, D), BF16),
            jax.ShapeDtypeStruct((tok, D), F32),
            jax.ShapeDtypeStruct((8, D), F32),
        ],
        compiler_params=vmem(56),
        cost_estimate=cost(4 * span * D * D, 16 << 20),
        name="normed_grad",
    )(dq, dk, dv, tokens_all, weights)


def project_grad_kernel(normed_ref, dq_ref, dk_ref, dv_ref, first_ref, out_ref, turned):
    tok = dq_ref.shape[0]
    own = normed_ref.shape[0] - tok
    step = pl.program_id(0)
    tiles = D // FTILE

    @pl.when(step == 0)
    def _():
        turned[...] = normed_ref[...].T

    @pl.when(step < tiles)
    def _():
        out_ref[...] = dot(turned[:, own:], dq_ref[...]).astype(BF16)

    @pl.when((step >= tiles) & (step < 2 * tiles))
    def _():
        out_ref[...] = dot(turned[...], dk_ref[...]).astype(BF16)

    @pl.when((step >= 2 * tiles) & (step < 3 * tiles))
    def _():
        out_ref[...] = dot(turned[...], dv_ref[...]).astype(BF16)

    @pl.when(step == 3 * tiles)
    def _():
        total = jnp.sum(first_ref[...], axis=0, keepdims=True)
        column = lax.broadcasted_iota(jnp.int32, (FTILE, D), 0)
        out_ref[...] = jnp.where(column == 0, total, 0.0).T.astype(BF16)


def project_grad(normed_all, dq, dk, dv, first):
    tok, span = dq.shape[0], dk.shape[0]
    tiles = D // FTILE
    fixed = lambda s: (0, 0)

    def tile(base):
        return lambda s: (0, jnp.clip(s - base, 0, tiles - 1))

    return pl.pallas_call(
        project_grad_kernel,
        grid=(3 * tiles + 1,),
        in_specs=[
            pl.BlockSpec((span, D), fixed),
            pl.BlockSpec((tok, FTILE), tile(0)),
            pl.BlockSpec((span, FTILE), tile(tiles)),
            pl.BlockSpec((span, FTILE), tile(2 * tiles)),
            pl.BlockSpec((8, D), fixed),
        ],
        out_specs=pl.BlockSpec((D, FTILE), lambda s: (0, s)),
        out_shape=jax.ShapeDtypeStruct((D, 3 * D + FTILE), BF16),
        scratch_shapes=[pltpu.VMEM((D, span), BF16)],
        compiler_params=vmem(56),
        cost_estimate=cost(4 * span * D * D, 12 << 20),
        name="project_grad",
    )(normed_all, dq, dk, dv, first)


def folded(count):
    return [0] + list(range(1, count, 2)) + list(range(2, count, 2))[::-1]


def siblings(count):
    return [(i, i ^ 1) for i in range(count)]


def ring_gather(x, count):
    chips = count // 2
    order = folded(chips)
    follow = {order[i]: order[(i + 1) % chips] for i in range(chips)}
    pairs = [(2 * z + c, 2 * follow[z] + c) for z in range(chips) for c in range(2)]
    me = lax.axis_index("fsdp")
    chip, core = me // 2, me % 2
    at = jnp.array([order.index(z) for z in range(chips)], jnp.int32)[chip]
    ring = jnp.array(order, jnp.int32)
    chunks, places = [], []
    current = x
    for k in range(chips):
        source = ring[(at - k) % chips]
        chunks += [current, lax.ppermute(current, "fsdp", siblings(count))]
        places += [2 * source + core, 2 * source + 1 - core]
        if k + 1 < chips:
            current = lax.ppermute(current, "fsdp", pairs)
    return chunks, jnp.stack(places).astype(jnp.int32)


def earlier_rows(x, count):
    up = [(i, i + 2) for i in range(count - 2)]
    second = lax.ppermute(x, "fsdp", up)
    core = lax.axis_index("fsdp") % 2
    first = lax.ppermute(jnp.where(core == 0, x, second), "fsdp", siblings(count))
    return second, first


def return_rows(second, first, own, count):
    down = [(i + 2, i) for i in range(count - 2)]
    core = lax.axis_index("fsdp") % 2
    across = lax.ppermute(first, "fsdp", siblings(count)).astype(F32)
    total = jnp.where(core == 0, second.astype(F32), second.astype(F32) + across)
    after = lax.ppermute(total.astype(BF16), "fsdp", down).astype(F32)
    return own + after + jnp.where(core == 0, across, 0.0)


def reduce_rows(x, experts, count):
    chips = count // 2
    rows, width = x.shape
    piece = rows // (count * experts)
    core = lax.axis_index("fsdp") % 2
    x = x.reshape(chips, 2, experts, piece, width)
    mine = lax.dynamic_index_in_dim(x, core, 1, False)
    theirs = lax.dynamic_index_in_dim(x, 1 - core, 1, False)
    other = lax.ppermute(theirs, "fsdp", siblings(count))
    x = (mine.astype(F32) + other.astype(F32)).astype(BF16)
    x = x.transpose(1, 0, 2, 3).reshape(experts, chips * piece, width)
    x = lax.all_to_all(x, "expert", split_axis=0, concat_axis=0, tiled=True)
    x = jnp.sum(x.astype(F32), axis=0).astype(BF16).reshape(chips, piece, width)
    groups = [[2 * z + c for z in range(chips)] for c in range(2)]
    x = lax.all_to_all(
        x, "fsdp", split_axis=0, concat_axis=0, tiled=True, axis_index_groups=groups
    )
    x = jnp.sum(x.astype(F32), axis=0)
    return lax.all_gather(x.astype(BF16), "expert", axis=0, tiled=True).astype(F32), x


def local(
    tokens,
    past_logits,
    routes,
    lengths,
    projector,
    collector,
    router,
    blender,
    constants,
    first_gain,
    second_gain,
    carryover,
    gating,
    upward,
    downward,
    cotangent,
):
    tok = tokens.shape[0]
    experts = lax.axis_size("expert")
    count = lax.axis_size("fsdp")
    names = experts + 4
    hops = WINDOW // tok
    me = lax.axis_index("fsdp")

    shard = projector.shape[0]
    gap = LANES - names - 8
    small = jnp.concatenate(
        [router, blender, constants, jnp.zeros((shard, gap), BF16)]
        + [first_gain[:, None], second_gain[:, None]],
        axis=1,
    )
    chunks, places = ring_gather(jnp.concatenate([projector, small], axis=1), count)
    second, first = earlier_rows(tokens, count)
    tokens_all = jnp.concatenate([second, first, tokens], axis=0)
    collector_all = lax.all_gather(collector, "fsdp", axis=0, tiled=True)
    gating_all = lax.all_gather(gating[0], "fsdp", axis=0, tiled=True)
    upward_all = lax.all_gather(upward[0], "fsdp", axis=0, tiled=True)
    downward_all = lax.all_gather(downward[0], "fsdp", axis=0, tiled=True)

    span = tok + WINDOW
    key_positions = (me - hops) * tok + jnp.arange(span, dtype=jnp.int32)
    cosine, sine = rope_tables(key_positions.astype(F32))
    bounds = jnp.cumsum(lengths[0])
    biases = []
    for t in range(tok // QTILE):
        at = me * tok + t * QTILE + jnp.arange(QTILE, dtype=jnp.int32)
        start = jnp.max(jnp.where(bounds[:, None] <= at[None, :], bounds[:, None], 0), axis=0)
        least = jnp.maximum(at - (WINDOW - 1), start)
        keys_at = key_positions[t * QTILE : t * QTILE + SPAN, None]
        inside = (keys_at >= least[None, :]) & (keys_at <= at[None, :])
        biases.append(jnp.where(inside, 0.0, masked_score).astype(F32))
    bias = jnp.stack(biases)
    onehot = (routes[:, :, None] == jnp.arange(experts, dtype=jnp.int32)).astype(BF16)
    per_token = jnp.sum(onehot, axis=1)
    lower = jnp.tril(jnp.ones((tok, tok), BF16), -1)
    before = jnp.dot(lower, per_token, preferred_element_type=F32)
    position_in = jnp.sum(onehot.astype(F32) * before[:, None, :], axis=2).astype(jnp.int32)
    slots = jnp.where(routes < experts, routes * CAP + position_in, experts * CAP)
    past_part = jnp.dot(
        past_logits, carryover, precision=lax.Precision.HIGHEST, preferred_element_type=F32
    )
    past_part = jnp.pad(past_part, ((0, 0), (0, LANES - names)))
    past_wide = jnp.pad(past_logits, ((0, 0), (0, LANES - names)))
    carry_wide = jnp.pad(carryover, ((0, LANES - names), (0, LANES - names)))

    weights, normed_all, q, k, v = project(places, chunks, tokens_all, cosine, sine, tok)
    small_all = weights[:, 3 * D :]
    attended, lse = attend(q, k, v, bias)
    residual, hidden, aux, send = route(
        experts, attended, collector_all, tokens, cotangent, small_all, past_part, routes, slots.T
    )

    def exchange(x):
        x = x.reshape(experts, CAP, 2 * D)
        x = lax.all_to_all(x, "expert", split_axis=0, concat_axis=0, tiled=True)
        return x.reshape(experts * CAP, 2 * D)

    arrived = exchange(send)
    answers, low = expert_rows(arrived, gating_all, upward_all, downward_all)
    returned = exchange(answers)
    sums = expert_sums(arrived, low)
    sums = lax.psum_scatter(sums, "fsdp", scatter_dimension=0, tiled=True).astype(F32)

    layer_output, residual_grad, attended_grad, logits_grad, col_grad, small_grad, carry_grad = (
        combine(
            experts, returned, residual, hidden, cotangent, aux, small_all, collector_all,
            attended, past_wide, carry_wide, routes, slots,
        )
    )
    piece = D // (count * experts)
    wide = -(-names * names // piece)
    flat = jnp.pad(carry_grad[:names, :names].reshape(-1), (0, piece * wide - names * names))
    ride = jnp.tile(flat.reshape(piece, wide), (count * experts, 1))
    small_grad = jnp.concatenate(
        [small_grad[:, : names + 6], ride, small_grad[:, names + 6 + wide :]], axis=1
    )
    col_rows, col_piece = reduce_rows(
        jnp.concatenate([col_grad, small_grad.astype(BF16)], axis=1), experts, count
    )
    dq, dk, dv = attend_back(q, k, v, attended, attended_grad, lse, bias, cosine, sine)
    halo_grad, own_grad, first_sum = normed_grad(dq, dk, dv, tokens_all, weights)
    projector_grad = project_grad(normed_all, dq, dk, dv, first_sum)
    own_grad = return_rows(halo_grad[:tok], halo_grad[tok:], own_grad, count)
    projector_rows, _ = reduce_rows(projector_grad, experts, count)

    tokens_wide = tokens.astype(F32)
    first_scale = norm_scale(tokens_wide)
    scaled = own_grad * weights[:, 3 * D + LANES - 2].astype(F32)
    gradient_tokens = (
        residual_grad
        + first_scale * scaled
        - tokens_wide
        * (first_scale * first_scale * first_scale)
        * jnp.mean(scaled * tokens_wide, axis=-1, keepdims=True)
    ).astype(BF16)
    ridden = col_piece[:, D + names + 6 : D + names + 6 + wide].reshape(-1)
    return (
        layer_output,
        gradient_tokens,
        logits_grad[:, :names],
        projector_rows[:, : 3 * D],
        col_rows[:, :D],
        col_rows[:, D : D + names],
        col_rows[:, D + names : D + names + 4],
        col_rows[:, D + names + 4 : D + names + 6],
        projector_rows[:, 3 * D],
        col_rows[:, D + LANES - 1],
        ridden[: names * names].reshape(names, names),
        sums[:, :FF][None],
        sums[:, FF : 2 * FF][None],
        sums[:, 2 * FF :][None],
    )


def solution(mesh):
    rows = P(("expert", "fsdp"), None)
    shared = P("fsdp", None)
    expert = P("expert", "fsdp", None)
    return jax.shard_map(
        local,
        mesh=mesh,
        in_specs=(
            rows, rows, rows, P("expert", None), shared, shared, shared, shared, shared,
            P("fsdp"), P("fsdp"), P(), expert, expert, expert, rows,
        ),
        out_specs=(
            rows, rows, rows, shared, shared, shared, shared, shared,
            P("fsdp"), P("fsdp"), P(), expert, expert, expert,
        ),
        check_vma=False,
    )
```

```python
import functools
import math

import jax
import jax.numpy as jnp
from jax import lax
from jax.experimental import pallas as pl
from jax.experimental.pallas import tpu as pltpu
from jax.sharding import PartitionSpec as P

D = 768
H = 12
HD = 64
FF = 2048
WINDOW = 1024
CAP = 128

epsilon = 1e-06
rope_base = 10000.0
masked_score = -1e30
QTILE = 256
SPAN = QTILE + WINDOW
LANES = 128
PAIRS = H * HD // LANES
FTILE = 512
STILE = 2048
NT = (((1,), (1,)), ((), ()))
TN = (((0,), (0,)), ((), ()))
F32 = jnp.float32
BF16 = jnp.bfloat16
query_scale = 1.0 / math.sqrt(HD)


def vmem(megabytes):
    return pltpu.CompilerParams(vmem_limit_bytes=megabytes << 20)


def cost(flops, moved, trans=0):
    return pl.CostEstimate(flops=int(flops), bytes_accessed=int(moved), transcendentals=int(trans))


def dot(a, b):
    return jnp.dot(a, b, preferred_element_type=F32)


def dot_nt(a, b):
    return lax.dot_general(a, b, NT, preferred_element_type=F32)


def dot_tn(a, b):
    return lax.dot_general(a, b, TN, preferred_element_type=F32)


def halves(x):
    high = x.astype(BF16)
    return high, (x - high.astype(F32)).astype(BF16)


def lanes_of(shape):
    return lax.broadcasted_iota(jnp.int32, shape, len(shape) - 1)


def norm_scale(values):
    return lax.rsqrt(jnp.mean(values * values, axis=-1, keepdims=True) + epsilon)


def piece_shapes(width, parts):
    each = -(-width // (parts * LANES)) * LANES
    return [jax.ShapeDtypeStruct((parts, D // 2, each), BF16)] * 2


def rows_of_core(ref, core, count):
    rows = D // count
    at = [pl.multiple_of((2 * z + core) * rows, rows) for z in range(count // 2)]
    return jnp.concatenate([ref[pl.ds(a, rows), :] for a in at], axis=0)


def store_pieces(out_ref, value, at):
    each = out_ref.shape[2]
    for left in range(0, value.shape[1], LANES):
        part, inner = divmod(at + left, each)
        out_ref[part, :, inner : inner + LANES] = value[:, left : left + LANES]


def core_number():
    return (lax.axis_index("fsdp") % 2).astype(jnp.int32).reshape(1)


def rope_tables(positions):
    lane = jnp.arange(LANES, dtype=jnp.int32)
    half = HD // 2
    freq_index = (lane % half).astype(F32)
    inverse = jnp.exp(freq_index * (-2.0 * math.log(rope_base) / HD))
    angles = positions[:, None] * inverse[None, :]
    sign = jnp.where(lane % HD < half, -1.0, 1.0).astype(F32)
    return jnp.cos(angles), jnp.sin(angles) * sign[None, :]


def swapped(x):
    half = HD // 2
    lane = lanes_of(x.shape)
    return jnp.where(
        lane % HD < half, pltpu.roll(x, LANES - half, 1), pltpu.roll(x, half, 1)
    )


def rotate(x, cosine, sine):
    return x * cosine + swapped(x) * sine


def rotate_back(x, cosine, sine):
    return x * cosine - swapped(x) * sine


def project_kernel(blocks_at, columns_at, *refs):
    chips, parts = blocks_at.shape[0] // 2, columns_at.shape[0]
    chunks = refs[: 2 * parts]
    tok_ref, cos_ref, sin_ref, w_ref, normed_ref, q_ref, k_ref, v_ref = refs[2 * parts :]
    rows, width = chunks[0].shape[1:]
    step = pl.program_id(0)

    @pl.when(step == 0)
    def _():
        for e in range(parts):
            left = pl.multiple_of(columns_at[e] * width, LANES)
            for z in range(chips):
                for c in range(2):
                    above = pl.multiple_of(blocks_at[2 * z + c] * rows, rows)
                    w_ref[pl.ds(above, rows), pl.ds(left, width)] = chunks[2 * e + c][z]

    small = w_ref[:, 3 * D : 3 * D + LANES].astype(F32).T
    gain = small[LANES - 2 : LANES - 1, :]
    x = tok_ref[...].astype(F32)
    normed = (x * norm_scale(x) * gain).astype(BF16)
    normed_ref[...] = normed
    cosine, sine = cos_ref[...], sin_ref[...]
    keys = dot(normed, w_ref[:, D : 2 * D])
    for j in range(PAIRS):
        part = slice(j * LANES, (j + 1) * LANES)
        k_ref[:, part] = rotate(keys[:, part], cosine, sine).astype(BF16)
    v_ref[...] = dot(normed, w_ref[:, 2 * D : 3 * D]).astype(BF16)

    @pl.when(step == pl.num_programs(0) - 1)
    def _():
        queries = dot(normed, w_ref[:, :D])
        for j in range(PAIRS):
            part = slice(j * LANES, (j + 1) * LANES)
            q_ref[:, part] = (rotate(queries[:, part], cosine, sine) * query_scale).astype(BF16)


def project(blocks_at, columns_at, chunks, tokens_all, cosine, sine, tok):
    chips, rows, width = chunks[0].shape
    parts = columns_at.shape[0]
    blocks = tokens_all.shape[0] // tok
    fixed = lambda s, *_: (0, 0)
    moving = lambda s, *_: (s, 0)
    span = tokens_all.shape[0]
    return pl.pallas_call(
        project_kernel,
        grid_spec=pltpu.PrefetchScalarGridSpec(
            num_scalar_prefetch=2,
            grid=(blocks,),
            in_specs=[pl.BlockSpec((chips, rows, width), lambda s, *_: (0, 0, 0))] * len(chunks)
            + [
                pl.BlockSpec((tok, D), moving),
                pl.BlockSpec((tok, LANES), moving),
                pl.BlockSpec((tok, LANES), moving),
            ],
            out_specs=[
                pl.BlockSpec((D, parts * width), fixed),
                pl.BlockSpec((tok, D), moving),
                pl.BlockSpec((tok, D), fixed),
                pl.BlockSpec((tok, D), moving),
                pl.BlockSpec((tok, D), moving),
            ],
        ),
        out_shape=[
            jax.ShapeDtypeStruct((D, parts * width), BF16),
            jax.ShapeDtypeStruct((span, D), BF16),
            jax.ShapeDtypeStruct((tok, D), BF16),
            jax.ShapeDtypeStruct((span, D), BF16),
            jax.ShapeDtypeStruct((span, D), BF16),
        ],
        compiler_params=vmem(56),
        cost_estimate=cost(2 * span * D * 2 * D, 20 << 20),
        name="project",
    )(blocks_at, columns_at, *chunks, tokens_all, cosine, sine)


def head_mask(x, head):
    return jnp.where(lanes_of(x.shape) // HD == head, x, jnp.zeros_like(x))


def both_heads(x):
    return jnp.concatenate([head_mask(x, 0), head_mask(x, 1)], axis=0)


def own_head(x):
    return jnp.concatenate([x[:HD, :QTILE], x[HD:, QTILE:]], axis=0).T


def attend_kernel(q_ref, k_ref, v_ref, bias_ref, o_ref, lse_ref, vt_ref):
    vt_ref[...] = v_ref[...].T
    for t in range(q_ref.shape[0] // QTILE):
        rows = slice(t * QTILE, (t + 1) * QTILE)
        span = slice(t * QTILE, t * QTILE + SPAN)
        s = dot_nt(k_ref[span, :], both_heads(q_ref[rows, :]))
        s += jnp.concatenate([bias_ref[t]] * 2, axis=1)
        top = jnp.max(s, axis=0, keepdims=True)
        e = jnp.exp(s - top)
        total = jnp.sum(e, axis=0, keepdims=True)
        o_ref[rows, :] = own_head(dot(vt_ref[:, span], e.astype(BF16)) / total).astype(BF16)
        lse = top + jnp.log(total)
        for h in range(2):
            lse_ref[0, h : h + 1, rows] = lse[:, h * QTILE : (h + 1) * QTILE]


def attend(q, k, v, bias, first, pairs):
    tok, span = q.shape[0], k.shape[0]
    col = lambda p: (0, first + p)
    return pl.pallas_call(
        attend_kernel,
        grid=(pairs,),
        in_specs=[
            pl.BlockSpec((tok, LANES), col),
            pl.BlockSpec((span, LANES), col),
            pl.BlockSpec((span, LANES), col),
            pl.BlockSpec(bias.shape, lambda p: (0, 0, 0)),
        ],
        out_specs=[
            pl.BlockSpec((tok, LANES), lambda p: (0, p)),
            pl.BlockSpec((1, 8, tok), lambda p: (p, 0, 0)),
        ],
        out_shape=[
            jax.ShapeDtypeStruct((tok, pairs * LANES), BF16),
            jax.ShapeDtypeStruct((pairs, 8, tok), F32),
        ],
        scratch_shapes=[pltpu.VMEM((LANES, span), BF16)],
        compiler_params=vmem(56),
        cost_estimate=cost(16 * tok * SPAN * pairs * LANES, pairs << 20, tok * SPAN * 2 * pairs),
        name="attend",
    )(q, k, v, bias)


def attend_back_kernel(
    q_ref, k_ref, v_ref, o_ref, do_ref, lse_ref, bias_ref, cos_ref, sin_ref,
    dq_ref, dk_ref, dv_ref, kt_ref, dk_sum, dv_sum,
):
    tok = q_ref.shape[0]
    own = k_ref.shape[0] - tok
    kt_ref[...] = k_ref[...].T
    dk_sum[...] = jnp.zeros_like(dk_sum)
    dv_sum[...] = jnp.zeros_like(dv_sum)
    for t in range(tok // QTILE):
        rows = slice(t * QTILE, (t + 1) * QTILE)
        span = slice(t * QTILE, t * QTILE + SPAN)
        keys, values = k_ref[span, :], v_ref[span, :]
        queries, upstream = q_ref[rows, :], do_ref[rows, :]
        product = (upstream.astype(F32) * o_ref[rows, :].astype(F32)).T
        qh, gh = both_heads(queries), both_heads(upstream)
        lse = jnp.concatenate([lse_ref[0, h : h + 1, rows] for h in range(2)], axis=1)
        delta = jnp.concatenate(
            [jnp.sum(product[h * HD : (h + 1) * HD], axis=0, keepdims=True) for h in range(2)],
            axis=1,
        )
        s = dot_nt(keys, qh) + jnp.concatenate([bias_ref[t]] * 2, axis=1)
        p = jnp.exp(s - lse)
        ds = (p * (dot_nt(values, gh) - delta)).astype(BF16)
        dv_sum[span, :] += dot(p.astype(BF16), gh)
        dk_sum[span, :] += dot(ds, qh)
        dq = own_head(dot(kt_ref[:, span], ds))
        there = slice(own + t * QTILE, own + (t + 1) * QTILE)
        dq = rotate_back(dq, cos_ref[there, :], sin_ref[there, :]) * query_scale
        dq_ref[rows, :] = dq.astype(BF16)
    dk_ref[...] = rotate_back(dk_sum[...], cos_ref[...], sin_ref[...]).astype(BF16)
    dv_ref[...] = dv_sum[...].astype(BF16)


def attend_back(q, k, v, o, do, lse, bias, cosine, sine):
    tok, span = q.shape[0], k.shape[0]
    pairs = PAIRS
    col = out = lambda p: (0, p)
    whole = lambda p: (0, 0)
    mine = pl.BlockSpec((tok, LANES), col)
    long = pl.BlockSpec((span, LANES), col)
    return pl.pallas_call(
        attend_back_kernel,
        grid=(pairs,),
        in_specs=[
            mine,
            long,
            long,
            pl.BlockSpec((tok, LANES), col),
            mine,
            pl.BlockSpec((1, 8, tok), lambda p: (p, 0, 0)),
            pl.BlockSpec(bias.shape, lambda p: (0, 0, 0)),
            pl.BlockSpec((span, LANES), whole),
            pl.BlockSpec((span, LANES), whole),
        ],
        out_specs=[
            pl.BlockSpec((tok, LANES), out),
            pl.BlockSpec((span, LANES), out),
            pl.BlockSpec((span, LANES), out),
        ],
        out_shape=[
            jax.ShapeDtypeStruct((tok, pairs * LANES), BF16),
            jax.ShapeDtypeStruct((span, pairs * LANES), BF16),
            jax.ShapeDtypeStruct((span, pairs * LANES), BF16),
        ],
        scratch_shapes=[
            pltpu.VMEM((LANES, span), BF16),
            pltpu.VMEM((span, LANES), F32),
            pltpu.VMEM((span, LANES), F32),
        ],
        compiler_params=vmem(56),
        cost_estimate=cost(40 * tok * SPAN * pairs * LANES, pairs << 21, tok * SPAN * 2 * pairs),
        name="attend_back",
    )(q, k, v, o, do, lse, bias, cosine, sine)


def route_kernel(
    experts, att_a, att_b, col_ref, tok_ref, cot_ref, small_ref, past_ref, routes_ref, slots_ref,
    att_ref, residual_ref, hidden_ref, aux_ref, send_ref,
):
    small = small_ref[...]
    gain = small.astype(F32).T[LANES - 1 : LANES, :]
    att_ref[...] = jnp.concatenate([att_a[...], att_b[...]], axis=1)
    residual = tok_ref[...].astype(F32) + dot(att_ref[...], col_ref[...])
    scale = norm_scale(residual)
    hidden = (residual * scale * gain).astype(BF16)
    residual_ref[...] = residual
    hidden_ref[...] = hidden
    mixed = dot(hidden, small)
    logits = mixed + past_ref[...]
    lane = lanes_of(logits.shape)
    routes = routes_ref[...]
    picked = [
        jnp.sum(jnp.where(lane == routes[:, k : k + 1], logits, 0.0), axis=1, keepdims=True)
        for k in range(2)
    ]
    top = jnp.maximum(picked[0], picked[1])
    raised = [jnp.exp(x - top) for x in picked]
    total = raised[0] + raised[1]
    gates = [x / total for x in raised]
    names = experts + 4
    aux = [gates[0], gates[1]]
    for c in range(2):
        pair = [mixed[:, names + 2 * c + i : names + 2 * c + i + 1] for i in range(2)]
        above = jnp.maximum(pair[0], pair[1])
        up = [jnp.exp(x - above) for x in pair]
        aux += [up[0] / (up[0] + up[1]), up[1] / (up[0] + up[1])]
    aux.append(scale)
    packed = jnp.zeros(logits.shape, F32)
    for i, value in enumerate(aux):
        packed = jnp.where(lane == i, value, packed)
    aux_ref[...] = packed
    cot = cot_ref[...].astype(F32)
    slots = slots_ref[...]
    count, tok = send_ref.shape[0], hidden.shape[0]
    where = lax.broadcasted_iota(jnp.int32, (count, tok), 0)
    hot = [(where == slots[k : k + 1, :]).astype(F32).astype(BF16) for k in range(2)]
    send_ref[:, :D] = dot(hot[0] + hot[1], hidden).astype(BF16)
    grads = dot(hot[0], (gates[0] * cot).astype(BF16)) + dot(hot[1], (gates[1] * cot).astype(BF16))
    send_ref[:, D:] = grads.astype(BF16)


def whole_specs(arrays):
    return [pl.BlockSpec(memory_space=pltpu.VMEM) for _ in arrays]


def route(experts, *args):
    tok = args[0].shape[0]
    outs = [
        jax.ShapeDtypeStruct((tok, D), BF16),
        jax.ShapeDtypeStruct((tok, D), F32),
        jax.ShapeDtypeStruct((tok, D), BF16),
        jax.ShapeDtypeStruct((tok, LANES), F32),
        jax.ShapeDtypeStruct((experts * CAP, 2 * D), BF16),
    ]
    return pl.pallas_call(
        functools.partial(route_kernel, experts),
        in_specs=whole_specs(args),
        out_specs=whole_specs(outs),
        out_shape=outs,
        compiler_params=vmem(56),
        cost_estimate=cost(2 * tok * D * (D + 3 * experts * CAP), 9 << 20),
        name="route",
    )(*args)


def expert_kernel(place, x_ref, *refs):
    count = place.shape[0]
    chunks = refs[: 3 * count]
    out_ref, low_ref, answer, back, gw_ref, uw_ref, dw_ref = refs[3 * count :]
    step = pl.program_id(0)
    height = chunks[0].shape[0]

    @pl.when(step == 0)
    def _():
        answer[...] = jnp.zeros_like(answer)
        back[...] = jnp.zeros_like(back)

    for i in range(count):
        at = pl.ds(pl.multiple_of(place[i] * height, height), height)
        for j, w_ref in enumerate((gw_ref, uw_ref, dw_ref)):
            w_ref[at, :] = chunks[3 * i + j][...]
    rows, grads = x_ref[:, :D], x_ref[:, D:]
    gw, uw, dw = gw_ref[...], uw_ref[...], dw_ref[...]
    pre = dot(rows, gw)
    up = dot(rows, uw)
    grad = dot(grads, dw)
    sigmoid = 1.0 / (1.0 + jnp.exp(-pre))
    active = pre * sigmoid
    hidden = (active * up).astype(BF16)
    gate_low = (grad * up * sigmoid * (1.0 + pre * (1.0 - sigmoid))).astype(BF16)
    up_low = (grad * active).astype(BF16)
    low_ref[0] = gate_low
    low_ref[1] = up_low
    low_ref[2] = hidden
    answer[...] += dot_nt(hidden, dw)
    back[...] += dot_nt(gate_low, gw) + dot_nt(up_low, uw)

    @pl.when(step == pl.num_programs(0) - 1)
    def _():
        out_ref[:, :D] = answer[...].astype(BF16)
        out_ref[:, D:] = back[...].astype(BF16)


def expert_rows(x, place, chunks):
    rows, height = x.shape[0], chunks[0].shape[0]
    tiles = FF // FTILE
    weights, operands = [], []
    for chunk in chunks:
        for j in range(3):
            weights.append(pl.BlockSpec((height, FTILE), lambda s, *_, j=j: (0, j * tiles + s)))
            operands.append(chunk)
    return pl.pallas_call(
        expert_kernel,
        grid_spec=pltpu.PrefetchScalarGridSpec(
            num_scalar_prefetch=1,
            grid=(tiles,),
            in_specs=[pl.BlockSpec((rows, 2 * D), lambda s, *_: (0, 0))] + weights,
            out_specs=[
                pl.BlockSpec((rows, 2 * D), lambda s, *_: (0, 0)),
                pl.BlockSpec((3, rows, FTILE), lambda s, *_: (0, 0, s)),
            ],
            scratch_shapes=[pltpu.VMEM((rows, D), F32)] * 2 + [pltpu.VMEM((D, FTILE), BF16)] * 3,
        ),
        out_shape=[
            jax.ShapeDtypeStruct((rows, 2 * D), BF16),
            jax.ShapeDtypeStruct((3, rows, FF), BF16),
        ],
        compiler_params=vmem(56),
        cost_estimate=cost(12 * rows * D * FF, 20 << 20),
        name="expert_rows",
    )(place, x, *operands)


def expert_sums_kernel(x_ref, low_ref, out_ref, turned):
    step = pl.program_id(0)
    tiles = FF // STILE

    @pl.when(step == 0)
    def _():
        turned[...] = x_ref[:, :D].T

    @pl.when(step == 2 * tiles)
    def _():
        turned[...] = x_ref[:, D:].T

    out_ref[...] = dot(turned[...], low_ref[0]).astype(BF16)


def expert_sums(x, low):
    rows = x.shape[0]
    tiles = FF // STILE
    return pl.pallas_call(
        expert_sums_kernel,
        grid=(3 * tiles,),
        in_specs=[
            pl.BlockSpec((rows, 2 * D), lambda j: (0, 0)),
            pl.BlockSpec((1, rows, STILE), lambda j: (j // tiles, 0, j % tiles)),
        ],
        out_specs=pl.BlockSpec((D, STILE), lambda j: (0, j)),
        out_shape=jax.ShapeDtypeStruct((D, 3 * FF), BF16),
        scratch_shapes=[pltpu.VMEM((D, rows), BF16)],
        compiler_params=vmem(56),
        cost_estimate=cost(6 * rows * D * FF, 20 << 20),
        name="expert_sums",
    )(x, low)


def combine_kernel(
    experts, fsdp, core_ref, back_ref, residual_ref, hidden_ref, cot_ref, aux_ref, small_ref, col_ref, att_ref,
    past_ref, carry_ref, routes_ref, slots_ref,
    layer_ref, rgrad_ref, agrad_ref, logits_ref, mine_ref, theirs_ref, turned_ref, small_sum,
):
    tok = hidden_ref.shape[0]
    names = experts + 4
    slots, routes = slots_ref[...], routes_ref[...]
    count = back_ref.shape[0]
    where = lax.broadcasted_iota(jnp.int32, (tok, count), 1)
    hot = [(where == slots[:, k : k + 1]).astype(F32).astype(BF16) for k in range(2)]
    answers, returned = back_ref[:, :D], back_ref[:, D:]
    values = [dot(hot[k], answers) for k in range(2)]
    hidden_grad = dot(hot[0] + hot[1], returned)
    hidden_low, cot_low = hidden_ref[...], cot_ref[...]
    hidden, cot = hidden_low.astype(F32), cot_low.astype(F32)
    residual = residual_ref[...]
    small = small_ref[...]
    turned = small.astype(F32).T
    aux = aux_ref[...]
    gates = [aux[:, k : k + 1] for k in range(2)]
    mixing = [[aux[:, 2 + 2 * c + i : 3 + 2 * c + i] for i in range(2)] for c in range(2)]
    scale = aux[:, 6:7]
    both = jnp.sum(hidden * cot, axis=1, keepdims=True)
    against = dot(cot_low, small)
    fixed = [against[:, names + 4 + c : names + 5 + c] for c in range(2)]
    constant = [turned[names + 4 + c : names + 5 + c, :] for c in range(2)]

    def on(k, e):
        return (routes[:, k : k + 1] == e).astype(F32)

    gate_grad = []
    for k in range(2):
        total = jnp.sum(values[k] * cot, axis=1, keepdims=True) + on(k, experts + 1) * both
        for c in range(2):
            total += on(k, experts + 2 + c) * (mixing[c][0] * both + mixing[c][1] * fixed[c])
        gate_grad.append(total)
    mean = gates[0] * gate_grad[0] + gates[1] * gate_grad[1]
    chosen = [gates[k] * (gate_grad[k] - mean) for k in range(2)]
    weight = [sum(on(k, experts + 2 + c) * gates[k] for k in range(2)) for c in range(2)]
    copied = sum(on(k, experts + 1) * gates[k] for k in range(2))
    copied += weight[0] * mixing[0][0] + weight[1] * mixing[1][0]
    lane = lanes_of((tok, LANES))
    logit_grad = jnp.where(lane == routes[:, 0:1], chosen[0], 0.0)
    logit_grad += jnp.where(lane == routes[:, 1:2], chosen[1], 0.0)
    wide = logit_grad
    shares = jnp.zeros((tok, LANES), F32)
    output = residual + gates[0] * values[0] + gates[1] * values[1] + copied * hidden
    for c in range(2):
        parts = [weight[c] * both, weight[c] * fixed[c]]
        middle = mixing[c][0] * parts[0] + mixing[c][1] * parts[1]
        for i in range(2):
            wide = jnp.where(lane == names + 2 * c + i, mixing[c][i] * (parts[i] - middle), wide)
        share = weight[c] * mixing[c][1]
        shares = jnp.where(lane == names + 4 + c, share, shares)
        output += share * constant[c]
    layer_ref[...] = output.astype(BF16)
    logits_ref[...] = lax.dot_general(
        logit_grad, carry_ref[...], NT, precision=lax.Precision.HIGHEST,
        preferred_element_type=F32,
    )
    ride = lax.dot_general(
        past_ref[...], pltpu.roll(logit_grad, names + 6, 1), TN, precision=lax.Precision.HIGHEST,
        preferred_element_type=F32,
    )
    high, low = halves(wide)
    hidden_grad += copied * cot + dot_nt(high, small) + dot_nt(low, small)
    scaled = hidden_grad * turned[LANES - 1 : LANES, :]
    residual_grad = (
        cot
        + scale * scaled
        - residual * (scale * scale * scale) * jnp.mean(scaled * residual, axis=1, keepdims=True)
    )
    rgrad_ref[...] = residual_grad
    residual_low = residual_grad.astype(BF16)
    agrad_ref[...] = dot_nt(residual_low, col_ref[...]).astype(BF16)
    gained = jnp.sum((hidden_grad * residual * scale).reshape(tok // 8, 8, D), axis=0)
    gained = jnp.sum(gained, axis=0, keepdims=True)
    column = lax.broadcasted_iota(jnp.int32, (LANES, D), 0)
    second = jnp.where(column == LANES - 1, gained, 0.0).T
    shares_high, shares_low = halves(shares)
    small_grad = (
        second
        + dot_tn(hidden_low, high)
        + dot_tn(hidden_low, low)
        + dot_tn(cot_low, shares_high)
        + dot_tn(cot_low, shares_low)
    )
    height = D // fsdp
    ride = jnp.concatenate([ride[:16], jnp.zeros((height - 16, LANES), F32)], axis=0)
    small_grad += jnp.concatenate([ride] * fsdp, axis=0)
    turned_ref[...] = att_ref[...].T
    small_sum[...] = small_grad.astype(BF16)
    for c, out_ref in enumerate((mine_ref, theirs_ref)):
        core = (core_ref[0] + c) % 2
        store_pieces(out_ref, dot(rows_of_core(turned_ref, core, fsdp), residual_low).astype(BF16), 0)
        store_pieces(out_ref, rows_of_core(small_sum, core, fsdp), D)


def combine(experts, fsdp, *args):
    tok = args[1].shape[0]
    outs = [
        jax.ShapeDtypeStruct((tok, D), BF16),
        jax.ShapeDtypeStruct((tok, D), F32),
        jax.ShapeDtypeStruct((tok, D), BF16),
        jax.ShapeDtypeStruct((tok, LANES), F32),
    ] + piece_shapes(D + LANES, experts)
    return pl.pallas_call(
        functools.partial(combine_kernel, experts, fsdp),
        in_specs=[pl.BlockSpec(memory_space=pltpu.SMEM)] + whole_specs(args),
        out_specs=whole_specs(outs),
        out_shape=outs,
        scratch_shapes=[pltpu.VMEM((D, tok), BF16), pltpu.VMEM((D, LANES), BF16)],
        compiler_params=vmem(56),
        cost_estimate=cost(2 * tok * D * (2 * D + 3 * experts * CAP), 14 << 20),
        name="combine",
    )(core_number(), *args)


def normed_grad_kernel(sizes, *refs):
    grads = refs[: 3 * len(sizes)]
    w_ref, *outs = refs[3 * len(sizes) :]
    step = pl.program_id(0)
    last = pl.num_programs(0) - 1

    def part(kind):
        total, at = None, kind * D
        for i, size in enumerate(sizes):
            term = dot_nt(grads[3 * i + kind][...], w_ref[:, at : at + size])
            total = term if total is None else total + term
            at += size
        return total

    grad = part(1) + part(2)

    for i, ref in enumerate(outs[:-1]):

        @pl.when(step == i)
        def _(ref=ref):
            ref[...] = grad.astype(BF16)

    @pl.when(step == last)
    def _():
        outs[-1][...] = grad + part(0)


def normed_grad(parts, weights):
    sizes = [p[0].shape[1] for p in parts]
    tok, span = parts[0][0].shape[0], parts[0][1].shape[0]
    blocks = span // tok
    fixed = lambda s: (0, 0)
    moving = lambda s: (s, 0)
    specs = []
    for size in sizes:
        specs += [pl.BlockSpec((tok, size), fixed)] + [pl.BlockSpec((tok, size), moving)] * 2
    return pl.pallas_call(
        functools.partial(normed_grad_kernel, sizes),
        grid=(blocks,),
        in_specs=specs + [pl.BlockSpec(weights.shape, fixed)],
        out_specs=[pl.BlockSpec((tok, D), fixed)] * blocks,
        out_shape=[jax.ShapeDtypeStruct((tok, D), BF16)] * (blocks - 1)
        + [jax.ShapeDtypeStruct((tok, D), F32)],
        compiler_params=vmem(56),
        cost_estimate=cost(4 * span * D * D, 16 << 20),
        name="normed_grad",
    )(*[g for p in parts for g in p], weights)


def turn_kernel(x_ref, out_ref):
    out_ref[...] = x_ref[...].T


def turn(x):
    return pl.pallas_call(
        turn_kernel,
        in_specs=whole_specs(range(1)),
        out_specs=pl.BlockSpec(memory_space=pltpu.VMEM),
        out_shape=jax.ShapeDtypeStruct(x.shape[::-1], x.dtype),
        compiler_params=vmem(24),
        cost_estimate=cost(0, 8 << 20),
        name="turn",
    )(x)


def project_grad_kernel(count, core_ref, normed_ref, dq_ref, dk_ref, dv_ref, out_ref):
    own = normed_ref.shape[1] - dq_ref.shape[0]
    turned = rows_of_core(normed_ref, core_ref[0], count)
    for kind, ref in enumerate((dq_ref, dk_ref, dv_ref)):
        left = turned[:, own:] if kind == 0 else turned
        store_pieces(out_ref, dot(left, ref[...]).astype(BF16), kind * D)


def project_grad(core, normed_turned, grads, parts, count):
    span = normed_turned.shape[1]
    out = piece_shapes(3 * D, parts)[0]
    return pl.pallas_call(
        functools.partial(project_grad_kernel, count),
        in_specs=[pl.BlockSpec(memory_space=pltpu.SMEM)] + whole_specs(range(4)),
        out_specs=pl.BlockSpec(memory_space=pltpu.VMEM),
        out_shape=out,
        compiler_params=vmem(56),
        cost_estimate=cost(2 * span * D * D, 8 << 20),
        name="project_grad",
    )(core, normed_turned, *grads)


def after(x, *others):
    return lax.optimization_barrier((x, others))[0]


class Sequence:
    def __init__(self):
        self.last = ()

    def take(self, *values):
        return lax.optimization_barrier((values, self.last))[0]

    def done(self, *values):
        self.last = values


def folded(count):
    return [0] + list(range(1, count, 2)) + list(range(2, count, 2))[::-1]


def siblings(count):
    return [(i, i ^ 1) for i in range(count)]


def ring_gather(x, count, gates):
    chips = count // 2
    order = folded(chips)
    follow = {order[i]: order[(i + 1) % chips] for i in range(chips)}
    pairs = [(2 * z + c, 2 * follow[z] + c) for z in range(chips) for c in range(2)]
    me = lax.axis_index("fsdp")
    chip, core = me // 2, me % 2
    at = jnp.array([order.index(z) for z in range(chips)], jnp.int32)[chip]
    ring = jnp.array(order, jnp.int32)
    chunks, places = [], []
    current = x
    for k in range(chips):
        source = ring[(at - k) % chips]
        chunks += [current, lax.ppermute(current, "fsdp", siblings(count))]
        places += [2 * source + core, 2 * source + 1 - core]
        if k + 1 < chips:
            if 0 < k <= len(gates) and gates[k - 1]:
                current = after(current, *gates[k - 1])
            current = lax.ppermute(current, "fsdp", pairs)
    return chunks, jnp.stack(places).astype(jnp.int32)


def earlier_rows(x, count, others):
    up = [(i, i + 2) for i in range(count - 2)]
    second = lax.ppermute(x, "fsdp", up)
    core = lax.axis_index("fsdp") % 2
    first = after(jnp.where(core == 0, x, second), *others)
    first = lax.ppermute(first, "fsdp", siblings(count))
    return second, first


def return_send(second, first, count):
    core = lax.axis_index("fsdp") % 2
    across = lax.ppermute(first, "fsdp", siblings(count)).astype(F32)
    total = jnp.where(core == 0, second.astype(F32), second.astype(F32) + across).astype(BF16)
    down = [(i + 2, i) for i in range(count - 2)]
    return lax.ppermute(total, "fsdp", down), jnp.where(core == 0, across, 0.0).astype(BF16), total


def quarter_gather(x, experts, count):
    chips = count // 2
    rows, width = x.shape
    each = width // experts
    me, group = lax.axis_index("fsdp"), lax.axis_index("expert")
    chip, core = me // 2, me % 2
    mine = lax.dynamic_slice_in_dim(x, group * each, each, 1)
    fetched = [mine]
    for k in range(1, chips):
        pairs = [(2 * z + c, 2 * ((z + k) % chips) + c) for z in range(chips) for c in range(2)]
        fetched.append(lax.ppermute(mine, "fsdp", pairs))
    stacked = jnp.stack(fetched)
    terms = plane_all(stacked, experts)
    chunks, columns = [], []
    for k in range(experts):
        here = after(terms[0], terms[-1]) if k == 0 else terms[k]
        chunks += [terms[k], sibling(here, count)]
        columns.append(group ^ k)
    blocks = []
    for k in range(chips):
        source = (chip - k) % chips
        blocks += [2 * source + core, 2 * source + 1 - core]
    places = [jnp.stack(p).astype(jnp.int32) for p in (blocks, columns)]
    return chunks, places, stacked


def sibling(x, count):
    return lax.ppermute(x, "fsdp", siblings(count))


def summed(terms):
    total = terms[0].astype(F32)
    for term in terms[1:]:
        total += term.astype(F32)
    return total.astype(BF16)


def plane_send(mine, other, experts):
    group = lax.axis_index("expert")

    def part(k):
        pair = [lax.dynamic_index_in_dim(x, group ^ k, 0, False) for x in (mine, other)]
        return summed(pair)

    parts = [part(k) for k in range(experts)]
    moved = [
        lax.ppermute(parts[k], "expert", [(i, i ^ k) for i in range(experts)])
        for k in range(1, experts)
    ]
    return parts[:1] + moved, parts


def line_send(pair, count):
    chips = count // 2
    chip = lax.axis_index("fsdp") // 2
    pair = [x.reshape(chips, x.shape[-2] // chips, x.shape[-1]) for x in pair]

    def part(k):
        at = (chip + k) % chips
        return summed([lax.dynamic_index_in_dim(x, at, 0, False) for x in pair])

    parts = [part(k) for k in range(chips)]
    moved = []
    for k in range(1, chips):
        pairs = [(2 * z + c, 2 * ((z + k) % chips) + c) for z in range(chips) for c in range(2)]
        moved.append(lax.ppermute(parts[k], "fsdp", pairs))
    return parts[:1] + moved, parts


def plane_all(x, experts):
    terms = [x]
    for k in range(1, experts):
        terms.append(lax.ppermute(x, "expert", [(i, i ^ k) for i in range(experts)]))
    return terms


def plane_columns(terms):
    experts = len(terms)
    terms = jnp.stack(terms)
    group = lax.axis_index("expert")
    parts = [lax.dynamic_index_in_dim(terms, j ^ group, 0, False) for j in range(experts)]
    return jnp.concatenate(parts, axis=1).astype(F32)


def plane_sum(terms):
    terms = [t.astype(F32) for t in terms]
    while len(terms) > 1:
        terms = [terms[i] + terms[i + 1] for i in range(0, len(terms), 2)]
    return terms[0]


def local(
    tokens,
    past_logits,
    routes,
    lengths,
    projector,
    collector,
    router,
    blender,
    constants,
    first_gain,
    second_gain,
    carryover,
    gating,
    upward,
    downward,
    cotangent,
):
    tok = tokens.shape[0]
    experts = lax.axis_size("expert")
    count = lax.axis_size("fsdp")
    names = experts + 4
    hops = WINDOW // tok
    me = lax.axis_index("fsdp")

    shard = projector.shape[0]
    gap = LANES - names - 8
    small = jnp.concatenate(
        [router, blender, constants, jnp.zeros((shard, gap), BF16)]
        + [first_gain[:, None], second_gain[:, None]],
        axis=1,
    )
    width = 3 * D + LANES
    filler = jnp.zeros((shard, -width % (experts * LANES)), BF16)
    shared = jnp.concatenate([projector, small, filler], axis=1)
    chunks, (blocks_at, columns_at), stacked = quarter_gather(shared, experts, count)
    own = jnp.concatenate([gating[0], upward[0], downward[0]], axis=1)
    second, first = earlier_rows(tokens, count, chunks[0::2])
    tokens_all = jnp.concatenate([second, first, tokens], axis=0)
    collector_all = lax.all_gather(collector, "fsdp", axis=0, tiled=True)

    span = tok + WINDOW
    key_positions = (me - hops) * tok + jnp.arange(span, dtype=jnp.int32)
    cosine, sine = rope_tables(key_positions.astype(F32))
    bounds = jnp.cumsum(lengths[0])
    biases = []
    for t in range(tok // QTILE):
        at = me * tok + t * QTILE + jnp.arange(QTILE, dtype=jnp.int32)
        start = jnp.max(jnp.where(bounds[:, None] <= at[None, :], bounds[:, None], 0), axis=0)
        least = jnp.maximum(at - (WINDOW - 1), start)
        keys_at = key_positions[t * QTILE : t * QTILE + SPAN, None]
        inside = (keys_at >= least[None, :]) & (keys_at <= at[None, :])
        biases.append(jnp.where(inside, 0.0, masked_score).astype(F32))
    bias = jnp.stack(biases)
    onehot = (routes[:, :, None] == jnp.arange(experts, dtype=jnp.int32)).astype(BF16)
    per_token = jnp.sum(onehot, axis=1)
    lower = jnp.tril(jnp.ones((tok, tok), BF16), -1)
    before = jnp.dot(lower, per_token, preferred_element_type=F32)
    position_in = jnp.sum(onehot.astype(F32) * before[:, None, :], axis=2).astype(jnp.int32)
    slots = jnp.where(routes < experts, routes * CAP + position_in, experts * CAP)
    past_part = jnp.dot(
        past_logits, carryover, precision=lax.Precision.HIGHEST, preferred_element_type=F32
    )
    past_part = jnp.pad(past_part, ((0, 0), (0, LANES - names)))
    past_wide = jnp.pad(past_logits, ((0, 0), (0, LANES - names)))
    carry_wide = jnp.pad(carryover, ((0, LANES - names), (0, LANES - names)))

    weights, normed_all, q, k, v = project(
        blocks_at, columns_at, chunks, tokens_all, cosine, sine, tok
    )
    small_all = weights[:, 3 * D : 3 * D + LANES]
    half = 4
    att_a, lse_a = attend(q, k, v, bias, 0, half)
    att_b, lse_b = attend(q, k, v, bias, half, PAIRS - half)
    lse = jnp.concatenate([lse_a, lse_b], axis=0)
    attended, residual, hidden, aux, send = route(
        experts, att_a, att_b, collector_all, tokens, cotangent, small_all, past_part, routes, slots.T
    )

    def exchange(x):
        x = x.reshape(experts, CAP, 2 * D)
        x = lax.all_to_all(x, "expert", split_axis=0, concat_axis=0, tiled=True)
        return x.reshape(experts * CAP, 2 * D)

    weight_chunks, weight_places = ring_gather(own, count, [[], [att_a]])
    arrived = exchange(send)
    answers, low = expert_rows(arrived, weight_places, weight_chunks)
    returned = exchange(answers)
    sums = expert_sums(arrived, low)
    sums = lax.psum_scatter(sums, "fsdp", scatter_dimension=0, tiled=True).astype(F32)

    layer_output, residual_grad, attended_grad, logits_grad, *col_grad = combine(
        experts, count, returned, residual, hidden, cotangent, aux, small_all, collector_all,
        attended, past_wide, carry_wide, routes, slots,
    )
    def back(upstream):
        return attend_back(q, k, v, attended, upstream, lse, bias, cosine, sine)

    normed_turned = turn(after(normed_all, send))
    col_mine, col_theirs = col_grad
    core = core_number()
    seq = Sequence()
    col_other = sibling(col_theirs, count)
    grads = back(attended_grad)
    seq.done(grads)
    (col_other,) = seq.take(col_other)
    col_terms, parts = plane_send(col_mine, col_other, experts)
    seq.done(parts)
    (turned,) = seq.take(normed_turned)
    theirs = project_grad(1 - core, turned, grads, experts, count)
    other = sibling(theirs, count)
    seq.done(theirs)
    (turned,) = seq.take(normed_turned)
    mine = project_grad(core, turned, grads, experts, count)
    seq.done(mine)
    (other,) = seq.take(other)
    terms, parts = plane_send(mine, other, experts)
    seq.done(parts)
    again, col_terms = seq.take(weights, col_terms)
    *halo_grads, own_grad = normed_grad([grads], again)
    seq.done(own_grad)
    after_rows, across, total = return_send(*halo_grads, count)
    seq.done(total)
    (terms,) = seq.take(terms)
    merged = jnp.concatenate([summed(terms), summed(col_terms)], axis=1)
    cut = mine.shape[2]
    terms, parts = line_send([merged], count)
    seq.done(parts)
    (terms,) = seq.take(terms)
    merged = summed(terms)
    terms = plane_all(merged, experts)
    seq.done(merged)
    (after_rows,) = seq.take(after_rows)
    own_grad = own_grad + across.astype(F32) + after_rows.astype(F32)
    tokens_wide = tokens.astype(F32)
    first_scale = norm_scale(tokens_wide)
    scaled = own_grad * weights[:, 3 * D + LANES - 2].astype(F32)
    gradient_tokens = (
        residual_grad
        + first_scale * scaled
        - tokens_wide
        * (first_scale * first_scale * first_scale)
        * jnp.mean(scaled * tokens_wide, axis=-1, keepdims=True)
    ).astype(BF16)
    seq.done(gradient_tokens)
    (terms,) = seq.take(terms)
    projector_rows = plane_columns([t[:, :cut] for t in terms])[:, : 3 * D]
    col_rows = plane_columns([t[:, cut:] for t in terms])
    first_rows = jnp.sum(projector.astype(F32) * projector_rows, axis=1) / first_gain.astype(F32)

    return (
        layer_output,
        gradient_tokens,
        logits_grad[:, :names],
        projector_rows,
        col_rows[:, :D],
        col_rows[:, D : D + names],
        col_rows[:, D + names : D + names + 4],
        col_rows[:, D + names + 4 : D + names + 6],
        first_rows,
        col_rows[:, D + LANES - 1],
        col_rows[:names, D + names + 6 : D + 2 * names + 6],
        sums[:, :FF][None],
        sums[:, FF : 2 * FF][None],
        sums[:, 2 * FF :][None],
    )


def solution(mesh):
    rows = P(("expert", "fsdp"), None)
    shared = P("fsdp", None)
    expert = P("expert", "fsdp", None)
    return jax.shard_map(
        local,
        mesh=mesh,
        in_specs=(
            rows, rows, rows, P("expert", None), shared, shared, shared, shared, shared,
            P("fsdp"), P("fsdp"), P(), expert, expert, expert, rows,
        ),
        out_specs=(
            rows, rows, rows, shared, shared, shared, shared, shared,
            P("fsdp"), P("fsdp"), P(), expert, expert, expert,
        ),
        check_vma=False,
    )
```

```python
import functools
import math

import jax
import jax.numpy as jnp
from jax import lax
from jax.experimental import pallas as pl
from jax.experimental.pallas import tpu as pltpu
from jax.sharding import PartitionSpec as P

D = 768
H = 12
HD = 64
FF = 2048
WINDOW = 1024
CAP = 128

epsilon = 1e-06
rope_base = 10000.0
masked_score = -1e30
QTILE = 256
SPAN = QTILE + WINDOW
LANES = 128
PAIRS = H * HD // LANES
FTILE = 512
STILE = 2048
LATE = 6
NT = (((1,), (1,)), ((), ()))
TN = (((0,), (0,)), ((), ()))
F32 = jnp.float32
BF16 = jnp.bfloat16
query_scale = 1.0 / math.sqrt(HD)


def vmem(megabytes):
    return pltpu.CompilerParams(vmem_limit_bytes=megabytes << 20)


def in_hbm(*arrays):
    return [pltpu.with_memory_space_constraint(a, pltpu.HBM) for a in arrays]


def in_vmem(*arrays):
    return [pltpu.with_memory_space_constraint(a, pltpu.VMEM) for a in arrays]


def cost(flops, moved, trans=0, weight=1):
    return pl.CostEstimate(
        flops=int(weight * flops), bytes_accessed=int(weight * moved), transcendentals=int(trans)
    )


def dot(a, b):
    return jnp.dot(a, b, preferred_element_type=F32)


def dot_nt(a, b):
    return lax.dot_general(a, b, NT, preferred_element_type=F32)


def dot_tn(a, b):
    return lax.dot_general(a, b, TN, preferred_element_type=F32)


def halves(x):
    high = x.astype(BF16)
    return high, (x - high.astype(F32)).astype(BF16)


def lanes_of(shape):
    return lax.broadcasted_iota(jnp.int32, shape, len(shape) - 1)


def norm_scale(values):
    return lax.rsqrt(jnp.mean(values * values, axis=-1, keepdims=True) + epsilon)


def piece_shapes(width, parts):
    each = -(-width // (parts * LANES)) * LANES
    return [jax.ShapeDtypeStruct((parts, D // 2, each), BF16)] * 2


def rows_of_core(ref, core, count):
    rows = D // count
    at = [pl.multiple_of((2 * z + core) * rows, rows) for z in range(count // 2)]
    return jnp.concatenate([ref[pl.ds(a, rows), :] for a in at], axis=0)


def store_pieces(out_ref, value, at):
    each = out_ref.shape[2]
    for left in range(0, value.shape[1], LANES):
        part, inner = divmod(at + left, each)
        out_ref[part, :, inner : inner + LANES] = value[:, left : left + LANES]


def core_number():
    return (lax.axis_index("fsdp") % 2).astype(jnp.int32).reshape(1)


def rope_tables(positions):
    lane = jnp.arange(LANES, dtype=jnp.int32)
    half = HD // 2
    freq_index = (lane % half).astype(F32)
    inverse = jnp.exp(freq_index * (-2.0 * math.log(rope_base) / HD))
    angles = positions[:, None] * inverse[None, :]
    sign = jnp.where(lane % HD < half, -1.0, 1.0).astype(F32)
    return jnp.cos(angles), jnp.sin(angles) * sign[None, :]


def swapped(x):
    half = HD // 2
    lane = lanes_of(x.shape)
    return jnp.where(
        lane % HD < half, pltpu.roll(x, LANES - half, 1), pltpu.roll(x, half, 1)
    )


def rotate(x, cosine, sine):
    return x * cosine + swapped(x) * sine


def rotate_back(x, cosine, sine):
    return x * cosine - swapped(x) * sine


def project_kernel(blocks_at, columns_at, *refs):
    chips, parts = blocks_at.shape[0] // 2, columns_at.shape[0]
    chunks = refs[: 2 * parts]
    tok_ref, cos_ref, sin_ref, w_ref, normed_ref, q_ref, k_ref, v_ref = refs[2 * parts :]
    rows, width = chunks[0].shape[1:]
    step = pl.program_id(0)

    @pl.when(step == 0)
    def _():
        for e in range(parts):
            left = pl.multiple_of(columns_at[e] * width, LANES)
            for z in range(chips):
                for c in range(2):
                    above = pl.multiple_of(blocks_at[2 * z + c] * rows, rows)
                    w_ref[pl.ds(above, rows), pl.ds(left, width)] = chunks[2 * e + c][z]

    small = w_ref[:, 3 * D : 3 * D + LANES].astype(F32).T
    gain = small[LANES - 2 : LANES - 1, :]
    x = tok_ref[...].astype(F32)
    normed = (x * norm_scale(x) * gain).astype(BF16)
    normed_ref[...] = normed
    cosine, sine = cos_ref[...], sin_ref[...]
    keys = dot(normed, w_ref[:, D : 2 * D])
    for j in range(PAIRS):
        part = slice(j * LANES, (j + 1) * LANES)
        k_ref[:, part] = rotate(keys[:, part], cosine, sine).astype(BF16)
    v_ref[...] = dot(normed, w_ref[:, 2 * D : 3 * D]).astype(BF16)

    @pl.when(step == pl.num_programs(0) - 1)
    def _():
        queries = dot(normed, w_ref[:, :D])
        for j in range(PAIRS):
            part = slice(j * LANES, (j + 1) * LANES)
            q_ref[:, part] = (rotate(queries[:, part], cosine, sine) * query_scale).astype(BF16)


def project(blocks_at, columns_at, chunks, tokens_all, cosine, sine, tok):
    chips, rows, width = chunks[0].shape
    parts = columns_at.shape[0]
    blocks = tokens_all.shape[0] // tok
    fixed = lambda s, *_: (0, 0)
    moving = lambda s, *_: (s, 0)
    span = tokens_all.shape[0]
    return pl.pallas_call(
        project_kernel,
        grid_spec=pltpu.PrefetchScalarGridSpec(
            num_scalar_prefetch=2,
            grid=(blocks,),
            in_specs=[pl.BlockSpec((chips, rows, width), lambda s, *_: (0, 0, 0))] * len(chunks)
            + [
                pl.BlockSpec((tok, D), moving),
                pl.BlockSpec((tok, LANES), moving),
                pl.BlockSpec((tok, LANES), moving),
            ],
            out_specs=[
                pl.BlockSpec((D, parts * width), fixed),
                pl.BlockSpec((tok, D), moving),
                pl.BlockSpec((tok, D), fixed),
                pl.BlockSpec((tok, D), moving),
                pl.BlockSpec((tok, D), moving),
            ],
        ),
        out_shape=[
            jax.ShapeDtypeStruct((D, parts * width), BF16),
            jax.ShapeDtypeStruct((span, D), BF16),
            jax.ShapeDtypeStruct((tok, D), BF16),
            jax.ShapeDtypeStruct((span, D), BF16),
            jax.ShapeDtypeStruct((span, D), BF16),
        ],
        compiler_params=vmem(24),
        cost_estimate=cost(2 * span * D * 2 * D, 20 << 20),
        name="project",
    )(blocks_at, columns_at, *chunks, tokens_all, cosine, sine)


def head_mask(x, head):
    return jnp.where(lanes_of(x.shape) // HD == head, x, jnp.zeros_like(x))


def both_heads(x):
    return jnp.concatenate([head_mask(x, 0), head_mask(x, 1)], axis=0)


def own_head(x):
    return jnp.concatenate([x[:HD, :QTILE], x[HD:, QTILE:]], axis=0).T


def attend_kernel(q_ref, k_ref, v_ref, bias_ref, o_ref, lse_ref, vt_ref):
    vt_ref[...] = v_ref[...].T
    for t in range(q_ref.shape[0] // QTILE):
        rows = slice(t * QTILE, (t + 1) * QTILE)
        span = slice(t * QTILE, t * QTILE + SPAN)
        s = dot_nt(k_ref[span, :], both_heads(q_ref[rows, :]))
        s += jnp.concatenate([bias_ref[t]] * 2, axis=1)
        top = jnp.max(s, axis=0, keepdims=True)
        e = jnp.exp(s - top)
        total = jnp.sum(e, axis=0, keepdims=True)
        o_ref[rows, :] = own_head(dot(vt_ref[:, span], e.astype(BF16)) / total).astype(BF16)
        lse = top + jnp.log(total)
        for h in range(2):
            lse_ref[0, h : h + 1, rows] = lse[:, h * QTILE : (h + 1) * QTILE]


def attend(q, k, v, bias, first, pairs):
    tok, span = q.shape[0], k.shape[0]
    col = lambda p: (0, first + p)
    return pl.pallas_call(
        attend_kernel,
        grid=(pairs,),
        in_specs=[
            pl.BlockSpec((tok, LANES), col),
            pl.BlockSpec((span, LANES), col),
            pl.BlockSpec((span, LANES), col),
            pl.BlockSpec(bias.shape, lambda p: (0, 0, 0)),
        ],
        out_specs=[
            pl.BlockSpec((tok, LANES), lambda p: (0, p)),
            pl.BlockSpec((1, 8, tok), lambda p: (p, 0, 0)),
        ],
        out_shape=[
            jax.ShapeDtypeStruct((tok, pairs * LANES), BF16),
            jax.ShapeDtypeStruct((pairs, 8, tok), F32),
        ],
        scratch_shapes=[pltpu.VMEM((LANES, span), BF16)],
        compiler_params=vmem(24),
        cost_estimate=cost(16 * tok * SPAN * pairs * LANES, pairs << 20, tok * SPAN * 2 * pairs),
        name="attend",
    )(q, k, v, bias)


def attend_back_kernel(
    q_ref, k_ref, v_ref, o_ref, do_ref, lse_ref, bias_ref, cos_ref, sin_ref,
    dq_ref, dk_ref, dv_ref, kt_ref, dk_sum, dv_sum,
):
    tok = q_ref.shape[0]
    own = k_ref.shape[0] - tok
    kt_ref[...] = k_ref[...].T
    dk_sum[...] = jnp.zeros_like(dk_sum)
    dv_sum[...] = jnp.zeros_like(dv_sum)
    for t in range(tok // QTILE):
        rows = slice(t * QTILE, (t + 1) * QTILE)
        span = slice(t * QTILE, t * QTILE + SPAN)
        keys, values = k_ref[span, :], v_ref[span, :]
        queries, upstream = q_ref[rows, :], do_ref[rows, :]
        product = (upstream.astype(F32) * o_ref[rows, :].astype(F32)).T
        qh, gh = both_heads(queries), both_heads(upstream)
        lse = jnp.concatenate([lse_ref[0, h : h + 1, rows] for h in range(2)], axis=1)
        delta = jnp.concatenate(
            [jnp.sum(product[h * HD : (h + 1) * HD], axis=0, keepdims=True) for h in range(2)],
            axis=1,
        )
        s = dot_nt(keys, qh) + jnp.concatenate([bias_ref[t]] * 2, axis=1)
        p = jnp.exp(s - lse)
        ds = (p * (dot_nt(values, gh) - delta)).astype(BF16)
        dv_sum[span, :] += dot(p.astype(BF16), gh)
        dk_sum[span, :] += dot(ds, qh)
        dq = own_head(dot(kt_ref[:, span], ds))
        there = slice(own + t * QTILE, own + (t + 1) * QTILE)
        dq = rotate_back(dq, cos_ref[there, :], sin_ref[there, :]) * query_scale
        dq_ref[rows, :] = dq.astype(BF16)
    dk_ref[...] = rotate_back(dk_sum[...], cos_ref[...], sin_ref[...]).astype(BF16)
    dv_ref[...] = dv_sum[...].astype(BF16)


def attend_back(q, k, v, o, do, lse, bias, cosine, sine):
    tok, span = q.shape[0], k.shape[0]
    pairs = PAIRS
    col = out = lambda p: (0, p)
    whole = lambda p: (0, 0)
    mine = pl.BlockSpec((tok, LANES), col)
    long = pl.BlockSpec((span, LANES), col)
    return pl.pallas_call(
        attend_back_kernel,
        grid=(pairs,),
        in_specs=[
            mine,
            long,
            long,
            pl.BlockSpec((tok, LANES), col),
            mine,
            pl.BlockSpec((1, 8, tok), lambda p: (p, 0, 0)),
            pl.BlockSpec(bias.shape, lambda p: (0, 0, 0)),
            pl.BlockSpec((span, LANES), whole),
            pl.BlockSpec((span, LANES), whole),
        ],
        out_specs=[
            pl.BlockSpec((tok, LANES), out),
            pl.BlockSpec((span, LANES), out),
            pl.BlockSpec((span, LANES), out),
        ],
        out_shape=[
            pltpu.VMEM((tok, pairs * LANES), BF16),
            pltpu.VMEM((span, pairs * LANES), BF16),
            pltpu.VMEM((span, pairs * LANES), BF16),
        ],
        scratch_shapes=[
            pltpu.VMEM((LANES, span), BF16),
            pltpu.VMEM((span, LANES), F32),
            pltpu.VMEM((span, LANES), F32),
        ],
        compiler_params=vmem(32),
        cost_estimate=cost(40 * tok * SPAN * pairs * LANES, pairs << 21, tok * SPAN * 2 * pairs, weight=LATE),
        name="attend_back",
    )(*in_hbm(q, k, v, o, do), lse, *in_hbm(bias, cosine, sine))


def route_kernel(
    experts, att_a, att_b, col_ref, tok_ref, cot_ref, small_ref, past_ref, routes_ref, slots_ref,
    att_ref, residual_ref, hidden_ref, aux_ref, send_ref,
):
    small = small_ref[...]
    gain = small.astype(F32).T[LANES - 1 : LANES, :]
    att_ref[...] = jnp.concatenate([att_a[...], att_b[...]], axis=1)
    residual = tok_ref[...].astype(F32) + dot(att_ref[...], col_ref[...])
    scale = norm_scale(residual)
    hidden = (residual * scale * gain).astype(BF16)
    residual_ref[...] = residual
    hidden_ref[...] = hidden
    mixed = dot(hidden, small)
    logits = mixed + past_ref[...]
    lane = lanes_of(logits.shape)
    routes = routes_ref[...]
    picked = [
        jnp.sum(jnp.where(lane == routes[:, k : k + 1], logits, 0.0), axis=1, keepdims=True)
        for k in range(2)
    ]
    top = jnp.maximum(picked[0], picked[1])
    raised = [jnp.exp(x - top) for x in picked]
    total = raised[0] + raised[1]
    gates = [x / total for x in raised]
    names = experts + 4
    aux = [gates[0], gates[1]]
    for c in range(2):
        pair = [mixed[:, names + 2 * c + i : names + 2 * c + i + 1] for i in range(2)]
        above = jnp.maximum(pair[0], pair[1])
        up = [jnp.exp(x - above) for x in pair]
        aux += [up[0] / (up[0] + up[1]), up[1] / (up[0] + up[1])]
    aux.append(scale)
    packed = jnp.zeros(logits.shape, F32)
    for i, value in enumerate(aux):
        packed = jnp.where(lane == i, value, packed)
    aux_ref[...] = packed
    cot = cot_ref[...].astype(F32)
    slots = slots_ref[...]
    count, tok = send_ref.shape[0], hidden.shape[0]
    where = lax.broadcasted_iota(jnp.int32, (count, tok), 0)
    hot = [(where == slots[k : k + 1, :]).astype(F32).astype(BF16) for k in range(2)]
    send_ref[:, :D] = dot(hot[0] + hot[1], hidden).astype(BF16)
    grads = dot(hot[0], (gates[0] * cot).astype(BF16)) + dot(hot[1], (gates[1] * cot).astype(BF16))
    send_ref[:, D:] = grads.astype(BF16)


def whole_specs(arrays):
    return [pl.BlockSpec(memory_space=pltpu.VMEM) for _ in arrays]


def route(experts, *args):
    tok = args[0].shape[0]
    outs = [
        jax.ShapeDtypeStruct((tok, D), BF16),
        jax.ShapeDtypeStruct((tok, D), F32),
        jax.ShapeDtypeStruct((tok, D), BF16),
        jax.ShapeDtypeStruct((tok, LANES), F32),
        jax.ShapeDtypeStruct((experts * CAP, 2 * D), BF16),
    ]
    return pl.pallas_call(
        functools.partial(route_kernel, experts),
        in_specs=whole_specs(args),
        out_specs=whole_specs(outs),
        out_shape=outs,
        compiler_params=vmem(56),
        cost_estimate=cost(2 * tok * D * (D + 3 * experts * CAP), 9 << 20),
        name="route",
    )(*args)


def expert_kernel(place, x_ref, *refs):
    count = place.shape[0]
    chunks = refs[: 3 * count]
    out_ref, low_ref, answer, back, gw_ref, uw_ref, dw_ref = refs[3 * count :]
    step = pl.program_id(0)
    height = chunks[0].shape[0]

    @pl.when(step == 0)
    def _():
        answer[...] = jnp.zeros_like(answer)
        back[...] = jnp.zeros_like(back)

    for i in range(count):
        at = pl.ds(pl.multiple_of(place[i] * height, height), height)
        for j, w_ref in enumerate((gw_ref, uw_ref, dw_ref)):
            w_ref[at, :] = chunks[3 * i + j][...]
    rows, grads = x_ref[:, :D], x_ref[:, D:]
    gw, uw, dw = gw_ref[...], uw_ref[...], dw_ref[...]
    pre = dot(rows, gw)
    up = dot(rows, uw)
    grad = dot(grads, dw)
    sigmoid = 1.0 / (1.0 + jnp.exp(-pre))
    active = pre * sigmoid
    hidden = (active * up).astype(BF16)
    gate_low = (grad * up * sigmoid * (1.0 + pre * (1.0 - sigmoid))).astype(BF16)
    up_low = (grad * active).astype(BF16)
    low_ref[0] = gate_low
    low_ref[1] = up_low
    low_ref[2] = hidden
    answer[...] += dot_nt(hidden, dw)
    back[...] += dot_nt(gate_low, gw) + dot_nt(up_low, uw)

    @pl.when(step == pl.num_programs(0) - 1)
    def _():
        out_ref[:, :D] = answer[...].astype(BF16)
        out_ref[:, D:] = back[...].astype(BF16)


def expert_rows(x, place, chunks):
    rows, height = x.shape[0], chunks[0].shape[0]
    tiles = FF // FTILE
    weights, operands = [], []
    for chunk in chunks:
        for j in range(3):
            weights.append(pl.BlockSpec((height, FTILE), lambda s, *_, j=j: (0, j * tiles + s)))
            operands.append(chunk)
    return pl.pallas_call(
        expert_kernel,
        grid_spec=pltpu.PrefetchScalarGridSpec(
            num_scalar_prefetch=1,
            grid=(tiles,),
            in_specs=[pl.BlockSpec((rows, 2 * D), lambda s, *_: (0, 0))] + weights,
            out_specs=[
                pl.BlockSpec((rows, 2 * D), lambda s, *_: (0, 0)),
                pl.BlockSpec((3, rows, FTILE), lambda s, *_: (0, 0, s)),
            ],
            scratch_shapes=[pltpu.VMEM((rows, D), F32)] * 2 + [pltpu.VMEM((D, FTILE), BF16)] * 3,
        ),
        out_shape=[
            jax.ShapeDtypeStruct((rows, 2 * D), BF16),
            pltpu.HBM((3, rows, FF), BF16),
        ],
        compiler_params=vmem(32),
        cost_estimate=cost(12 * rows * D * FF, 20 << 20),
        name="expert_rows",
    )(place, x, *operands)


def expert_sums_kernel(x_ref, low_ref, out_ref, turned):
    step = pl.program_id(0)
    tiles = FF // STILE

    @pl.when(step == 0)
    def _():
        turned[...] = x_ref[:, :D].T

    @pl.when(step == 2 * tiles)
    def _():
        turned[...] = x_ref[:, D:].T

    out_ref[...] = dot(turned[...], low_ref[0]).astype(BF16)


def expert_sums(x, low):
    rows = x.shape[0]
    tiles = FF // STILE
    return pl.pallas_call(
        expert_sums_kernel,
        grid=(3 * tiles,),
        in_specs=[
            pl.BlockSpec((rows, 2 * D), lambda j: (0, 0)),
            pl.BlockSpec((1, rows, STILE), lambda j: (j // tiles, 0, j % tiles)),
        ],
        out_specs=pl.BlockSpec((D, STILE), lambda j: (0, j)),
        out_shape=pltpu.HBM((D, 3 * FF), BF16),
        scratch_shapes=[pltpu.VMEM((D, rows), BF16)],
        compiler_params=vmem(24),
        cost_estimate=cost(6 * rows * D * FF, 20 << 20),
        name="expert_sums",
    )(x, *in_hbm(low))


def combine_kernel(
    experts, fsdp, core_ref, back_ref, residual_ref, hidden_ref, cot_ref, aux_ref, small_ref, col_ref, att_ref,
    past_ref, carry_ref, routes_ref, slots_ref,
    layer_ref, rgrad_ref, agrad_ref, logits_ref, mine_ref, theirs_ref, turned_ref, small_sum,
):
    tok = hidden_ref.shape[0]
    names = experts + 4
    slots, routes = slots_ref[...], routes_ref[...]
    count = back_ref.shape[0]
    where = lax.broadcasted_iota(jnp.int32, (tok, count), 1)
    hot = [(where == slots[:, k : k + 1]).astype(F32).astype(BF16) for k in range(2)]
    answers, returned = back_ref[:, :D], back_ref[:, D:]
    values = [dot(hot[k], answers) for k in range(2)]
    hidden_grad = dot(hot[0] + hot[1], returned)
    hidden_low, cot_low = hidden_ref[...], cot_ref[...]
    hidden, cot = hidden_low.astype(F32), cot_low.astype(F32)
    residual = residual_ref[...]
    small = small_ref[...]
    turned = small.astype(F32).T
    aux = aux_ref[...]
    gates = [aux[:, k : k + 1] for k in range(2)]
    mixing = [[aux[:, 2 + 2 * c + i : 3 + 2 * c + i] for i in range(2)] for c in range(2)]
    scale = aux[:, 6:7]
    both = jnp.sum(hidden * cot, axis=1, keepdims=True)
    against = dot(cot_low, small)
    fixed = [against[:, names + 4 + c : names + 5 + c] for c in range(2)]
    constant = [turned[names + 4 + c : names + 5 + c, :] for c in range(2)]

    def on(k, e):
        return (routes[:, k : k + 1] == e).astype(F32)

    gate_grad = []
    for k in range(2):
        total = jnp.sum(values[k] * cot, axis=1, keepdims=True) + on(k, experts + 1) * both
        for c in range(2):
            total += on(k, experts + 2 + c) * (mixing[c][0] * both + mixing[c][1] * fixed[c])
        gate_grad.append(total)
    mean = gates[0] * gate_grad[0] + gates[1] * gate_grad[1]
    chosen = [gates[k] * (gate_grad[k] - mean) for k in range(2)]
    weight = [sum(on(k, experts + 2 + c) * gates[k] for k in range(2)) for c in range(2)]
    copied = sum(on(k, experts + 1) * gates[k] for k in range(2))
    copied += weight[0] * mixing[0][0] + weight[1] * mixing[1][0]
    lane = lanes_of((tok, LANES))
    logit_grad = jnp.where(lane == routes[:, 0:1], chosen[0], 0.0)
    logit_grad += jnp.where(lane == routes[:, 1:2], chosen[1], 0.0)
    wide = logit_grad
    shares = jnp.zeros((tok, LANES), F32)
    output = residual + gates[0] * values[0] + gates[1] * values[1] + copied * hidden
    for c in range(2):
        parts = [weight[c] * both, weight[c] * fixed[c]]
        middle = mixing[c][0] * parts[0] + mixing[c][1] * parts[1]
        for i in range(2):
            wide = jnp.where(lane == names + 2 * c + i, mixing[c][i] * (parts[i] - middle), wide)
        share = weight[c] * mixing[c][1]
        shares = jnp.where(lane == names + 4 + c, share, shares)
        output += share * constant[c]
    layer_ref[...] = output.astype(BF16)
    logits_ref[...] = lax.dot_general(
        logit_grad, carry_ref[...], NT, precision=lax.Precision.HIGHEST,
        preferred_element_type=F32,
    )
    ride = lax.dot_general(
        past_ref[...], pltpu.roll(logit_grad, names + 6, 1), TN, precision=lax.Precision.HIGHEST,
        preferred_element_type=F32,
    )
    high, low = halves(wide)
    hidden_grad += copied * cot + dot_nt(high, small) + dot_nt(low, small)
    scaled = hidden_grad * turned[LANES - 1 : LANES, :]
    residual_grad = (
        cot
        + scale * scaled
        - residual * (scale * scale * scale) * jnp.mean(scaled * residual, axis=1, keepdims=True)
    )
    rgrad_ref[...] = residual_grad
    residual_low = residual_grad.astype(BF16)
    agrad_ref[...] = dot_nt(residual_low, col_ref[...]).astype(BF16)
    gained = jnp.sum((hidden_grad * residual * scale).reshape(tok // 8, 8, D), axis=0)
    gained = jnp.sum(gained, axis=0, keepdims=True)
    column = lax.broadcasted_iota(jnp.int32, (LANES, D), 0)
    second = jnp.where(column == LANES - 1, gained, 0.0).T
    shares_high, shares_low = halves(shares)
    small_grad = (
        second
        + dot_tn(hidden_low, high)
        + dot_tn(hidden_low, low)
        + dot_tn(cot_low, shares_high)
        + dot_tn(cot_low, shares_low)
    )
    height = D // fsdp
    ride = jnp.concatenate([ride[:16], jnp.zeros((height - 16, LANES), F32)], axis=0)
    small_grad += jnp.concatenate([ride] * fsdp, axis=0)
    turned_ref[...] = att_ref[...].T
    small_sum[...] = small_grad.astype(BF16)
    for c, out_ref in enumerate((mine_ref, theirs_ref)):
        core = (core_ref[0] + c) % 2
        store_pieces(out_ref, dot(rows_of_core(turned_ref, core, fsdp), residual_low).astype(BF16), 0)
        store_pieces(out_ref, rows_of_core(small_sum, core, fsdp), D)


def combine(experts, fsdp, *args):
    tok = args[1].shape[0]
    outs = [
        jax.ShapeDtypeStruct((tok, D), BF16),
        jax.ShapeDtypeStruct((tok, D), F32),
        jax.ShapeDtypeStruct((tok, D), BF16),
        jax.ShapeDtypeStruct((tok, LANES), F32),
    ] + piece_shapes(D + LANES, experts)
    return pl.pallas_call(
        functools.partial(combine_kernel, experts, fsdp),
        in_specs=[pl.BlockSpec(memory_space=pltpu.SMEM)] + whole_specs(args),
        out_specs=whole_specs(outs),
        out_shape=outs,
        scratch_shapes=[pltpu.VMEM((D, tok), BF16), pltpu.VMEM((D, LANES), BF16)],
        compiler_params=vmem(56),
        cost_estimate=cost(2 * tok * D * (2 * D + 3 * experts * CAP), 14 << 20, weight=LATE),
        name="combine",
    )(core_number(), *args)


def normed_grad_kernel(sizes, *refs):
    grads = refs[: 3 * len(sizes)]
    w_ref, *outs = refs[3 * len(sizes) :]
    step = pl.program_id(0)
    last = pl.num_programs(0) - 1

    def part(kind):
        total, at = None, kind * D
        for i, size in enumerate(sizes):
            term = dot_nt(grads[3 * i + kind][...], w_ref[:, at : at + size])
            total = term if total is None else total + term
            at += size
        return total

    grad = part(1) + part(2)

    for i, ref in enumerate(outs[:-1]):

        @pl.when(step == i)
        def _(ref=ref):
            ref[...] = grad.astype(BF16)

    @pl.when(step == last)
    def _():
        outs[-1][...] = grad + part(0)


def normed_grad(parts, weights):
    sizes = [p[0].shape[1] for p in parts]
    tok, span = parts[0][0].shape[0], parts[0][1].shape[0]
    blocks = span // tok
    fixed = lambda s: (0, 0)
    moving = lambda s: (s, 0)
    specs = []
    for size in sizes:
        specs += [pl.BlockSpec((tok, size), fixed)] + [pl.BlockSpec((tok, size), moving)] * 2
    return pl.pallas_call(
        functools.partial(normed_grad_kernel, sizes),
        grid=(blocks,),
        in_specs=specs + [pl.BlockSpec(weights.shape, fixed)],
        out_specs=[pl.BlockSpec((tok, D), fixed)] * blocks,
        out_shape=[jax.ShapeDtypeStruct((tok, D), BF16)] * (blocks - 1)
        + [jax.ShapeDtypeStruct((tok, D), F32)],
        compiler_params=vmem(24),
        cost_estimate=cost(4 * span * D * D, 16 << 20, weight=LATE),
        name="normed_grad",
    )(*in_vmem(*[g for p in parts for g in p]), weights)


def turn_kernel(x_ref, out_ref):
    out_ref[...] = x_ref[...].T


def turn(x):
    return pl.pallas_call(
        turn_kernel,
        in_specs=whole_specs(range(1)),
        out_specs=pl.BlockSpec(memory_space=pltpu.VMEM),
        out_shape=jax.ShapeDtypeStruct(x.shape[::-1], x.dtype),
        compiler_params=vmem(24),
        cost_estimate=cost(0, 8 << 20),
        name="turn",
    )(x)


def project_grad_kernel(count, core_ref, normed_ref, dq_ref, dk_ref, dv_ref, out_ref):
    own = normed_ref.shape[1] - dq_ref.shape[0]
    turned = rows_of_core(normed_ref, core_ref[0], count)
    for kind, ref in enumerate((dq_ref, dk_ref, dv_ref)):
        left = turned[:, own:] if kind == 0 else turned
        store_pieces(out_ref, dot(left, ref[...]).astype(BF16), kind * D)


def project_grad(core, normed_turned, grads, parts, count):
    span = normed_turned.shape[1]
    out = piece_shapes(3 * D, parts)[0]
    return pl.pallas_call(
        functools.partial(project_grad_kernel, count),
        in_specs=[pl.BlockSpec(memory_space=pltpu.SMEM)] + whole_specs(range(4)),
        out_specs=pl.BlockSpec(memory_space=pltpu.VMEM),
        out_shape=out,
        compiler_params=vmem(24),
        cost_estimate=cost(2 * span * D * D, 8 << 20, weight=LATE),
        name="project_grad",
    )(core, normed_turned, *in_vmem(*grads))


def after(x, *others):
    return lax.optimization_barrier((x, others))[0]


class Sequence:
    def __init__(self):
        self.last = ()

    def take(self, *values):
        return lax.optimization_barrier((values, self.last))[0]

    def done(self, *values):
        self.last = values


def folded(count):
    return [0] + list(range(1, count, 2)) + list(range(2, count, 2))[::-1]


def siblings(count):
    return [(i, i ^ 1) for i in range(count)]


def ring_gather(x, count, gates):
    chips = count // 2
    order = folded(chips)
    follow = {order[i]: order[(i + 1) % chips] for i in range(chips)}
    pairs = [(2 * z + c, 2 * follow[z] + c) for z in range(chips) for c in range(2)]
    me = lax.axis_index("fsdp")
    chip, core = me // 2, me % 2
    at = jnp.array([order.index(z) for z in range(chips)], jnp.int32)[chip]
    ring = jnp.array(order, jnp.int32)
    chunks, places = [], []
    current = x
    for k in range(chips):
        source = ring[(at - k) % chips]
        chunks += [current, lax.ppermute(current, "fsdp", siblings(count))]
        places += [2 * source + core, 2 * source + 1 - core]
        if k + 1 < chips:
            if 0 < k <= len(gates) and gates[k - 1]:
                current = after(current, *gates[k - 1])
            current = lax.ppermute(current, "fsdp", pairs)
    return chunks, jnp.stack(places).astype(jnp.int32)


def earlier_rows(x, count, others):
    up = [(i, i + 2) for i in range(count - 2)]
    second = lax.ppermute(x, "fsdp", up)
    core = lax.axis_index("fsdp") % 2
    first = after(jnp.where(core == 0, x, second), *others)
    first = lax.ppermute(first, "fsdp", siblings(count))
    return second, first


def return_send(second, across, count):
    core = lax.axis_index("fsdp") % 2
    across = across.astype(F32)
    total = jnp.where(core == 0, second.astype(F32), second.astype(F32) + across).astype(BF16)
    down = [(i + 2, i) for i in range(count - 2)]
    return lax.ppermute(total, "fsdp", down), jnp.where(core == 0, across, 0.0).astype(BF16), total


def quarter_gather(x, experts, count):
    chips = count // 2
    rows, width = x.shape
    each = width // experts
    me, group = lax.axis_index("fsdp"), lax.axis_index("expert")
    chip, core = me // 2, me % 2
    mine = lax.dynamic_slice_in_dim(x, group * each, each, 1)
    fetched = [mine]
    for k in range(1, chips):
        pairs = [(2 * z + c, 2 * ((z + k) % chips) + c) for z in range(chips) for c in range(2)]
        fetched.append(lax.ppermute(mine, "fsdp", pairs))
    stacked = jnp.stack(fetched)
    terms = plane_all(stacked, experts)
    chunks, columns = [], []
    for k in range(experts):
        here = after(terms[0], terms[-1]) if k == 0 else terms[k]
        chunks += [terms[k], sibling(here, count)]
        columns.append(group ^ k)
    blocks = []
    for k in range(chips):
        source = (chip - k) % chips
        blocks += [2 * source + core, 2 * source + 1 - core]
    places = [jnp.stack(p).astype(jnp.int32) for p in (blocks, columns)]
    return chunks, places, stacked


def sibling(x, count):
    return lax.ppermute(x, "fsdp", siblings(count))


def summed(terms):
    total = terms[0].astype(F32)
    for term in terms[1:]:
        total += term.astype(F32)
    return total.astype(BF16)


def in_plane(x):
    return lax.all_to_all(x, "expert", split_axis=0, concat_axis=0, tiled=True)


def plane_send(mine, other, experts):
    group = lax.axis_index("expert")

    def part(k):
        pair = [lax.dynamic_index_in_dim(x, group ^ k, 0, False) for x in (mine, other)]
        return summed(pair)

    parts = [part(k) for k in range(experts)]
    moved = [
        lax.ppermute(parts[k], "expert", [(i, i ^ k) for i in range(experts)])
        for k in range(1, experts)
    ]
    return parts[:1] + moved, parts


def line_send(pair, count):
    chips = count // 2
    chip = lax.axis_index("fsdp") // 2
    pair = [x.reshape(chips, x.shape[-2] // chips, x.shape[-1]) for x in pair]

    def part(k):
        at = (chip + k) % chips
        return summed([lax.dynamic_index_in_dim(x, at, 0, False) for x in pair])

    parts = [part(k) for k in range(chips)]
    moved = []
    for k in range(1, chips):
        pairs = [(2 * z + c, 2 * ((z + k) % chips) + c) for z in range(chips) for c in range(2)]
        moved.append(lax.ppermute(parts[k], "fsdp", pairs))
    return parts[:1] + moved, parts


def plane_all(x, experts):
    terms = [x]
    for k in range(1, experts):
        terms.append(lax.ppermute(x, "expert", [(i, i ^ k) for i in range(experts)]))
    return terms


def plane_columns(terms):
    experts = len(terms)
    terms = jnp.stack(terms)
    group = lax.axis_index("expert")
    parts = [lax.dynamic_index_in_dim(terms, j ^ group, 0, False) for j in range(experts)]
    return jnp.concatenate(parts, axis=1).astype(F32)


def plane_sum(terms):
    terms = [t.astype(F32) for t in terms]
    while len(terms) > 1:
        terms = [terms[i] + terms[i + 1] for i in range(0, len(terms), 2)]
    return terms[0]


def local(
    tokens,
    past_logits,
    routes,
    lengths,
    projector,
    collector,
    router,
    blender,
    constants,
    first_gain,
    second_gain,
    carryover,
    gating,
    upward,
    downward,
    cotangent,
):
    tok = tokens.shape[0]
    experts = lax.axis_size("expert")
    count = lax.axis_size("fsdp")
    names = experts + 4
    hops = WINDOW // tok
    me = lax.axis_index("fsdp")

    shard = projector.shape[0]
    gap = LANES - names - 8
    small = jnp.concatenate(
        [router, blender, constants, jnp.zeros((shard, gap), BF16)]
        + [first_gain[:, None], second_gain[:, None]],
        axis=1,
    )
    width = 3 * D + LANES
    filler = jnp.zeros((shard, -width % (experts * LANES)), BF16)
    shared = jnp.concatenate([projector, small, filler], axis=1)
    chunks, (blocks_at, columns_at), stacked = quarter_gather(shared, experts, count)
    own = jnp.concatenate([gating[0], upward[0], downward[0]], axis=1)
    second, first = earlier_rows(tokens, count, chunks[0::2])
    tokens_all = jnp.concatenate([second, first, tokens], axis=0)
    collector_all = lax.all_gather(collector, "fsdp", axis=0, tiled=True)

    span = tok + WINDOW
    key_positions = (me - hops) * tok + jnp.arange(span, dtype=jnp.int32)
    cosine, sine = rope_tables(key_positions.astype(F32))
    bounds = jnp.cumsum(lengths[0])
    biases = []
    for t in range(tok // QTILE):
        at = me * tok + t * QTILE + jnp.arange(QTILE, dtype=jnp.int32)
        start = jnp.max(jnp.where(bounds[:, None] <= at[None, :], bounds[:, None], 0), axis=0)
        least = jnp.maximum(at - (WINDOW - 1), start)
        keys_at = key_positions[t * QTILE : t * QTILE + SPAN, None]
        inside = (keys_at >= least[None, :]) & (keys_at <= at[None, :])
        biases.append(jnp.where(inside, 0.0, masked_score).astype(F32))
    bias = jnp.stack(biases)
    onehot = (routes[:, :, None] == jnp.arange(experts, dtype=jnp.int32)).astype(BF16)
    per_token = jnp.sum(onehot, axis=1)
    lower = jnp.tril(jnp.ones((tok, tok), BF16), -1)
    before = jnp.dot(lower, per_token, preferred_element_type=F32)
    position_in = jnp.sum(onehot.astype(F32) * before[:, None, :], axis=2).astype(jnp.int32)
    slots = jnp.where(routes < experts, routes * CAP + position_in, experts * CAP)
    past_part = jnp.dot(
        past_logits, carryover, precision=lax.Precision.HIGHEST, preferred_element_type=F32
    )
    past_part = jnp.pad(past_part, ((0, 0), (0, LANES - names)))
    past_wide = jnp.pad(past_logits, ((0, 0), (0, LANES - names)))
    carry_wide = jnp.pad(carryover, ((0, LANES - names), (0, LANES - names)))

    weights, normed_all, q, k, v = project(
        blocks_at, columns_at, chunks, tokens_all, cosine, sine, tok
    )
    small_all = weights[:, 3 * D : 3 * D + LANES]
    half = 4
    att_a, lse_a = attend(q, k, v, bias, 0, half)
    att_b, lse_b = attend(q, k, v, bias, half, PAIRS - half)
    lse = jnp.concatenate([lse_a, lse_b], axis=0)
    attended, residual, hidden, aux, send = route(
        experts, att_a, att_b, collector_all, tokens, cotangent, small_all, past_part, routes, slots.T
    )

    def exchange(x):
        x = x.reshape(experts, CAP, 2 * D)
        x = lax.all_to_all(x, "expert", split_axis=0, concat_axis=0, tiled=True)
        return x.reshape(experts * CAP, 2 * D)

    weight_chunks, weight_places = ring_gather(own, count, [[q], [send]])
    arrived = exchange(send)
    answers, low = expert_rows(arrived, weight_places, weight_chunks)
    returned = exchange(answers)
    sums = expert_sums(arrived, low)
    sums = lax.psum_scatter(sums, "fsdp", scatter_dimension=0, tiled=True)

    layer_output, residual_grad, attended_grad, logits_grad, *col_grad = combine(
        experts, count, returned, residual, hidden, cotangent, aux, small_all, collector_all,
        attended, past_wide, carry_wide, routes, slots,
    )
    def back(upstream):
        return attend_back(q, k, v, attended, upstream, lse, bias, cosine, sine)

    normed_turned = turn(after(normed_all, send))
    col_mine, col_theirs = col_grad
    core = core_number()
    seq = Sequence()
    col_other = sibling(col_theirs, count)
    grads = back(attended_grad)
    seq.done(grads)
    (col_other,) = seq.take(col_other)
    col_terms, parts = plane_send(col_mine, col_other, experts)
    seq.done(parts)
    (turned,) = seq.take(normed_turned)
    theirs = project_grad(1 - core, turned, grads, experts, count)
    other = sibling(theirs, count)
    seq.done(theirs)
    (again,) = seq.take(weights)
    *halo_grads, own_grad = normed_grad([grads], again)
    across = sibling(halo_grads[1], count)
    seq.done(own_grad)
    (turned,) = seq.take(normed_turned)
    mine = project_grad(core, turned, grads, experts, count)
    seq.done(mine)
    (other,) = seq.take(other)
    terms, parts = plane_send(mine, other, experts)
    seq.done(parts)
    (across,) = seq.take(across)
    after_rows, across, total = return_send(halo_grads[0], across, count)
    seq.done(total)
    (col_terms,) = seq.take(col_terms)
    col_part = summed(col_terms)
    seq.done(col_part)
    (terms,) = seq.take(terms)
    merged = jnp.concatenate([summed(terms), col_part], axis=1)
    cut = mine.shape[2]
    terms, parts = line_send([merged], count)
    seq.done(parts)
    (sums,) = seq.take(sums)
    sums = sums.astype(F32)
    seq.done(sums)
    (terms,) = seq.take(terms)
    merged = summed(terms)
    terms = plane_all(merged, experts)
    seq.done(merged)
    (after_rows,) = seq.take(after_rows)
    own_grad = own_grad + across.astype(F32) + after_rows.astype(F32)
    tokens_wide = tokens.astype(F32)
    first_scale = norm_scale(tokens_wide)
    scaled = own_grad * weights[:, 3 * D + LANES - 2].astype(F32)
    gradient_tokens = (
        residual_grad
        + first_scale * scaled
        - tokens_wide
        * (first_scale * first_scale * first_scale)
        * jnp.mean(scaled * tokens_wide, axis=-1, keepdims=True)
    ).astype(BF16)
    seq.done(gradient_tokens)
    (terms,) = seq.take(terms)
    projector_rows = plane_columns([t[:, :cut] for t in terms])[:, : 3 * D]
    col_rows = plane_columns([t[:, cut:] for t in terms])
    first_rows = jnp.sum(projector.astype(F32) * projector_rows, axis=1) / first_gain.astype(F32)

    return (
        layer_output,
        gradient_tokens,
        logits_grad[:, :names],
        projector_rows,
        col_rows[:, :D],
        col_rows[:, D : D + names],
        col_rows[:, D + names : D + names + 4],
        col_rows[:, D + names + 4 : D + names + 6],
        first_rows,
        col_rows[:, D + LANES - 1],
        col_rows[:names, D + names + 6 : D + 2 * names + 6],
        sums[:, :FF][None],
        sums[:, FF : 2 * FF][None],
        sums[:, 2 * FF :][None],
    )


def solution(mesh):
    rows = P(("expert", "fsdp"), None)
    shared = P("fsdp", None)
    expert = P("expert", "fsdp", None)
    return jax.shard_map(
        local,
        mesh=mesh,
        in_specs=(
            rows, rows, rows, P("expert", None), shared, shared, shared, shared, shared,
            P("fsdp"), P("fsdp"), P(), expert, expert, expert, rows,
        ),
        out_specs=(
            rows, rows, rows, shared, shared, shared, shared, shared,
            P("fsdp"), P("fsdp"), P(), expert, expert, expert,
        ),
        check_vma=False,
    )
```

```python
import functools
import math

import jax
import jax.numpy as jnp
from jax import lax
from jax.experimental import pallas as pl
from jax.experimental.pallas import tpu as pltpu
from jax.sharding import PartitionSpec as P

D = 768
H = 12
HD = 64
FF = 2048
WINDOW = 1024
CAP = 128

epsilon = 1e-06
rope_base = 10000.0
masked_score = -1e30
QTILE = 256
SPAN = QTILE + WINDOW
LANES = 128
PAIRS = H * HD // LANES
FTILE = 512
STILE = 2048
LATE = 6
NT = (((1,), (1,)), ((), ()))
TN = (((0,), (0,)), ((), ()))
F32 = jnp.float32
BF16 = jnp.bfloat16
query_scale = 1.0 / math.sqrt(HD)


def vmem(megabytes):
    return pltpu.CompilerParams(vmem_limit_bytes=megabytes << 20)


def in_hbm(*arrays):
    return [pltpu.with_memory_space_constraint(a, pltpu.HBM) for a in arrays]


def in_vmem(*arrays):
    return [pltpu.with_memory_space_constraint(a, pltpu.VMEM) for a in arrays]


def cost(flops, moved, trans=0, weight=1):
    return pl.CostEstimate(
        flops=int(weight * flops), bytes_accessed=int(weight * moved), transcendentals=int(trans)
    )


def dot(a, b):
    return jnp.dot(a, b, preferred_element_type=F32)


def dot_nt(a, b):
    return lax.dot_general(a, b, NT, preferred_element_type=F32)


def dot_tn(a, b):
    return lax.dot_general(a, b, TN, preferred_element_type=F32)


def halves(x):
    high = x.astype(BF16)
    return high, (x - high.astype(F32)).astype(BF16)


def lanes_of(shape):
    return lax.broadcasted_iota(jnp.int32, shape, len(shape) - 1)


def norm_scale(values):
    return lax.rsqrt(jnp.mean(values * values, axis=-1, keepdims=True) + epsilon)


def piece_shapes(width, parts):
    each = -(-width // (parts * LANES)) * LANES
    return [jax.ShapeDtypeStruct((parts, D // 2, each), BF16)] * 2


def rows_of_core(ref, core, count):
    rows = D // count
    at = [pl.multiple_of((2 * z + core) * rows, rows) for z in range(count // 2)]
    return jnp.concatenate([ref[pl.ds(a, rows), :] for a in at], axis=0)


def store_pieces(out_ref, value, at):
    each = out_ref.shape[2]
    for left in range(0, value.shape[1], LANES):
        part, inner = divmod(at + left, each)
        out_ref[part, :, inner : inner + LANES] = value[:, left : left + LANES]


def core_number():
    return (lax.axis_index("fsdp") % 2).astype(jnp.int32).reshape(1)


def rope_tables(positions):
    lane = jnp.arange(LANES, dtype=jnp.int32)
    half = HD // 2
    freq_index = (lane % half).astype(F32)
    inverse = jnp.exp(freq_index * (-2.0 * math.log(rope_base) / HD))
    angles = positions[:, None] * inverse[None, :]
    sign = jnp.where(lane % HD < half, -1.0, 1.0).astype(F32)
    return jnp.cos(angles), jnp.sin(angles) * sign[None, :]


def swapped(x):
    half = HD // 2
    lane = lanes_of(x.shape)
    return jnp.where(
        lane % HD < half, pltpu.roll(x, LANES - half, 1), pltpu.roll(x, half, 1)
    )


def rotate(x, cosine, sine):
    return x * cosine + swapped(x) * sine


def rotate_back(x, cosine, sine):
    return x * cosine - swapped(x) * sine


def project_kernel(blocks_at, columns_at, *refs):
    chips, parts = blocks_at.shape[0] // 2, columns_at.shape[0]
    chunks = refs[: 2 * parts]
    *tok_refs, cos_ref, sin_ref, w_ref, small_ref, normed_ref, q_ref, k_ref, v_ref, x_ref = refs[
        2 * parts :
    ]
    rows, width = chunks[0].shape[1:]
    step = pl.program_id(0)

    @pl.when(step == 0)
    def _():
        for e in range(parts):
            left = pl.multiple_of(columns_at[e] * width, LANES)
            for z in range(chips):
                for c in range(2):
                    above = pl.multiple_of(blocks_at[2 * z + c] * rows, rows)
                    w_ref[pl.ds(above, rows), pl.ds(left, width)] = chunks[2 * e + c][z]
        small_ref[...] = w_ref[:, 3 * D : 3 * D + LANES]

    for i, ref in enumerate(tok_refs):

        @pl.when(step == i)
        def _(ref=ref):
            x_ref[...] = ref[...]

    gain = small_ref[...].astype(F32).T[LANES - 2 : LANES - 1, :]
    x = x_ref[...].astype(F32)
    normed = (x * norm_scale(x) * gain).astype(BF16)
    normed_ref[...] = normed
    cosine, sine = cos_ref[...], sin_ref[...]
    keys = dot(normed, w_ref[:, D : 2 * D])
    for j in range(PAIRS):
        part = slice(j * LANES, (j + 1) * LANES)
        k_ref[:, part] = rotate(keys[:, part], cosine, sine).astype(BF16)
    v_ref[...] = dot(normed, w_ref[:, 2 * D : 3 * D]).astype(BF16)

    @pl.when(step == pl.num_programs(0) - 1)
    def _():
        queries = dot(normed, w_ref[:, :D])
        for j in range(PAIRS):
            part = slice(j * LANES, (j + 1) * LANES)
            q_ref[:, part] = (rotate(queries[:, part], cosine, sine) * query_scale).astype(BF16)


def project(blocks_at, columns_at, chunks, tokens, cosine, sine):
    chips, rows, width = chunks[0].shape
    parts = columns_at.shape[0]
    blocks, tok = len(tokens), tokens[0].shape[0]
    fixed = lambda s, *_: (0, 0)
    moving = lambda s, *_: (s, 0)
    span = blocks * tok
    return pl.pallas_call(
        project_kernel,
        grid_spec=pltpu.PrefetchScalarGridSpec(
            num_scalar_prefetch=2,
            grid=(blocks,),
            in_specs=[pl.BlockSpec((chips, rows, width), lambda s, *_: (0, 0, 0))] * len(chunks)
            + [pl.BlockSpec((tok, D), fixed)] * blocks
            + [pl.BlockSpec((tok, LANES), moving)] * 2,
            out_specs=[
                pl.BlockSpec((D, parts * width), fixed),
                pl.BlockSpec((D, LANES), fixed),
                pl.BlockSpec((tok, D), moving),
                pl.BlockSpec((tok, D), fixed),
                pl.BlockSpec((tok, D), moving),
                pl.BlockSpec((tok, D), moving),
            ],
            scratch_shapes=[pltpu.VMEM((tok, D), BF16)],
        ),
        out_shape=[
            jax.ShapeDtypeStruct((D, parts * width), BF16),
            jax.ShapeDtypeStruct((D, LANES), BF16),
            jax.ShapeDtypeStruct((span, D), BF16),
            jax.ShapeDtypeStruct((tok, D), BF16),
            jax.ShapeDtypeStruct((span, D), BF16),
            jax.ShapeDtypeStruct((span, D), BF16),
        ],
        compiler_params=vmem(24),
        cost_estimate=cost(2 * span * D * 2 * D, 20 << 20),
        name="project",
    )(blocks_at, columns_at, *chunks, *tokens, cosine, sine)


def head_mask(x, head):
    return jnp.where(lanes_of(x.shape) // HD == head, x, jnp.zeros_like(x))


def both_heads(x):
    return jnp.concatenate([head_mask(x, 0), head_mask(x, 1)], axis=0)


def own_head(x):
    return jnp.concatenate([x[:HD, :QTILE], x[HD:, QTILE:]], axis=0).T


def attend_kernel(q_ref, k_ref, v_ref, bias_ref, o_ref, lse_ref, vt_ref):
    vt_ref[...] = v_ref[...].T
    for t in range(q_ref.shape[0] // QTILE):
        rows = slice(t * QTILE, (t + 1) * QTILE)
        span = slice(t * QTILE, t * QTILE + SPAN)
        s = dot_nt(k_ref[span, :], both_heads(q_ref[rows, :]))
        s += jnp.concatenate([bias_ref[t]] * 2, axis=1)
        top = jnp.max(s, axis=0, keepdims=True)
        e = jnp.exp(s - top)
        total = jnp.sum(e, axis=0, keepdims=True)
        o_ref[rows, :] = own_head(dot(vt_ref[:, span], e.astype(BF16)) / total).astype(BF16)
        lse = top + jnp.log(total)
        for h in range(2):
            lse_ref[0, h : h + 1, rows] = lse[:, h * QTILE : (h + 1) * QTILE]


def attend(q, k, v, bias, first, pairs):
    tok, span = q.shape[0], k.shape[0]
    col = lambda p: (0, first + p)
    return pl.pallas_call(
        attend_kernel,
        grid=(pairs,),
        in_specs=[
            pl.BlockSpec((tok, LANES), col),
            pl.BlockSpec((span, LANES), col),
            pl.BlockSpec((span, LANES), col),
            pl.BlockSpec(bias.shape, lambda p: (0, 0, 0)),
        ],
        out_specs=[
            pl.BlockSpec((tok, LANES), lambda p: (0, p)),
            pl.BlockSpec((1, 8, tok), lambda p: (p, 0, 0)),
        ],
        out_shape=[
            jax.ShapeDtypeStruct((tok, pairs * LANES), BF16),
            jax.ShapeDtypeStruct((pairs, 8, tok), F32),
        ],
        scratch_shapes=[pltpu.VMEM((LANES, span), BF16)],
        compiler_params=vmem(24),
        cost_estimate=cost(16 * tok * SPAN * pairs * LANES, pairs << 20, tok * SPAN * 2 * pairs),
        name="attend",
    )(q, k, v, bias)


def weigh_kernel(q_ref, k_ref, lse_ref, bias_ref, p_ref):
    for t in range(q_ref.shape[0] // QTILE):
        rows = slice(t * QTILE, (t + 1) * QTILE)
        lse = jnp.concatenate([lse_ref[0, h : h + 1, rows] for h in range(2)], axis=1)
        s = dot_nt(k_ref[t * QTILE : t * QTILE + SPAN, :], both_heads(q_ref[rows, :]))
        s += jnp.concatenate([bias_ref[t]] * 2, axis=1)
        p_ref[0, t] = jnp.exp(s - lse).astype(BF16)


def weigh(q, k, lse, bias):
    tok, span = q.shape[0], k.shape[0]
    col = lambda p: (0, p)
    shape = (PAIRS, tok // QTILE, SPAN, 2 * QTILE)
    return pl.pallas_call(
        weigh_kernel,
        grid=(PAIRS,),
        in_specs=[
            pl.BlockSpec((tok, LANES), col),
            pl.BlockSpec((span, LANES), col),
            pl.BlockSpec((1, 8, tok), lambda p: (p, 0, 0)),
            pl.BlockSpec(bias.shape, lambda p: (0, 0, 0)),
        ],
        out_specs=pl.BlockSpec((1, *shape[1:]), lambda p: (p, 0, 0, 0)),
        out_shape=pltpu.HBM(shape, BF16),
        compiler_params=vmem(32),
        cost_estimate=cost(8 * tok * SPAN * D, 20 << 20),
        name="weigh",
    )(*in_hbm(q, k), lse, bias)


def attend_back_kernel(
    q_ref, k_ref, v_ref, o_ref, do_ref, p_ref, cos_ref, sin_ref,
    dq_ref, dk_ref, dv_ref, kt_ref, dk_sum, dv_sum,
):
    tok = q_ref.shape[0]
    own = k_ref.shape[0] - tok
    kt_ref[...] = k_ref[...].T
    dk_sum[...] = jnp.zeros_like(dk_sum)
    dv_sum[...] = jnp.zeros_like(dv_sum)
    for t in range(tok // QTILE):
        rows = slice(t * QTILE, (t + 1) * QTILE)
        span = slice(t * QTILE, t * QTILE + SPAN)
        values = v_ref[span, :]
        queries, upstream = q_ref[rows, :], do_ref[rows, :]
        product = (upstream.astype(F32) * o_ref[rows, :].astype(F32)).T
        qh, gh = both_heads(queries), both_heads(upstream)
        delta = jnp.concatenate(
            [jnp.sum(product[h * HD : (h + 1) * HD], axis=0, keepdims=True) for h in range(2)],
            axis=1,
        )
        p = p_ref[0, t]
        ds = (p.astype(F32) * (dot_nt(values, gh) - delta)).astype(BF16)
        dv_sum[span, :] += dot(p, gh)
        dk_sum[span, :] += dot(ds, qh)
        dq = own_head(dot(kt_ref[:, span], ds))
        there = slice(own + t * QTILE, own + (t + 1) * QTILE)
        dq = rotate_back(dq, cos_ref[there, :], sin_ref[there, :]) * query_scale
        dq_ref[rows, :] = dq.astype(BF16)
    dk_ref[...] = rotate_back(dk_sum[...], cos_ref[...], sin_ref[...]).astype(BF16)
    dv_ref[...] = dv_sum[...].astype(BF16)


def attend_back(q, k, v, o, do, p, cosine, sine):
    tok, span = q.shape[0], k.shape[0]
    pairs = PAIRS
    col = out = lambda p: (0, p)
    whole = lambda p: (0, 0)
    mine = pl.BlockSpec((tok, LANES), col)
    long = pl.BlockSpec((span, LANES), col)
    return pl.pallas_call(
        attend_back_kernel,
        grid=(pairs,),
        in_specs=[
            mine,
            long,
            long,
            pl.BlockSpec((tok, LANES), col),
            mine,
            pl.BlockSpec((1, *p.shape[1:]), lambda p: (p, 0, 0, 0)),
            pl.BlockSpec((span, LANES), whole),
            pl.BlockSpec((span, LANES), whole),
        ],
        out_specs=[
            pl.BlockSpec((tok, LANES), out),
            pl.BlockSpec((span, LANES), out),
            pl.BlockSpec((span, LANES), out),
        ],
        out_shape=[
            pltpu.VMEM((tok, pairs * LANES), BF16),
            pltpu.VMEM((span, pairs * LANES), BF16),
            pltpu.VMEM((span, pairs * LANES), BF16),
        ],
        scratch_shapes=[
            pltpu.VMEM((LANES, span), BF16),
            pltpu.VMEM((span, LANES), F32),
            pltpu.VMEM((span, LANES), F32),
        ],
        compiler_params=vmem(32),
        cost_estimate=cost(40 * tok * SPAN * pairs * LANES, pairs << 21, tok * SPAN * 2 * pairs, weight=LATE),
        name="attend_back",
    )(*in_hbm(q, k, v, o, do, p, cosine, sine))


def route_kernel(
    experts, att_a, att_b, col_ref, tok_ref, cot_ref, small_ref, past_ref, routes_ref, slots_ref,
    att_ref, residual_ref, hidden_ref, aux_ref, send_ref,
):
    small = small_ref[...]
    gain = small.astype(F32).T[LANES - 1 : LANES, :]
    att_ref[...] = jnp.concatenate([att_a[...], att_b[...]], axis=1)
    residual = tok_ref[...].astype(F32) + dot(att_ref[...], col_ref[...])
    scale = norm_scale(residual)
    hidden = (residual * scale * gain).astype(BF16)
    residual_ref[...] = residual
    hidden_ref[...] = hidden
    mixed = dot(hidden, small)
    logits = mixed + past_ref[...]
    lane = lanes_of(logits.shape)
    routes = routes_ref[...]
    picked = [
        jnp.sum(jnp.where(lane == routes[:, k : k + 1], logits, 0.0), axis=1, keepdims=True)
        for k in range(2)
    ]
    top = jnp.maximum(picked[0], picked[1])
    raised = [jnp.exp(x - top) for x in picked]
    total = raised[0] + raised[1]
    gates = [x / total for x in raised]
    names = experts + 4
    aux = [gates[0], gates[1]]
    for c in range(2):
        pair = [mixed[:, names + 2 * c + i : names + 2 * c + i + 1] for i in range(2)]
        above = jnp.maximum(pair[0], pair[1])
        up = [jnp.exp(x - above) for x in pair]
        aux += [up[0] / (up[0] + up[1]), up[1] / (up[0] + up[1])]
    aux.append(scale)
    packed = jnp.zeros(logits.shape, F32)
    for i, value in enumerate(aux):
        packed = jnp.where(lane == i, value, packed)
    aux_ref[...] = packed
    cot = cot_ref[...].astype(F32)
    slots = slots_ref[...]
    count, tok = send_ref.shape[0], hidden.shape[0]
    where = lax.broadcasted_iota(jnp.int32, (count, tok), 0)
    hot = [(where == slots[k : k + 1, :]).astype(F32).astype(BF16) for k in range(2)]
    send_ref[:, :D] = dot(hot[0] + hot[1], hidden).astype(BF16)
    grads = dot(hot[0], (gates[0] * cot).astype(BF16)) + dot(hot[1], (gates[1] * cot).astype(BF16))
    send_ref[:, D:] = grads.astype(BF16)


def whole_specs(arrays):
    return [pl.BlockSpec(memory_space=pltpu.VMEM) for _ in arrays]


def route(experts, *args):
    tok = args[0].shape[0]
    outs = [
        jax.ShapeDtypeStruct((tok, D), BF16),
        jax.ShapeDtypeStruct((tok, D), F32),
        jax.ShapeDtypeStruct((tok, D), BF16),
        jax.ShapeDtypeStruct((tok, LANES), F32),
        jax.ShapeDtypeStruct((experts * CAP, 2 * D), BF16),
    ]
    return pl.pallas_call(
        functools.partial(route_kernel, experts),
        in_specs=whole_specs(args),
        out_specs=whole_specs(outs),
        out_shape=outs,
        compiler_params=vmem(56),
        cost_estimate=cost(2 * tok * D * (D + 3 * experts * CAP), 9 << 20),
        name="route",
    )(*args)


def expert_kernel(place, x_ref, *refs):
    count = place.shape[0]
    chunks = refs[: 3 * count]
    out_ref, low_ref, answer, back, gw_ref, uw_ref, dw_ref = refs[3 * count :]
    step = pl.program_id(0)
    height = chunks[0].shape[0]

    @pl.when(step == 0)
    def _():
        answer[...] = jnp.zeros_like(answer)
        back[...] = jnp.zeros_like(back)

    for i in range(count):
        at = pl.ds(pl.multiple_of(place[i] * height, height), height)
        for j, w_ref in enumerate((gw_ref, uw_ref, dw_ref)):
            w_ref[at, :] = chunks[3 * i + j][...]
    rows, grads = x_ref[:, :D], x_ref[:, D:]
    gw, uw, dw = gw_ref[...], uw_ref[...], dw_ref[...]
    pre = dot(rows, gw)
    up = dot(rows, uw)
    grad = dot(grads, dw)
    sigmoid = 1.0 / (1.0 + jnp.exp(-pre))
    active = pre * sigmoid
    hidden = (active * up).astype(BF16)
    gate_low = (grad * up * sigmoid * (1.0 + pre * (1.0 - sigmoid))).astype(BF16)
    up_low = (grad * active).astype(BF16)
    low_ref[0] = gate_low
    low_ref[1] = up_low
    low_ref[2] = hidden
    answer[...] += dot_nt(hidden, dw)
    back[...] += dot_nt(gate_low, gw) + dot_nt(up_low, uw)

    @pl.when(step == pl.num_programs(0) - 1)
    def _():
        out_ref[:, :D] = answer[...].astype(BF16)
        out_ref[:, D:] = back[...].astype(BF16)


def expert_rows(x, place, chunks):
    rows, height = x.shape[0], chunks[0].shape[0]
    tiles = FF // FTILE
    weights, operands = [], []
    for chunk in chunks:
        for j in range(3):
            weights.append(pl.BlockSpec((height, FTILE), lambda s, *_, j=j: (0, j * tiles + s)))
            operands.append(chunk)
    return pl.pallas_call(
        expert_kernel,
        grid_spec=pltpu.PrefetchScalarGridSpec(
            num_scalar_prefetch=1,
            grid=(tiles,),
            in_specs=[pl.BlockSpec((rows, 2 * D), lambda s, *_: (0, 0))] + weights,
            out_specs=[
                pl.BlockSpec((rows, 2 * D), lambda s, *_: (0, 0)),
                pl.BlockSpec((3, rows, FTILE), lambda s, *_: (0, 0, s)),
            ],
            scratch_shapes=[pltpu.VMEM((rows, D), F32)] * 2 + [pltpu.VMEM((D, FTILE), BF16)] * 3,
        ),
        out_shape=[
            jax.ShapeDtypeStruct((rows, 2 * D), BF16),
            pltpu.HBM((3, rows, FF), BF16),
        ],
        compiler_params=vmem(32),
        cost_estimate=cost(12 * rows * D * FF, 20 << 20),
        name="expert_rows",
    )(place, x, *operands)


def expert_sums_kernel(x_ref, low_ref, out_ref, turned):
    step = pl.program_id(0)
    tiles = FF // STILE

    @pl.when(step == 0)
    def _():
        turned[...] = x_ref[:, :D].T

    @pl.when(step == 2 * tiles)
    def _():
        turned[...] = x_ref[:, D:].T

    out_ref[...] = dot(turned[...], low_ref[0]).astype(BF16)


def expert_sums(x, low):
    rows = x.shape[0]
    tiles = FF // STILE
    return pl.pallas_call(
        expert_sums_kernel,
        grid=(3 * tiles,),
        in_specs=[
            pl.BlockSpec((rows, 2 * D), lambda j: (0, 0)),
            pl.BlockSpec((1, rows, STILE), lambda j: (j // tiles, 0, j % tiles)),
        ],
        out_specs=pl.BlockSpec((D, STILE), lambda j: (0, j)),
        out_shape=pltpu.HBM((D, 3 * FF), BF16),
        scratch_shapes=[pltpu.VMEM((D, rows), BF16)],
        compiler_params=vmem(24),
        cost_estimate=cost(6 * rows * D * FF, 20 << 20),
        name="expert_sums",
    )(x, *in_hbm(low))


def combine_kernel(
    experts, fsdp, core_ref, back_ref, residual_ref, hidden_ref, cot_ref, aux_ref, small_ref, col_ref, att_ref,
    past_ref, carry_ref, routes_ref, slots_ref,
    layer_ref, rgrad_ref, agrad_ref, logits_ref, mine_ref, theirs_ref, small_sum,
):
    tok = hidden_ref.shape[0]
    names = experts + 4
    slots, routes = slots_ref[...], routes_ref[...]
    count = back_ref.shape[0]
    where = lax.broadcasted_iota(jnp.int32, (tok, count), 1)
    hot = [(where == slots[:, k : k + 1]).astype(F32).astype(BF16) for k in range(2)]
    answers, returned = back_ref[:, :D], back_ref[:, D:]
    values = [dot(hot[k], answers) for k in range(2)]
    hidden_grad = dot(hot[0] + hot[1], returned)
    hidden_low, cot_low = hidden_ref[...], cot_ref[...]
    hidden, cot = hidden_low.astype(F32), cot_low.astype(F32)
    residual = residual_ref[...]
    small = small_ref[...]
    turned = small.astype(F32).T
    aux = aux_ref[...]
    gates = [aux[:, k : k + 1] for k in range(2)]
    mixing = [[aux[:, 2 + 2 * c + i : 3 + 2 * c + i] for i in range(2)] for c in range(2)]
    scale = aux[:, 6:7]
    both = jnp.sum(hidden * cot, axis=1, keepdims=True)
    against = dot(cot_low, small)
    fixed = [against[:, names + 4 + c : names + 5 + c] for c in range(2)]
    constant = [turned[names + 4 + c : names + 5 + c, :] for c in range(2)]

    def on(k, e):
        return (routes[:, k : k + 1] == e).astype(F32)

    gate_grad = []
    for k in range(2):
        total = jnp.sum(values[k] * cot, axis=1, keepdims=True) + on(k, experts + 1) * both
        for c in range(2):
            total += on(k, experts + 2 + c) * (mixing[c][0] * both + mixing[c][1] * fixed[c])
        gate_grad.append(total)
    mean = gates[0] * gate_grad[0] + gates[1] * gate_grad[1]
    chosen = [gates[k] * (gate_grad[k] - mean) for k in range(2)]
    weight = [sum(on(k, experts + 2 + c) * gates[k] for k in range(2)) for c in range(2)]
    copied = sum(on(k, experts + 1) * gates[k] for k in range(2))
    copied += weight[0] * mixing[0][0] + weight[1] * mixing[1][0]
    lane = lanes_of((tok, LANES))
    logit_grad = jnp.where(lane == routes[:, 0:1], chosen[0], 0.0)
    logit_grad += jnp.where(lane == routes[:, 1:2], chosen[1], 0.0)
    wide = logit_grad
    shares = jnp.zeros((tok, LANES), F32)
    output = residual + gates[0] * values[0] + gates[1] * values[1] + copied * hidden
    for c in range(2):
        parts = [weight[c] * both, weight[c] * fixed[c]]
        middle = mixing[c][0] * parts[0] + mixing[c][1] * parts[1]
        for i in range(2):
            wide = jnp.where(lane == names + 2 * c + i, mixing[c][i] * (parts[i] - middle), wide)
        share = weight[c] * mixing[c][1]
        shares = jnp.where(lane == names + 4 + c, share, shares)
        output += share * constant[c]
    layer_ref[...] = output.astype(BF16)
    logits_ref[...] = lax.dot_general(
        logit_grad, carry_ref[...], NT, precision=lax.Precision.HIGHEST,
        preferred_element_type=F32,
    )
    ride = lax.dot_general(
        past_ref[...], pltpu.roll(logit_grad, names + 6, 1), TN, precision=lax.Precision.HIGHEST,
        preferred_element_type=F32,
    )
    high, low = halves(wide)
    hidden_grad += copied * cot + dot_nt(high, small) + dot_nt(low, small)
    scaled = hidden_grad * turned[LANES - 1 : LANES, :]
    residual_grad = (
        cot
        + scale * scaled
        - residual * (scale * scale * scale) * jnp.mean(scaled * residual, axis=1, keepdims=True)
    )
    rgrad_ref[...] = residual_grad
    residual_low = residual_grad.astype(BF16)
    agrad_ref[...] = dot_nt(residual_low, col_ref[...]).astype(BF16)
    gained = jnp.sum((hidden_grad * residual * scale).reshape(tok // 8, 8, D), axis=0)
    gained = jnp.sum(gained, axis=0, keepdims=True)
    column = lax.broadcasted_iota(jnp.int32, (LANES, D), 0)
    second = jnp.where(column == LANES - 1, gained, 0.0).T
    shares_high, shares_low = halves(shares)
    small_grad = (
        second
        + dot_tn(hidden_low, high)
        + dot_tn(hidden_low, low)
        + dot_tn(cot_low, shares_high)
        + dot_tn(cot_low, shares_low)
    )
    height = D // fsdp
    ride = jnp.concatenate([ride[:16], jnp.zeros((height - 16, LANES), F32)], axis=0)
    small_grad += jnp.concatenate([ride] * fsdp, axis=0)
    small_sum[...] = small_grad.astype(BF16)
    for c, out_ref in enumerate((mine_ref, theirs_ref)):
        core = (core_ref[0] + c) % 2
        store_pieces(out_ref, dot(rows_of_core(att_ref, core, fsdp), residual_low).astype(BF16), 0)
        store_pieces(out_ref, rows_of_core(small_sum, core, fsdp), D)


def combine(experts, fsdp, *args):
    tok = args[1].shape[0]
    outs = [
        jax.ShapeDtypeStruct((tok, D), BF16),
        jax.ShapeDtypeStruct((tok, D), F32),
        jax.ShapeDtypeStruct((tok, D), BF16),
        jax.ShapeDtypeStruct((tok, LANES), F32),
    ] + piece_shapes(D + LANES, experts)
    return pl.pallas_call(
        functools.partial(combine_kernel, experts, fsdp),
        in_specs=[pl.BlockSpec(memory_space=pltpu.SMEM)] + whole_specs(args),
        out_specs=whole_specs(outs),
        out_shape=outs,
        scratch_shapes=[pltpu.VMEM((D, LANES), BF16)],
        compiler_params=vmem(56),
        cost_estimate=cost(2 * tok * D * (2 * D + 3 * experts * CAP), 14 << 20, weight=LATE),
        name="combine",
    )(core_number(), *args)


def normed_grad_kernel(sizes, *refs):
    grads = refs[: 3 * len(sizes)]
    w_ref, *outs = refs[3 * len(sizes) :]
    step = pl.program_id(0)
    last = pl.num_programs(0) - 1

    def part(kind):
        total, at = None, kind * D
        for i, size in enumerate(sizes):
            term = dot_nt(grads[3 * i + kind][...], w_ref[:, at : at + size])
            total = term if total is None else total + term
            at += size
        return total

    grad = part(1) + part(2)

    for i, ref in enumerate(outs[:-1]):

        @pl.when(step == i)
        def _(ref=ref):
            ref[...] = grad.astype(BF16)

    @pl.when(step == last)
    def _():
        outs[-1][...] = grad + part(0)


def normed_grad(parts, weights):
    sizes = [p[0].shape[1] for p in parts]
    tok, span = parts[0][0].shape[0], parts[0][1].shape[0]
    blocks = span // tok
    fixed = lambda s: (0, 0)
    moving = lambda s: (s, 0)
    specs = []
    for size in sizes:
        specs += [pl.BlockSpec((tok, size), fixed)] + [pl.BlockSpec((tok, size), moving)] * 2
    return pl.pallas_call(
        functools.partial(normed_grad_kernel, sizes),
        grid=(blocks,),
        in_specs=specs + [pl.BlockSpec(weights.shape, fixed)],
        out_specs=[pl.BlockSpec((tok, D), fixed)] * blocks,
        out_shape=[jax.ShapeDtypeStruct((tok, D), BF16)] * (blocks - 1)
        + [jax.ShapeDtypeStruct((tok, D), F32)],
        compiler_params=vmem(24),
        cost_estimate=cost(4 * span * D * D, 16 << 20, weight=LATE),
        name="normed_grad",
    )(*in_vmem(*[g for p in parts for g in p]), weights)


def turn_kernel(x_ref, out_ref):
    out_ref[...] = x_ref[...].T


def turn(x):
    return pl.pallas_call(
        turn_kernel,
        in_specs=whole_specs(range(1)),
        out_specs=pl.BlockSpec(memory_space=pltpu.VMEM),
        out_shape=jax.ShapeDtypeStruct(x.shape[::-1], x.dtype),
        compiler_params=vmem(24),
        cost_estimate=cost(0, 8 << 20),
        name="turn",
    )(x)


def project_grad_kernel(count, core_ref, normed_ref, dq_ref, dk_ref, dv_ref, out_ref):
    own = normed_ref.shape[1] - dq_ref.shape[0]
    turned = rows_of_core(normed_ref, core_ref[0], count)
    for kind, ref in enumerate((dq_ref, dk_ref, dv_ref)):
        left = turned[:, own:] if kind == 0 else turned
        store_pieces(out_ref, dot(left, ref[...]).astype(BF16), kind * D)


def project_grad(core, normed_turned, grads, parts, count):
    span = normed_turned.shape[1]
    out = piece_shapes(3 * D, parts)[0]
    return pl.pallas_call(
        functools.partial(project_grad_kernel, count),
        in_specs=[pl.BlockSpec(memory_space=pltpu.SMEM)] + whole_specs(range(4)),
        out_specs=pl.BlockSpec(memory_space=pltpu.VMEM),
        out_shape=out,
        compiler_params=vmem(24),
        cost_estimate=cost(2 * span * D * D, 8 << 20, weight=LATE),
        name="project_grad",
    )(core, normed_turned, *in_vmem(*grads))


def after(x, *others):
    return lax.optimization_barrier((x, others))[0]


class Sequence:
    def __init__(self):
        self.last = ()

    def take(self, *values):
        return lax.optimization_barrier((values, self.last))[0]

    def done(self, *values):
        self.last = values


def folded(count):
    return [0] + list(range(1, count, 2)) + list(range(2, count, 2))[::-1]


def siblings(count):
    return [(i, i ^ 1) for i in range(count)]


def ring_gather(x, count, gates, last):
    chips = count // 2
    order = folded(chips)
    follow = {order[i]: order[(i + 1) % chips] for i in range(chips)}
    pairs = [(2 * z + c, 2 * follow[z] + c) for z in range(chips) for c in range(2)]
    me = lax.axis_index("fsdp")
    chip, core = me // 2, me % 2
    at = jnp.array([order.index(z) for z in range(chips)], jnp.int32)[chip]
    ring = jnp.array(order, jnp.int32)
    chunks, places = [], []
    current = x
    for k in range(chips):
        source = ring[(at - k) % chips]
        chunks += [current, lax.ppermute(current, "fsdp", siblings(count))]
        places += [2 * source + core, 2 * source + 1 - core]
        if k + 1 < chips:
            if 0 < k <= len(gates) and gates[k - 1]:
                current = after(current, *gates[k - 1])
            current = lax.ppermute(current, "fsdp", pairs)
            if k + 2 == chips:
                current = after(current, *last)
    return chunks, jnp.stack(places).astype(jnp.int32)


def earlier_rows(x, count, others):
    up = [(i, i + 2) for i in range(count - 2)]
    second = lax.ppermute(x, "fsdp", up)
    core = lax.axis_index("fsdp") % 2
    first = after(jnp.where(core == 0, x, second), *others)
    first = lax.ppermute(first, "fsdp", siblings(count))
    return second, first


def return_send(second, across, count):
    core = lax.axis_index("fsdp") % 2
    across = across.astype(F32)
    total = jnp.where(core == 0, second.astype(F32), second.astype(F32) + across).astype(BF16)
    down = [(i + 2, i) for i in range(count - 2)]
    return lax.ppermute(total, "fsdp", down), jnp.where(core == 0, across, 0.0).astype(BF16), total


def quarter_gather(x, experts, count):
    chips = count // 2
    rows, width = x.shape
    each = width // experts
    me, group = lax.axis_index("fsdp"), lax.axis_index("expert")
    chip, core = me // 2, me % 2
    mine = lax.dynamic_slice_in_dim(x, group * each, each, 1)
    fetched = [mine]
    for k in range(1, chips):
        pairs = [(2 * z + c, 2 * ((z + k) % chips) + c) for z in range(chips) for c in range(2)]
        fetched.append(lax.ppermute(mine, "fsdp", pairs))
    stacked = jnp.stack(fetched)
    terms = plane_all(stacked, experts)
    chunks, columns = [], []
    for k in range(experts):
        here = after(terms[0], terms[-1]) if k == 0 else terms[k]
        chunks += [terms[k], sibling(here, count)]
        columns.append(group ^ k)
    blocks = []
    for k in range(chips):
        source = (chip - k) % chips
        blocks += [2 * source + core, 2 * source + 1 - core]
    places = [jnp.stack(p).astype(jnp.int32) for p in (blocks, columns)]
    return chunks, places, stacked


def sibling(x, count):
    return lax.ppermute(x, "fsdp", siblings(count))


def summed(terms):
    total = terms[0].astype(F32)
    for term in terms[1:]:
        total += term.astype(F32)
    return total.astype(BF16)


def in_plane(x):
    return lax.all_to_all(x, "expert", split_axis=0, concat_axis=0, tiled=True)


def plane_send(mine, other, experts):
    group = lax.axis_index("expert")

    def part(k):
        pair = [lax.dynamic_index_in_dim(x, group ^ k, 0, False) for x in (mine, other)]
        return summed(pair)

    parts = [part(k) for k in range(experts)]
    moved = [
        lax.ppermute(parts[k], "expert", [(i, i ^ k) for i in range(experts)])
        for k in range(1, experts)
    ]
    return parts[:1] + moved, parts


def line_send(pair, count):
    chips = count // 2
    chip = lax.axis_index("fsdp") // 2
    pair = [x.reshape(chips, x.shape[-2] // chips, x.shape[-1]) for x in pair]

    def part(k):
        at = (chip + k) % chips
        return summed([lax.dynamic_index_in_dim(x, at, 0, False) for x in pair])

    parts = [part(k) for k in range(chips)]
    moved = []
    for k in range(1, chips):
        pairs = [(2 * z + c, 2 * ((z + k) % chips) + c) for z in range(chips) for c in range(2)]
        moved.append(lax.ppermute(parts[k], "fsdp", pairs))
    return parts[:1] + moved, parts


def plane_all(x, experts):
    terms = [x]
    for k in range(1, experts):
        terms.append(lax.ppermute(x, "expert", [(i, i ^ k) for i in range(experts)]))
    return terms


def plane_columns(terms):
    experts = len(terms)
    terms = jnp.stack(terms)
    group = lax.axis_index("expert")
    parts = [lax.dynamic_index_in_dim(terms, j ^ group, 0, False) for j in range(experts)]
    return jnp.concatenate(parts, axis=1).astype(F32)


def plane_sum(terms):
    terms = [t.astype(F32) for t in terms]
    while len(terms) > 1:
        terms = [terms[i] + terms[i + 1] for i in range(0, len(terms), 2)]
    return terms[0]


def local(
    tokens,
    past_logits,
    routes,
    lengths,
    projector,
    collector,
    router,
    blender,
    constants,
    first_gain,
    second_gain,
    carryover,
    gating,
    upward,
    downward,
    cotangent,
):
    tok = tokens.shape[0]
    experts = lax.axis_size("expert")
    count = lax.axis_size("fsdp")
    names = experts + 4
    hops = WINDOW // tok
    me = lax.axis_index("fsdp")

    shard = projector.shape[0]
    gap = LANES - names - 8
    small = jnp.concatenate(
        [router, blender, constants, jnp.zeros((shard, gap), BF16)]
        + [first_gain[:, None], second_gain[:, None]],
        axis=1,
    )
    width = 3 * D + LANES
    filler = jnp.zeros((shard, -width % (experts * LANES)), BF16)
    shared = jnp.concatenate([projector, small, filler], axis=1)
    chunks, (blocks_at, columns_at), stacked = quarter_gather(shared, experts, count)
    own = jnp.concatenate([gating[0], upward[0], downward[0]], axis=1)
    second, first = earlier_rows(tokens, count, chunks[0::2])
    collector_all = lax.all_gather(collector, "fsdp", axis=0, tiled=True)

    span = tok + WINDOW
    key_positions = (me - hops) * tok + jnp.arange(span, dtype=jnp.int32)
    cosine, sine = rope_tables(key_positions.astype(F32))
    bounds = jnp.cumsum(lengths[0])
    biases = []
    for t in range(tok // QTILE):
        at = me * tok + t * QTILE + jnp.arange(QTILE, dtype=jnp.int32)
        start = jnp.max(jnp.where(bounds[:, None] <= at[None, :], bounds[:, None], 0), axis=0)
        least = jnp.maximum(at - (WINDOW - 1), start)
        keys_at = key_positions[t * QTILE : t * QTILE + SPAN, None]
        inside = (keys_at >= least[None, :]) & (keys_at <= at[None, :])
        biases.append(jnp.where(inside, 0.0, masked_score).astype(F32))
    bias = jnp.stack(biases)
    onehot = (routes[:, :, None] == jnp.arange(experts, dtype=jnp.int32)).astype(BF16)
    per_token = jnp.sum(onehot, axis=1)
    lower = jnp.tril(jnp.ones((tok, tok), BF16), -1)
    before = jnp.dot(lower, per_token, preferred_element_type=F32)
    position_in = jnp.sum(onehot.astype(F32) * before[:, None, :], axis=2).astype(jnp.int32)
    slots = jnp.where(routes < experts, routes * CAP + position_in, experts * CAP)
    past_part = jnp.dot(
        past_logits, carryover, precision=lax.Precision.HIGHEST, preferred_element_type=F32
    )
    past_part = jnp.pad(past_part, ((0, 0), (0, LANES - names)))
    past_wide = jnp.pad(past_logits, ((0, 0), (0, LANES - names)))
    carry_wide = jnp.pad(carryover, ((0, LANES - names), (0, LANES - names)))

    weights, small_all, normed_all, q, k, v = project(
        blocks_at, columns_at, chunks, [second, first, tokens], cosine, sine
    )
    half = 4
    att_a, lse_a = attend(q, k, v, bias, 0, half)
    att_b, lse_b = attend(q, k, v, bias, half, PAIRS - half)
    lse = jnp.concatenate([lse_a, lse_b], axis=0)
    attended, residual, hidden, aux, send = route(
        experts, att_a, att_b, collector_all, tokens, cotangent, small_all, past_part, routes, slots.T
    )

    def exchange(x):
        x = x.reshape(experts, CAP, 2 * D)
        x = lax.all_to_all(x, "expert", split_axis=0, concat_axis=0, tiled=True)
        return x.reshape(experts * CAP, 2 * D)

    normed_turned, attended_turned = turn(after(normed_all, send)), turn(after(attended, send))
    probability = weigh(after(q, send), k, lse, bias)
    waiting = [probability, normed_turned, attended_turned]
    weight_chunks, weight_places = ring_gather(own, count, [[q], [send]], waiting)
    arrived = after(exchange(send), *waiting)
    answers, low = expert_rows(arrived, weight_places, weight_chunks)
    returned = exchange(answers)
    sums = expert_sums(arrived, low)
    sums = lax.psum_scatter(sums, "fsdp", scatter_dimension=0, tiled=True)

    layer_output, residual_grad, attended_grad, logits_grad, *col_grad = combine(
        experts, count, returned, residual, hidden, cotangent, aux, small_all, collector_all,
        attended_turned, past_wide, carry_wide, routes, slots,
    )
    def back(upstream):
        return attend_back(q, k, v, attended, upstream, probability, cosine, sine)

    col_mine, col_theirs = col_grad
    core = core_number()
    seq = Sequence()
    col_other = sibling(col_theirs, count)
    grads = back(attended_grad)
    seq.done(grads)
    (col_other,) = seq.take(col_other)
    col_terms, parts = plane_send(col_mine, col_other, experts)
    seq.done(parts)
    (turned,) = seq.take(normed_turned)
    theirs = project_grad(1 - core, turned, grads, experts, count)
    other = sibling(theirs, count)
    seq.done(theirs)
    (again,) = seq.take(weights)
    *halo_grads, own_grad = normed_grad([grads], again)
    across = sibling(halo_grads[1], count)
    seq.done(own_grad)
    (turned,) = seq.take(normed_turned)
    mine = project_grad(core, turned, grads, experts, count)
    seq.done(mine)
    (other,) = seq.take(other)
    terms, parts = plane_send(mine, other, experts)
    seq.done(parts)
    (across,) = seq.take(across)
    after_rows, across, total = return_send(halo_grads[0], across, count)
    seq.done(total)
    (col_terms,) = seq.take(col_terms)
    col_part = summed(col_terms)
    seq.done(col_part)
    (terms,) = seq.take(terms)
    merged = jnp.concatenate([summed(terms), col_part], axis=1)
    cut = mine.shape[2]
    terms, parts = line_send([merged], count)
    seq.done(parts)
    (sums,) = seq.take(sums)
    sums = sums.astype(F32)
    seq.done(sums)
    (terms,) = seq.take(terms)
    merged = summed(terms)
    terms = plane_all(merged, experts)
    seq.done(merged)
    (after_rows,) = seq.take(after_rows)
    own_grad = own_grad + across.astype(F32) + after_rows.astype(F32)
    tokens_wide = tokens.astype(F32)
    first_scale = norm_scale(tokens_wide)
    scaled = own_grad * small_all[:, LANES - 2].astype(F32)
    gradient_tokens = (
        residual_grad
        + first_scale * scaled
        - tokens_wide
        * (first_scale * first_scale * first_scale)
        * jnp.mean(scaled * tokens_wide, axis=-1, keepdims=True)
    ).astype(BF16)
    seq.done(gradient_tokens)
    (terms,) = seq.take(terms)
    projector_rows = plane_columns([t[:, :cut] for t in terms])[:, : 3 * D]
    col_rows = plane_columns([t[:, cut:] for t in terms])
    first_rows = jnp.sum(projector.astype(F32) * projector_rows, axis=1) / first_gain.astype(F32)

    return (
        layer_output,
        gradient_tokens,
        logits_grad[:, :names],
        projector_rows,
        col_rows[:, :D],
        col_rows[:, D : D + names],
        col_rows[:, D + names : D + names + 4],
        col_rows[:, D + names + 4 : D + names + 6],
        first_rows,
        col_rows[:, D + LANES - 1],
        col_rows[:names, D + names + 6 : D + 2 * names + 6],
        sums[:, :FF][None],
        sums[:, FF : 2 * FF][None],
        sums[:, 2 * FF :][None],
    )


def solution(mesh):
    rows = P(("expert", "fsdp"), None)
    shared = P("fsdp", None)
    expert = P("expert", "fsdp", None)
    return jax.shard_map(
        local,
        mesh=mesh,
        in_specs=(
            rows, rows, rows, P("expert", None), shared, shared, shared, shared, shared,
            P("fsdp"), P("fsdp"), P(), expert, expert, expert, rows,
        ),
        out_specs=(
            rows, rows, rows, shared, shared, shared, shared, shared,
            P("fsdp"), P("fsdp"), P(), expert, expert, expert,
        ),
        check_vma=False,
    )
```

```python
import functools
import math

import jax
import jax.numpy as jnp
from jax import lax
from jax.experimental import pallas as pl
from jax.experimental.pallas import tpu as pltpu
from jax.sharding import PartitionSpec as P

D = 768
H = 12
HD = 64
FF = 2048
WINDOW = 1024
CAP = 128

epsilon = 1e-06
rope_base = 10000.0
masked_score = -1e30
QTILE = 256
SPAN = QTILE + WINDOW
LANES = 128
PAIRS = H * HD // LANES
FTILE = 512
STILE = 2048
LATE = 6
NT = (((1,), (1,)), ((), ()))
TN = (((0,), (0,)), ((), ()))
F32 = jnp.float32
BF16 = jnp.bfloat16
query_scale = 1.0 / math.sqrt(HD)


def vmem(megabytes):
    return pltpu.CompilerParams(vmem_limit_bytes=megabytes << 20)


def in_hbm(*arrays):
    return [pltpu.with_memory_space_constraint(a, pltpu.HBM) for a in arrays]


def in_vmem(*arrays):
    return [pltpu.with_memory_space_constraint(a, pltpu.VMEM) for a in arrays]


def cost(flops, moved, trans=0, weight=1):
    return pl.CostEstimate(
        flops=int(weight * flops), bytes_accessed=int(weight * moved), transcendentals=int(trans)
    )


def dot(a, b):
    return jnp.dot(a, b, preferred_element_type=F32)


def dot_nt(a, b):
    return lax.dot_general(a, b, NT, preferred_element_type=F32)


def dot_tn(a, b):
    return lax.dot_general(a, b, TN, preferred_element_type=F32)


def halves(x):
    high = x.astype(BF16)
    return high, (x - high.astype(F32)).astype(BF16)


def lanes_of(shape):
    return lax.broadcasted_iota(jnp.int32, shape, len(shape) - 1)


def norm_scale(values):
    return lax.rsqrt(jnp.mean(values * values, axis=-1, keepdims=True) + epsilon)


def piece_shapes(width, parts):
    each = -(-width // (parts * LANES)) * LANES
    return [jax.ShapeDtypeStruct((parts, D // 2, each), BF16)] * 2


def rows_of_core(ref, core, count):
    rows = D // count
    at = [pl.multiple_of((2 * z + core) * rows, rows) for z in range(count // 2)]
    return jnp.concatenate([ref[pl.ds(a, rows), :] for a in at], axis=0)


def store_pieces(out_ref, value, at):
    each = out_ref.shape[2]
    for left in range(0, value.shape[1], LANES):
        part, inner = divmod(at + left, each)
        out_ref[part, :, inner : inner + LANES] = value[:, left : left + LANES]


def core_number():
    return (lax.axis_index("fsdp") % 2).astype(jnp.int32).reshape(1)


def rope_tables(positions):
    lane = jnp.arange(LANES, dtype=jnp.int32)
    half = HD // 2
    freq_index = (lane % half).astype(F32)
    inverse = jnp.exp(freq_index * (-2.0 * math.log(rope_base) / HD))
    angles = positions[:, None] * inverse[None, :]
    sign = jnp.where(lane % HD < half, -1.0, 1.0).astype(F32)
    return jnp.cos(angles), jnp.sin(angles) * sign[None, :]


def swapped(x):
    half = HD // 2
    lane = lanes_of(x.shape)
    return jnp.where(
        lane % HD < half, pltpu.roll(x, LANES - half, 1), pltpu.roll(x, half, 1)
    )


def rotate(x, cosine, sine):
    return x * cosine + swapped(x) * sine


def rotate_back(x, cosine, sine):
    return x * cosine - swapped(x) * sine


def project_kernel(blocks_at, columns_at, *refs):
    chips, parts = blocks_at.shape[0] // 2, columns_at.shape[0]
    chunks = refs[: 2 * parts]
    tok_ref, cos_ref, sin_ref, w_ref, normed_ref, q_ref, k_ref, v_ref = refs[2 * parts :]
    rows, width = chunks[0].shape[1:]
    step = pl.program_id(0)

    @pl.when(step == 0)
    def _():
        for e in range(parts):
            left = pl.multiple_of(columns_at[e] * width, LANES)
            for z in range(chips):
                for c in range(2):
                    above = pl.multiple_of(blocks_at[2 * z + c] * rows, rows)
                    w_ref[pl.ds(above, rows), pl.ds(left, width)] = chunks[2 * e + c][z]

    small = w_ref[:, 3 * D : 3 * D + LANES].astype(F32).T
    gain = small[LANES - 2 : LANES - 1, :]
    x = tok_ref[...].astype(F32)
    normed = (x * norm_scale(x) * gain).astype(BF16)
    normed_ref[...] = normed
    cosine, sine = cos_ref[...], sin_ref[...]
    keys = dot(normed, w_ref[:, D : 2 * D])
    for j in range(PAIRS):
        part = slice(j * LANES, (j + 1) * LANES)
        k_ref[:, part] = rotate(keys[:, part], cosine, sine).astype(BF16)
    v_ref[...] = dot(normed, w_ref[:, 2 * D : 3 * D]).astype(BF16)

    @pl.when(step == pl.num_programs(0) - 1)
    def _():
        queries = dot(normed, w_ref[:, :D])
        for j in range(PAIRS):
            part = slice(j * LANES, (j + 1) * LANES)
            q_ref[:, part] = (rotate(queries[:, part], cosine, sine) * query_scale).astype(BF16)


def project(blocks_at, columns_at, chunks, tokens_all, cosine, sine, tok):
    chips, rows, width = chunks[0].shape
    parts = columns_at.shape[0]
    blocks = tokens_all.shape[0] // tok
    fixed = lambda s, *_: (0, 0)
    moving = lambda s, *_: (s, 0)
    span = tokens_all.shape[0]
    return pl.pallas_call(
        project_kernel,
        grid_spec=pltpu.PrefetchScalarGridSpec(
            num_scalar_prefetch=2,
            grid=(blocks,),
            in_specs=[pl.BlockSpec((chips, rows, width), lambda s, *_: (0, 0, 0))] * len(chunks)
            + [
                pl.BlockSpec((tok, D), moving),
                pl.BlockSpec((tok, LANES), moving),
                pl.BlockSpec((tok, LANES), moving),
            ],
            out_specs=[
                pl.BlockSpec((D, parts * width), fixed),
                pl.BlockSpec((tok, D), moving),
                pl.BlockSpec((tok, D), fixed),
                pl.BlockSpec((tok, D), moving),
                pl.BlockSpec((tok, D), moving),
            ],
        ),
        out_shape=[
            jax.ShapeDtypeStruct((D, parts * width), BF16),
            jax.ShapeDtypeStruct((span, D), BF16),
            jax.ShapeDtypeStruct((tok, D), BF16),
            jax.ShapeDtypeStruct((span, D), BF16),
            jax.ShapeDtypeStruct((span, D), BF16),
        ],
        compiler_params=vmem(24),
        cost_estimate=cost(2 * span * D * 2 * D, 20 << 20),
        name="project",
    )(blocks_at, columns_at, *chunks, tokens_all, cosine, sine)


def head_mask(x, head):
    return jnp.where(lanes_of(x.shape) // HD == head, x, jnp.zeros_like(x))


def both_heads(x):
    return jnp.concatenate([head_mask(x, 0), head_mask(x, 1)], axis=0)


def own_head(x):
    return jnp.concatenate([x[:HD, :QTILE], x[HD:, QTILE:]], axis=0).T


def attend_kernel(q_ref, k_ref, v_ref, bias_ref, o_ref, lse_ref, vt_ref):
    vt_ref[...] = v_ref[...].T
    for t in range(q_ref.shape[0] // QTILE):
        rows = slice(t * QTILE, (t + 1) * QTILE)
        span = slice(t * QTILE, t * QTILE + SPAN)
        s = dot_nt(k_ref[span, :], both_heads(q_ref[rows, :]))
        s += jnp.concatenate([bias_ref[t]] * 2, axis=1)
        top = jnp.max(s, axis=0, keepdims=True)
        e = jnp.exp(s - top)
        total = jnp.sum(e, axis=0, keepdims=True)
        o_ref[rows, :] = own_head(dot(vt_ref[:, span], e.astype(BF16)) / total).astype(BF16)
        lse = top + jnp.log(total)
        for h in range(2):
            lse_ref[0, h : h + 1, rows] = lse[:, h * QTILE : (h + 1) * QTILE]


def attend(q, k, v, bias, first, pairs):
    tok, span = q.shape[0], k.shape[0]
    col = lambda p: (0, first + p)
    return pl.pallas_call(
        attend_kernel,
        grid=(pairs,),
        in_specs=[
            pl.BlockSpec((tok, LANES), col),
            pl.BlockSpec((span, LANES), col),
            pl.BlockSpec((span, LANES), col),
            pl.BlockSpec(bias.shape, lambda p: (0, 0, 0)),
        ],
        out_specs=[
            pl.BlockSpec((tok, LANES), lambda p: (0, p)),
            pl.BlockSpec((1, 8, tok), lambda p: (p, 0, 0)),
        ],
        out_shape=[
            jax.ShapeDtypeStruct((tok, pairs * LANES), BF16),
            jax.ShapeDtypeStruct((pairs, 8, tok), F32),
        ],
        scratch_shapes=[pltpu.VMEM((LANES, span), BF16)],
        compiler_params=vmem(24),
        cost_estimate=cost(16 * tok * SPAN * pairs * LANES, pairs << 20, tok * SPAN * 2 * pairs),
        name="attend",
    )(q, k, v, bias)


def weigh_kernel(q_ref, k_ref, lse_ref, bias_ref, p_ref):
    for t in range(q_ref.shape[0] // QTILE):
        rows = slice(t * QTILE, (t + 1) * QTILE)
        lse = jnp.concatenate([lse_ref[0, h : h + 1, rows] for h in range(2)], axis=1)
        s = dot_nt(k_ref[t * QTILE : t * QTILE + SPAN, :], both_heads(q_ref[rows, :]))
        s += jnp.concatenate([bias_ref[t]] * 2, axis=1)
        p_ref[0, t] = jnp.exp(s - lse).astype(BF16)


def weigh(q, k, lse, bias):
    tok, span = q.shape[0], k.shape[0]
    col = lambda p: (0, p)
    shape = (PAIRS, tok // QTILE, SPAN, 2 * QTILE)
    return pl.pallas_call(
        weigh_kernel,
        grid=(PAIRS,),
        in_specs=[
            pl.BlockSpec((tok, LANES), col),
            pl.BlockSpec((span, LANES), col),
            pl.BlockSpec((1, 8, tok), lambda p: (p, 0, 0)),
            pl.BlockSpec(bias.shape, lambda p: (0, 0, 0)),
        ],
        out_specs=pl.BlockSpec((1, *shape[1:]), lambda p: (p, 0, 0, 0)),
        out_shape=pltpu.HBM(shape, BF16),
        compiler_params=vmem(32),
        cost_estimate=cost(8 * tok * SPAN * D, 20 << 20),
        name="weigh",
    )(*in_hbm(q, k), lse, bias)


def attend_back_kernel(
    q_ref, k_ref, v_ref, o_ref, do_ref, p_ref, cos_ref, sin_ref,
    dq_ref, dk_ref, dv_ref, kt_ref, dk_sum, dv_sum,
):
    tok = q_ref.shape[0]
    own = k_ref.shape[0] - tok
    kt_ref[...] = k_ref[...].T
    dk_sum[...] = jnp.zeros_like(dk_sum)
    dv_sum[...] = jnp.zeros_like(dv_sum)
    for t in range(tok // QTILE):
        rows = slice(t * QTILE, (t + 1) * QTILE)
        span = slice(t * QTILE, t * QTILE + SPAN)
        values = v_ref[span, :]
        queries, upstream = q_ref[rows, :], do_ref[rows, :]
        product = (upstream.astype(F32) * o_ref[rows, :].astype(F32)).T
        qh, gh = both_heads(queries), both_heads(upstream)
        delta = jnp.concatenate(
            [jnp.sum(product[h * HD : (h + 1) * HD], axis=0, keepdims=True) for h in range(2)],
            axis=1,
        )
        p = p_ref[0, t]
        ds = (p.astype(F32) * (dot_nt(values, gh) - delta)).astype(BF16)
        dv_sum[span, :] += dot(p, gh)
        dk_sum[span, :] += dot(ds, qh)
        dq = own_head(dot(kt_ref[:, span], ds))
        there = slice(own + t * QTILE, own + (t + 1) * QTILE)
        dq = rotate_back(dq, cos_ref[there, :], sin_ref[there, :]) * query_scale
        dq_ref[rows, :] = dq.astype(BF16)
    dk_ref[...] = rotate_back(dk_sum[...], cos_ref[...], sin_ref[...]).astype(BF16)
    dv_ref[...] = dv_sum[...].astype(BF16)


def attend_back(q, k, v, o, do, p, cosine, sine):
    tok, span = q.shape[0], k.shape[0]
    pairs = PAIRS
    col = out = lambda p: (0, p)
    whole = lambda p: (0, 0)
    mine = pl.BlockSpec((tok, LANES), col)
    long = pl.BlockSpec((span, LANES), col)
    return pl.pallas_call(
        attend_back_kernel,
        grid=(pairs,),
        in_specs=[
            mine,
            long,
            long,
            pl.BlockSpec((tok, LANES), col),
            mine,
            pl.BlockSpec((1, *p.shape[1:]), lambda p: (p, 0, 0, 0)),
            pl.BlockSpec((span, LANES), whole),
            pl.BlockSpec((span, LANES), whole),
        ],
        out_specs=[
            pl.BlockSpec((tok, LANES), out),
            pl.BlockSpec((span, LANES), out),
            pl.BlockSpec((span, LANES), out),
        ],
        out_shape=[
            pltpu.VMEM((tok, pairs * LANES), BF16),
            pltpu.VMEM((span, pairs * LANES), BF16),
            pltpu.VMEM((span, pairs * LANES), BF16),
        ],
        scratch_shapes=[
            pltpu.VMEM((LANES, span), BF16),
            pltpu.VMEM((span, LANES), F32),
            pltpu.VMEM((span, LANES), F32),
        ],
        compiler_params=vmem(32),
        cost_estimate=cost(40 * tok * SPAN * pairs * LANES, pairs << 21, tok * SPAN * 2 * pairs, weight=LATE),
        name="attend_back",
    )(*in_hbm(q, k, v, o, do, p, cosine, sine))


def route_kernel(
    experts, att_a, att_b, col_ref, tok_ref, cot_ref, small_ref, past_ref, routes_ref, slots_ref,
    att_ref, residual_ref, hidden_ref, aux_ref, send_ref,
):
    small = small_ref[...]
    gain = small.astype(F32).T[LANES - 1 : LANES, :]
    att_ref[...] = jnp.concatenate([att_a[...], att_b[...]], axis=1)
    residual = tok_ref[...].astype(F32) + dot(att_ref[...], col_ref[...])
    scale = norm_scale(residual)
    hidden = (residual * scale * gain).astype(BF16)
    residual_ref[...] = residual
    hidden_ref[...] = hidden
    mixed = dot(hidden, small)
    logits = mixed + past_ref[...]
    lane = lanes_of(logits.shape)
    routes = routes_ref[...]
    picked = [
        jnp.sum(jnp.where(lane == routes[:, k : k + 1], logits, 0.0), axis=1, keepdims=True)
        for k in range(2)
    ]
    top = jnp.maximum(picked[0], picked[1])
    raised = [jnp.exp(x - top) for x in picked]
    total = raised[0] + raised[1]
    gates = [x / total for x in raised]
    names = experts + 4
    aux = [gates[0], gates[1]]
    for c in range(2):
        pair = [mixed[:, names + 2 * c + i : names + 2 * c + i + 1] for i in range(2)]
        above = jnp.maximum(pair[0], pair[1])
        up = [jnp.exp(x - above) for x in pair]
        aux += [up[0] / (up[0] + up[1]), up[1] / (up[0] + up[1])]
    aux.append(scale)
    packed = jnp.zeros(logits.shape, F32)
    for i, value in enumerate(aux):
        packed = jnp.where(lane == i, value, packed)
    aux_ref[...] = packed
    cot = cot_ref[...].astype(F32)
    slots = slots_ref[...]
    count, tok = send_ref.shape[0], hidden.shape[0]
    where = lax.broadcasted_iota(jnp.int32, (count, tok), 0)
    hot = [(where == slots[k : k + 1, :]).astype(F32).astype(BF16) for k in range(2)]
    send_ref[:, :D] = dot(hot[0] + hot[1], hidden).astype(BF16)
    grads = dot(hot[0], (gates[0] * cot).astype(BF16)) + dot(hot[1], (gates[1] * cot).astype(BF16))
    send_ref[:, D:] = grads.astype(BF16)


def whole_specs(arrays):
    return [pl.BlockSpec(memory_space=pltpu.VMEM) for _ in arrays]


def route(experts, *args):
    tok = args[0].shape[0]
    outs = [
        jax.ShapeDtypeStruct((tok, D), BF16),
        jax.ShapeDtypeStruct((tok, D), F32),
        jax.ShapeDtypeStruct((tok, D), BF16),
        jax.ShapeDtypeStruct((tok, LANES), F32),
        jax.ShapeDtypeStruct((experts * CAP, 2 * D), BF16),
    ]
    return pl.pallas_call(
        functools.partial(route_kernel, experts),
        in_specs=whole_specs(args),
        out_specs=whole_specs(outs),
        out_shape=outs,
        compiler_params=vmem(56),
        cost_estimate=cost(2 * tok * D * (D + 3 * experts * CAP), 9 << 20),
        name="route",
    )(*args)


def expert_kernel(place, x_ref, *refs):
    count = place.shape[0]
    chunks = refs[: 3 * count]
    out_ref, low_ref, answer, back, gw_ref, uw_ref, dw_ref = refs[3 * count :]
    step = pl.program_id(0)
    height = chunks[0].shape[0]

    @pl.when(step == 0)
    def _():
        answer[...] = jnp.zeros_like(answer)
        back[...] = jnp.zeros_like(back)

    for i in range(count):
        at = pl.ds(pl.multiple_of(place[i] * height, height), height)
        for j, w_ref in enumerate((gw_ref, uw_ref, dw_ref)):
            w_ref[at, :] = chunks[3 * i + j][...]
    rows, grads = x_ref[:, :D], x_ref[:, D:]
    gw, uw, dw = gw_ref[...], uw_ref[...], dw_ref[...]
    pre = dot(rows, gw)
    up = dot(rows, uw)
    grad = dot(grads, dw)
    sigmoid = 1.0 / (1.0 + jnp.exp(-pre))
    active = pre * sigmoid
    hidden = (active * up).astype(BF16)
    gate_low = (grad * up * sigmoid * (1.0 + pre * (1.0 - sigmoid))).astype(BF16)
    up_low = (grad * active).astype(BF16)
    low_ref[0] = gate_low
    low_ref[1] = up_low
    low_ref[2] = hidden
    answer[...] += dot_nt(hidden, dw)
    back[...] += dot_nt(gate_low, gw) + dot_nt(up_low, uw)

    @pl.when(step == pl.num_programs(0) - 1)
    def _():
        out_ref[:, :D] = answer[...].astype(BF16)
        out_ref[:, D:] = back[...].astype(BF16)


def expert_rows(x, place, chunks):
    rows, height = x.shape[0], chunks[0].shape[0]
    tiles = FF // FTILE
    weights, operands = [], []
    for chunk in chunks:
        for j in range(3):
            weights.append(pl.BlockSpec((height, FTILE), lambda s, *_, j=j: (0, j * tiles + s)))
            operands.append(chunk)
    return pl.pallas_call(
        expert_kernel,
        grid_spec=pltpu.PrefetchScalarGridSpec(
            num_scalar_prefetch=1,
            grid=(tiles,),
            in_specs=[pl.BlockSpec((rows, 2 * D), lambda s, *_: (0, 0))] + weights,
            out_specs=[
                pl.BlockSpec((rows, 2 * D), lambda s, *_: (0, 0)),
                pl.BlockSpec((3, rows, FTILE), lambda s, *_: (0, 0, s)),
            ],
            scratch_shapes=[pltpu.VMEM((rows, D), F32)] * 2 + [pltpu.VMEM((D, FTILE), BF16)] * 3,
        ),
        out_shape=[
            jax.ShapeDtypeStruct((rows, 2 * D), BF16),
            pltpu.HBM((3, rows, FF), BF16),
        ],
        compiler_params=vmem(32),
        cost_estimate=cost(12 * rows * D * FF, 20 << 20),
        name="expert_rows",
    )(place, x, *operands)


def expert_sums_kernel(x_ref, low_ref, out_ref, turned):
    step = pl.program_id(0)
    tiles = FF // STILE

    @pl.when(step == 0)
    def _():
        turned[...] = x_ref[:, :D].T

    @pl.when(step == 2 * tiles)
    def _():
        turned[...] = x_ref[:, D:].T

    out_ref[...] = dot(turned[...], low_ref[0]).astype(BF16)


def expert_sums(x, low):
    rows = x.shape[0]
    tiles = FF // STILE
    return pl.pallas_call(
        expert_sums_kernel,
        grid=(3 * tiles,),
        in_specs=[
            pl.BlockSpec((rows, 2 * D), lambda j: (0, 0)),
            pl.BlockSpec((1, rows, STILE), lambda j: (j // tiles, 0, j % tiles)),
        ],
        out_specs=pl.BlockSpec((D, STILE), lambda j: (0, j)),
        out_shape=pltpu.HBM((D, 3 * FF), BF16),
        scratch_shapes=[pltpu.VMEM((D, rows), BF16)],
        compiler_params=vmem(24),
        cost_estimate=cost(6 * rows * D * FF, 20 << 20),
        name="expert_sums",
    )(x, *in_hbm(low))


def combine_kernel(
    experts, fsdp, core_ref, back_ref, residual_ref, hidden_ref, cot_ref, aux_ref, small_ref, col_ref, att_ref,
    past_ref, carry_ref, routes_ref, slots_ref,
    layer_ref, rgrad_ref, agrad_ref, logits_ref, mine_ref, theirs_ref, small_sum,
):
    tok = hidden_ref.shape[0]
    names = experts + 4
    slots, routes = slots_ref[...], routes_ref[...]
    count = back_ref.shape[0]
    where = lax.broadcasted_iota(jnp.int32, (tok, count), 1)
    hot = [(where == slots[:, k : k + 1]).astype(F32).astype(BF16) for k in range(2)]
    answers, returned = back_ref[:, :D], back_ref[:, D:]
    values = [dot(hot[k], answers) for k in range(2)]
    hidden_grad = dot(hot[0] + hot[1], returned)
    hidden_low, cot_low = hidden_ref[...], cot_ref[...]
    hidden, cot = hidden_low.astype(F32), cot_low.astype(F32)
    residual = residual_ref[...]
    small = small_ref[...]
    turned = small.astype(F32).T
    aux = aux_ref[...]
    gates = [aux[:, k : k + 1] for k in range(2)]
    mixing = [[aux[:, 2 + 2 * c + i : 3 + 2 * c + i] for i in range(2)] for c in range(2)]
    scale = aux[:, 6:7]
    both = jnp.sum(hidden * cot, axis=1, keepdims=True)
    against = dot(cot_low, small)
    fixed = [against[:, names + 4 + c : names + 5 + c] for c in range(2)]
    constant = [turned[names + 4 + c : names + 5 + c, :] for c in range(2)]

    def on(k, e):
        return (routes[:, k : k + 1] == e).astype(F32)

    gate_grad = []
    for k in range(2):
        total = jnp.sum(values[k] * cot, axis=1, keepdims=True) + on(k, experts + 1) * both
        for c in range(2):
            total += on(k, experts + 2 + c) * (mixing[c][0] * both + mixing[c][1] * fixed[c])
        gate_grad.append(total)
    mean = gates[0] * gate_grad[0] + gates[1] * gate_grad[1]
    chosen = [gates[k] * (gate_grad[k] - mean) for k in range(2)]
    weight = [sum(on(k, experts + 2 + c) * gates[k] for k in range(2)) for c in range(2)]
    copied = sum(on(k, experts + 1) * gates[k] for k in range(2))
    copied += weight[0] * mixing[0][0] + weight[1] * mixing[1][0]
    lane = lanes_of((tok, LANES))
    logit_grad = jnp.where(lane == routes[:, 0:1], chosen[0], 0.0)
    logit_grad += jnp.where(lane == routes[:, 1:2], chosen[1], 0.0)
    wide = logit_grad
    shares = jnp.zeros((tok, LANES), F32)
    output = residual + gates[0] * values[0] + gates[1] * values[1] + copied * hidden
    for c in range(2):
        parts = [weight[c] * both, weight[c] * fixed[c]]
        middle = mixing[c][0] * parts[0] + mixing[c][1] * parts[1]
        for i in range(2):
            wide = jnp.where(lane == names + 2 * c + i, mixing[c][i] * (parts[i] - middle), wide)
        share = weight[c] * mixing[c][1]
        shares = jnp.where(lane == names + 4 + c, share, shares)
        output += share * constant[c]
    layer_ref[...] = output.astype(BF16)
    logits_ref[...] = lax.dot_general(
        logit_grad, carry_ref[...], NT, precision=lax.Precision.HIGHEST,
        preferred_element_type=F32,
    )
    ride = lax.dot_general(
        past_ref[...], pltpu.roll(logit_grad, names + 6, 1), TN, precision=lax.Precision.HIGHEST,
        preferred_element_type=F32,
    )
    high, low = halves(wide)
    hidden_grad += copied * cot + dot_nt(high, small) + dot_nt(low, small)
    scaled = hidden_grad * turned[LANES - 1 : LANES, :]
    residual_grad = (
        cot
        + scale * scaled
        - residual * (scale * scale * scale) * jnp.mean(scaled * residual, axis=1, keepdims=True)
    )
    rgrad_ref[...] = residual_grad
    residual_low = residual_grad.astype(BF16)
    agrad_ref[...] = dot_nt(residual_low, col_ref[...]).astype(BF16)
    gained = jnp.sum((hidden_grad * residual * scale).reshape(tok // 8, 8, D), axis=0)
    gained = jnp.sum(gained, axis=0, keepdims=True)
    column = lax.broadcasted_iota(jnp.int32, (LANES, D), 0)
    second = jnp.where(column == LANES - 1, gained, 0.0).T
    shares_high, shares_low = halves(shares)
    small_grad = (
        second
        + dot_tn(hidden_low, high)
        + dot_tn(hidden_low, low)
        + dot_tn(cot_low, shares_high)
        + dot_tn(cot_low, shares_low)
    )
    height = D // fsdp
    ride = jnp.concatenate([ride[:16], jnp.zeros((height - 16, LANES), F32)], axis=0)
    small_grad += jnp.concatenate([ride] * fsdp, axis=0)
    small_sum[...] = small_grad.astype(BF16)
    for c, out_ref in enumerate((mine_ref, theirs_ref)):
        core = (core_ref[0] + c) % 2
        store_pieces(out_ref, dot(rows_of_core(att_ref, core, fsdp), residual_low).astype(BF16), 0)
        store_pieces(out_ref, rows_of_core(small_sum, core, fsdp), D)


def combine(experts, fsdp, *args):
    tok = args[1].shape[0]
    outs = [
        jax.ShapeDtypeStruct((tok, D), BF16),
        jax.ShapeDtypeStruct((tok, D), F32),
        jax.ShapeDtypeStruct((tok, D), BF16),
        jax.ShapeDtypeStruct((tok, LANES), F32),
    ] + piece_shapes(D + LANES, experts)
    return pl.pallas_call(
        functools.partial(combine_kernel, experts, fsdp),
        in_specs=[pl.BlockSpec(memory_space=pltpu.SMEM)] + whole_specs(args),
        out_specs=whole_specs(outs),
        out_shape=outs,
        scratch_shapes=[pltpu.VMEM((D, LANES), BF16)],
        compiler_params=vmem(56),
        cost_estimate=cost(2 * tok * D * (2 * D + 3 * experts * CAP), 14 << 20, weight=LATE),
        name="combine",
    )(core_number(), *args)


def normed_grad_kernel(sizes, *refs):
    grads = refs[: 3 * len(sizes)]
    w_ref, *outs = refs[3 * len(sizes) :]
    step = pl.program_id(0)
    last = pl.num_programs(0) - 1

    def part(kind):
        total, at = None, kind * D
        for i, size in enumerate(sizes):
            term = dot_nt(grads[3 * i + kind][...], w_ref[:, at : at + size])
            total = term if total is None else total + term
            at += size
        return total

    grad = part(1) + part(2)

    for i, ref in enumerate(outs[:-1]):

        @pl.when(step == i)
        def _(ref=ref):
            ref[...] = grad.astype(BF16)

    @pl.when(step == last)
    def _():
        outs[-1][...] = grad + part(0)


def normed_grad(parts, weights):
    sizes = [p[0].shape[1] for p in parts]
    tok, span = parts[0][0].shape[0], parts[0][1].shape[0]
    blocks = span // tok
    fixed = lambda s: (0, 0)
    moving = lambda s: (s, 0)
    specs = []
    for size in sizes:
        specs += [pl.BlockSpec((tok, size), fixed)] + [pl.BlockSpec((tok, size), moving)] * 2
    return pl.pallas_call(
        functools.partial(normed_grad_kernel, sizes),
        grid=(blocks,),
        in_specs=specs + [pl.BlockSpec(weights.shape, fixed)],
        out_specs=[pl.BlockSpec((tok, D), fixed)] * blocks,
        out_shape=[jax.ShapeDtypeStruct((tok, D), BF16)] * (blocks - 1)
        + [jax.ShapeDtypeStruct((tok, D), F32)],
        compiler_params=vmem(24),
        cost_estimate=cost(4 * span * D * D, 16 << 20, weight=LATE),
        name="normed_grad",
    )(*in_vmem(*[g for p in parts for g in p]), weights)


def turn_kernel(x_ref, out_ref):
    out_ref[...] = x_ref[...].T


def turn(x):
    return pl.pallas_call(
        turn_kernel,
        in_specs=whole_specs(range(1)),
        out_specs=pl.BlockSpec(memory_space=pltpu.VMEM),
        out_shape=jax.ShapeDtypeStruct(x.shape[::-1], x.dtype),
        compiler_params=vmem(24),
        cost_estimate=cost(0, 8 << 20),
        name="turn",
    )(x)


def project_grad_kernel(count, core_ref, normed_ref, dq_ref, dk_ref, dv_ref, out_ref):
    own = normed_ref.shape[1] - dq_ref.shape[0]
    turned = rows_of_core(normed_ref, core_ref[0], count)
    for kind, ref in enumerate((dq_ref, dk_ref, dv_ref)):
        left = turned[:, own:] if kind == 0 else turned
        store_pieces(out_ref, dot(left, ref[...]).astype(BF16), kind * D)


def project_grad(core, normed_turned, grads, parts, count):
    span = normed_turned.shape[1]
    out = piece_shapes(3 * D, parts)[0]
    return pl.pallas_call(
        functools.partial(project_grad_kernel, count),
        in_specs=[pl.BlockSpec(memory_space=pltpu.SMEM)] + whole_specs(range(4)),
        out_specs=pl.BlockSpec(memory_space=pltpu.VMEM),
        out_shape=out,
        compiler_params=vmem(24),
        cost_estimate=cost(2 * span * D * D, 8 << 20, weight=LATE),
        name="project_grad",
    )(core, normed_turned, *in_vmem(*grads))


def after(x, *others):
    return lax.optimization_barrier((x, others))[0]


class Sequence:
    def __init__(self):
        self.last = ()

    def take(self, *values):
        return lax.optimization_barrier((values, self.last))[0]

    def done(self, *values):
        self.last = values


def folded(count):
    return [0] + list(range(1, count, 2)) + list(range(2, count, 2))[::-1]


def siblings(count):
    return [(i, i ^ 1) for i in range(count)]


def ring_gather(x, count, gates, last):
    chips = count // 2
    order = folded(chips)
    follow = {order[i]: order[(i + 1) % chips] for i in range(chips)}
    pairs = [(2 * z + c, 2 * follow[z] + c) for z in range(chips) for c in range(2)]
    me = lax.axis_index("fsdp")
    chip, core = me // 2, me % 2
    at = jnp.array([order.index(z) for z in range(chips)], jnp.int32)[chip]
    ring = jnp.array(order, jnp.int32)
    chunks, places = [], []
    current = x
    for k in range(chips):
        source = ring[(at - k) % chips]
        chunks += [current, lax.ppermute(current, "fsdp", siblings(count))]
        places += [2 * source + core, 2 * source + 1 - core]
        if k + 1 < chips:
            if 0 < k <= len(gates) and gates[k - 1]:
                current = after(current, *gates[k - 1])
            current = lax.ppermute(current, "fsdp", pairs)
            if k + 2 == chips:
                current = after(current, *last)
    return chunks, jnp.stack(places).astype(jnp.int32)


def earlier_rows(x, count, others):
    up = [(i, i + 2) for i in range(count - 2)]
    second = lax.ppermute(x, "fsdp", up)
    core = lax.axis_index("fsdp") % 2
    first = after(jnp.where(core == 0, x, second), *others)
    first = lax.ppermute(first, "fsdp", siblings(count))
    return second, first


def return_send(second, across, count):
    core = lax.axis_index("fsdp") % 2
    across = across.astype(F32)
    total = jnp.where(core == 0, second.astype(F32), second.astype(F32) + across).astype(BF16)
    down = [(i + 2, i) for i in range(count - 2)]
    return lax.ppermute(total, "fsdp", down), jnp.where(core == 0, across, 0.0).astype(BF16), total


def quarter_gather(x, experts, count):
    chips = count // 2
    rows, width = x.shape
    each = width // experts
    me, group = lax.axis_index("fsdp"), lax.axis_index("expert")
    chip, core = me // 2, me % 2
    mine = lax.dynamic_slice_in_dim(x, group * each, each, 1)
    fetched = [mine]
    for k in range(1, chips):
        pairs = [(2 * z + c, 2 * ((z + k) % chips) + c) for z in range(chips) for c in range(2)]
        fetched.append(lax.ppermute(mine, "fsdp", pairs))
    stacked = jnp.stack(fetched)
    terms = plane_all(stacked, experts)
    chunks, columns = [], []
    for k in range(experts):
        here = after(terms[0], terms[-1]) if k == 0 else terms[k]
        chunks += [terms[k], sibling(here, count)]
        columns.append(group ^ k)
    blocks = []
    for k in range(chips):
        source = (chip - k) % chips
        blocks += [2 * source + core, 2 * source + 1 - core]
    places = [jnp.stack(p).astype(jnp.int32) for p in (blocks, columns)]
    return chunks, places, stacked


def sibling(x, count):
    return lax.ppermute(x, "fsdp", siblings(count))


def summed(terms):
    total = terms[0].astype(F32)
    for term in terms[1:]:
        total += term.astype(F32)
    return total.astype(BF16)


def in_plane(x):
    return lax.all_to_all(x, "expert", split_axis=0, concat_axis=0, tiled=True)


def plane_send(mine, other, experts):
    group = lax.axis_index("expert")

    def part(k):
        pair = [lax.dynamic_index_in_dim(x, group ^ k, 0, False) for x in (mine, other)]
        return summed(pair)

    parts = [part(k) for k in range(experts)]
    moved = [
        lax.ppermute(parts[k], "expert", [(i, i ^ k) for i in range(experts)])
        for k in range(1, experts)
    ]
    return parts[:1] + moved, parts


def line_send(pair, count):
    chips = count // 2
    chip = lax.axis_index("fsdp") // 2
    pair = [x.reshape(chips, x.shape[-2] // chips, x.shape[-1]) for x in pair]

    def part(k):
        at = (chip + k) % chips
        return summed([lax.dynamic_index_in_dim(x, at, 0, False) for x in pair])

    parts = [part(k) for k in range(chips)]
    moved = []
    for k in range(1, chips):
        pairs = [(2 * z + c, 2 * ((z + k) % chips) + c) for z in range(chips) for c in range(2)]
        moved.append(lax.ppermute(parts[k], "fsdp", pairs))
    return parts[:1] + moved, parts


def plane_all(x, experts):
    terms = [x]
    for k in range(1, experts):
        terms.append(lax.ppermute(x, "expert", [(i, i ^ k) for i in range(experts)]))
    return terms


def plane_columns(terms):
    experts = len(terms)
    terms = jnp.stack(terms)
    group = lax.axis_index("expert")
    parts = [lax.dynamic_index_in_dim(terms, j ^ group, 0, False) for j in range(experts)]
    return jnp.concatenate(parts, axis=1).astype(F32)


def plane_sum(terms):
    terms = [t.astype(F32) for t in terms]
    while len(terms) > 1:
        terms = [terms[i] + terms[i + 1] for i in range(0, len(terms), 2)]
    return terms[0]


def local(
    tokens,
    past_logits,
    routes,
    lengths,
    projector,
    collector,
    router,
    blender,
    constants,
    first_gain,
    second_gain,
    carryover,
    gating,
    upward,
    downward,
    cotangent,
):
    tok = tokens.shape[0]
    experts = lax.axis_size("expert")
    count = lax.axis_size("fsdp")
    names = experts + 4
    hops = WINDOW // tok
    me = lax.axis_index("fsdp")

    shard = projector.shape[0]
    gap = LANES - names - 8
    small = jnp.concatenate(
        [router, blender, constants, jnp.zeros((shard, gap), BF16)]
        + [first_gain[:, None], second_gain[:, None]],
        axis=1,
    )
    width = 3 * D + LANES
    filler = jnp.zeros((shard, -width % (experts * LANES)), BF16)
    shared = jnp.concatenate([projector, small, filler], axis=1)
    chunks, (blocks_at, columns_at), stacked = quarter_gather(shared, experts, count)
    own = jnp.concatenate([gating[0], upward[0], downward[0]], axis=1)
    second, first = earlier_rows(tokens, count, chunks[0::2])
    tokens_all = jnp.concatenate([second, first, tokens], axis=0)
    collector_all = lax.all_gather(collector, "fsdp", axis=0, tiled=True)

    span = tok + WINDOW
    key_positions = (me - hops) * tok + jnp.arange(span, dtype=jnp.int32)
    cosine, sine = rope_tables(key_positions.astype(F32))
    bounds = jnp.cumsum(lengths[0])
    biases = []
    for t in range(tok // QTILE):
        at = me * tok + t * QTILE + jnp.arange(QTILE, dtype=jnp.int32)
        start = jnp.max(jnp.where(bounds[:, None] <= at[None, :], bounds[:, None], 0), axis=0)
        least = jnp.maximum(at - (WINDOW - 1), start)
        keys_at = key_positions[t * QTILE : t * QTILE + SPAN, None]
        inside = (keys_at >= least[None, :]) & (keys_at <= at[None, :])
        biases.append(jnp.where(inside, 0.0, masked_score).astype(F32))
    bias = jnp.stack(biases)
    onehot = (routes[:, :, None] == jnp.arange(experts, dtype=jnp.int32)).astype(BF16)
    per_token = jnp.sum(onehot, axis=1)
    lower = jnp.tril(jnp.ones((tok, tok), BF16), -1)
    before = jnp.dot(lower, per_token, preferred_element_type=F32)
    position_in = jnp.sum(onehot.astype(F32) * before[:, None, :], axis=2).astype(jnp.int32)
    slots = jnp.where(routes < experts, routes * CAP + position_in, experts * CAP)
    past_part = jnp.dot(
        past_logits, carryover, precision=lax.Precision.HIGHEST, preferred_element_type=F32
    )
    past_part = jnp.pad(past_part, ((0, 0), (0, LANES - names)))
    past_wide = jnp.pad(past_logits, ((0, 0), (0, LANES - names)))
    carry_wide = jnp.pad(carryover, ((0, LANES - names), (0, LANES - names)))

    weights, normed_all, q, k, v = project(
        blocks_at, columns_at, chunks, tokens_all, cosine, sine, tok
    )
    small_all = weights[:, 3 * D : 3 * D + LANES]
    half = 4
    att_a, lse_a = attend(q, k, v, bias, 0, half)
    att_b, lse_b = attend(q, k, v, bias, half, PAIRS - half)
    lse = jnp.concatenate([lse_a, lse_b], axis=0)
    attended, residual, hidden, aux, send = route(
        experts, att_a, att_b, collector_all, tokens, cotangent, small_all, past_part, routes, slots.T
    )

    def exchange(x):
        x = x.reshape(experts, CAP, 2 * D)
        x = lax.all_to_all(x, "expert", split_axis=0, concat_axis=0, tiled=True)
        return x.reshape(experts * CAP, 2 * D)

    normed_turned, attended_turned = turn(after(normed_all, send)), turn(after(attended, send))
    probability = weigh(after(q, send), k, lse, bias)
    waiting = [probability, normed_turned, attended_turned]
    weight_chunks, weight_places = ring_gather(own, count, [[q], [send]], waiting)
    arrived = after(exchange(send), *waiting)
    answers, low = expert_rows(arrived, weight_places, weight_chunks)
    returned = exchange(answers)
    sums = expert_sums(arrived, low)
    sums = lax.psum_scatter(sums, "fsdp", scatter_dimension=0, tiled=True)

    layer_output, residual_grad, attended_grad, logits_grad, *col_grad = combine(
        experts, count, returned, residual, hidden, cotangent, aux, small_all, collector_all,
        attended_turned, past_wide, carry_wide, routes, slots,
    )
    def back(upstream):
        return attend_back(q, k, v, attended, upstream, probability, cosine, sine)

    col_mine, col_theirs = col_grad
    core = core_number()
    seq = Sequence()
    col_other = sibling(col_theirs, count)
    grads = back(attended_grad)
    seq.done(grads)
    (col_other,) = seq.take(col_other)
    col_terms, parts = plane_send(col_mine, col_other, experts)
    seq.done(parts)
    (turned,) = seq.take(normed_turned)
    theirs = project_grad(1 - core, turned, grads, experts, count)
    other = sibling(theirs, count)
    seq.done(theirs)
    (again,) = seq.take(weights)
    *halo_grads, own_grad = normed_grad([grads], again)
    across = sibling(halo_grads[1], count)
    seq.done(own_grad)
    (turned,) = seq.take(normed_turned)
    mine = project_grad(core, turned, grads, experts, count)
    seq.done(mine)
    (other,) = seq.take(other)
    terms, parts = plane_send(mine, other, experts)
    seq.done(parts)
    (across,) = seq.take(across)
    after_rows, across, total = return_send(halo_grads[0], across, count)
    seq.done(total)
    (col_terms,) = seq.take(col_terms)
    col_part = summed(col_terms)
    seq.done(col_part)
    (terms,) = seq.take(terms)
    merged = jnp.concatenate([summed(terms), col_part], axis=1)
    cut = mine.shape[2]
    terms, parts = line_send([merged], count)
    seq.done(parts)
    (sums,) = seq.take(sums)
    sums = sums.astype(F32)
    seq.done(sums)
    (terms,) = seq.take(terms)
    merged = summed(terms)
    terms = plane_all(merged, experts)
    seq.done(merged)
    (after_rows,) = seq.take(after_rows)
    own_grad = own_grad + across.astype(F32) + after_rows.astype(F32)
    tokens_wide = tokens.astype(F32)
    first_scale = norm_scale(tokens_wide)
    scaled = own_grad * small_all[:, LANES - 2].astype(F32)
    gradient_tokens = (
        residual_grad
        + first_scale * scaled
        - tokens_wide
        * (first_scale * first_scale * first_scale)
        * jnp.mean(scaled * tokens_wide, axis=-1, keepdims=True)
    ).astype(BF16)
    seq.done(gradient_tokens)
    (terms,) = seq.take(terms)
    projector_rows = plane_columns([t[:, :cut] for t in terms])[:, : 3 * D]
    col_rows = plane_columns([t[:, cut:] for t in terms])
    first_rows = jnp.sum(projector.astype(F32) * projector_rows, axis=1) / first_gain.astype(F32)

    return (
        layer_output,
        gradient_tokens,
        logits_grad[:, :names],
        projector_rows,
        col_rows[:, :D],
        col_rows[:, D : D + names],
        col_rows[:, D + names : D + names + 4],
        col_rows[:, D + names + 4 : D + names + 6],
        first_rows,
        col_rows[:, D + LANES - 1],
        col_rows[:names, D + names + 6 : D + 2 * names + 6],
        sums[:, :FF][None],
        sums[:, FF : 2 * FF][None],
        sums[:, 2 * FF :][None],
    )


def solution(mesh):
    rows = P(("expert", "fsdp"), None)
    shared = P("fsdp", None)
    expert = P("expert", "fsdp", None)
    return jax.shard_map(
        local,
        mesh=mesh,
        in_specs=(
            rows, rows, rows, P("expert", None), shared, shared, shared, shared, shared,
            P("fsdp"), P("fsdp"), P(), expert, expert, expert, rows,
        ),
        out_specs=(
            rows, rows, rows, shared, shared, shared, shared, shared,
            P("fsdp"), P("fsdp"), P(), expert, expert, expert,
        ),
        check_vma=False,
    )
```

```python
import functools
import math

import jax
import jax.numpy as jnp
from jax import lax
from jax.experimental import pallas as pl
from jax.experimental.pallas import tpu as pltpu
from jax.sharding import PartitionSpec as P

D = 768
H = 12
HD = 64
FF = 2048
WINDOW = 1024
CAP = 128

epsilon = 1e-06
rope_base = 10000.0
masked_score = -1e30
QTILE = 256
SPAN = QTILE + WINDOW
LANES = 128
PAIRS = H * HD // LANES
FTILE = 512
STILE = 2048
LATE = 6
NT = (((1,), (1,)), ((), ()))
TN = (((0,), (0,)), ((), ()))
F32 = jnp.float32
BF16 = jnp.bfloat16
query_scale = 1.0 / math.sqrt(HD)


def vmem(megabytes):
    return pltpu.CompilerParams(vmem_limit_bytes=megabytes << 20)


def in_hbm(*arrays):
    return [pltpu.with_memory_space_constraint(a, pltpu.HBM) for a in arrays]


def in_vmem(*arrays):
    return [pltpu.with_memory_space_constraint(a, pltpu.VMEM) for a in arrays]


def cost(flops, moved, trans=0, weight=1):
    return pl.CostEstimate(
        flops=int(weight * flops), bytes_accessed=int(weight * moved), transcendentals=int(trans)
    )


def dot(a, b):
    return jnp.dot(a, b, preferred_element_type=F32)


def dot_nt(a, b):
    return lax.dot_general(a, b, NT, preferred_element_type=F32)


def dot_tn(a, b):
    return lax.dot_general(a, b, TN, preferred_element_type=F32)


def halves(x):
    high = x.astype(BF16)
    return high, (x - high.astype(F32)).astype(BF16)


def lanes_of(shape):
    return lax.broadcasted_iota(jnp.int32, shape, len(shape) - 1)


def norm_scale(values):
    return lax.rsqrt(jnp.mean(values * values, axis=-1, keepdims=True) + epsilon)


def piece_shapes(width, parts):
    each = -(-width // (parts * LANES)) * LANES
    return [jax.ShapeDtypeStruct((parts, D // 2, each), BF16)] * 2


def rows_of_core(ref, core, count):
    rows = D // count
    at = [pl.multiple_of((2 * z + core) * rows, rows) for z in range(count // 2)]
    return jnp.concatenate([ref[pl.ds(a, rows), :] for a in at], axis=0)


def store_pieces(out_ref, value, at):
    each = out_ref.shape[2]
    for left in range(0, value.shape[1], LANES):
        part, inner = divmod(at + left, each)
        out_ref[part, :, inner : inner + LANES] = value[:, left : left + LANES]


def core_number():
    return (lax.axis_index("fsdp") % 2).astype(jnp.int32).reshape(1)


def rope_tables(positions):
    lane = jnp.arange(LANES, dtype=jnp.int32)
    half = HD // 2
    freq_index = (lane % half).astype(F32)
    inverse = jnp.exp(freq_index * (-2.0 * math.log(rope_base) / HD))
    angles = positions[:, None] * inverse[None, :]
    sign = jnp.where(lane % HD < half, -1.0, 1.0).astype(F32)
    return jnp.cos(angles), jnp.sin(angles) * sign[None, :]


def swapped(x):
    half = HD // 2
    lane = lanes_of(x.shape)
    return jnp.where(
        lane % HD < half, pltpu.roll(x, LANES - half, 1), pltpu.roll(x, half, 1)
    )


def rotate(x, cosine, sine):
    return x * cosine + swapped(x) * sine


def rotate_back(x, cosine, sine):
    return x * cosine - swapped(x) * sine


def project_kernel(blocks_at, columns_at, *refs):
    chips, parts = blocks_at.shape[0] // 2, columns_at.shape[0]
    chunks = refs[: 2 * parts]
    *tok_refs, cos_ref, sin_ref, w_ref, small_ref, normed_ref, q_ref, k_ref, v_ref, x_ref = refs[
        2 * parts :
    ]
    rows, width = chunks[0].shape[1:]
    step = pl.program_id(0)

    @pl.when(step == 0)
    def _():
        for e in range(parts):
            left = pl.multiple_of(columns_at[e] * width, LANES)
            for z in range(chips):
                for c in range(2):
                    above = pl.multiple_of(blocks_at[2 * z + c] * rows, rows)
                    w_ref[pl.ds(above, rows), pl.ds(left, width)] = chunks[2 * e + c][z]
        small_ref[...] = w_ref[:, 3 * D : 3 * D + LANES]

    for i, ref in enumerate(tok_refs):

        @pl.when(step == i)
        def _(ref=ref):
            x_ref[...] = ref[...]

    gain = small_ref[...].astype(F32).T[LANES - 2 : LANES - 1, :]
    x = x_ref[...].astype(F32)
    normed = (x * norm_scale(x) * gain).astype(BF16)
    normed_ref[...] = normed
    cosine, sine = cos_ref[...], sin_ref[...]
    keys = dot(normed, w_ref[:, D : 2 * D])
    for j in range(PAIRS):
        part = slice(j * LANES, (j + 1) * LANES)
        k_ref[:, part] = rotate(keys[:, part], cosine, sine).astype(BF16)
    v_ref[...] = dot(normed, w_ref[:, 2 * D : 3 * D]).astype(BF16)

    @pl.when(step == pl.num_programs(0) - 1)
    def _():
        queries = dot(normed, w_ref[:, :D])
        for j in range(PAIRS):
            part = slice(j * LANES, (j + 1) * LANES)
            q_ref[:, part] = (rotate(queries[:, part], cosine, sine) * query_scale).astype(BF16)


def project(blocks_at, columns_at, chunks, tokens, cosine, sine):
    chips, rows, width = chunks[0].shape
    parts = columns_at.shape[0]
    blocks, tok = len(tokens), tokens[0].shape[0]
    fixed = lambda s, *_: (0, 0)
    moving = lambda s, *_: (s, 0)
    span = blocks * tok
    return pl.pallas_call(
        project_kernel,
        grid_spec=pltpu.PrefetchScalarGridSpec(
            num_scalar_prefetch=2,
            grid=(blocks,),
            in_specs=[pl.BlockSpec((chips, rows, width), lambda s, *_: (0, 0, 0))] * len(chunks)
            + [pl.BlockSpec((tok, D), fixed)] * blocks
            + [pl.BlockSpec((tok, LANES), moving)] * 2,
            out_specs=[
                pl.BlockSpec((D, parts * width), fixed),
                pl.BlockSpec((D, LANES), fixed),
                pl.BlockSpec((tok, D), moving),
                pl.BlockSpec((tok, D), fixed),
                pl.BlockSpec((tok, D), moving),
                pl.BlockSpec((tok, D), moving),
            ],
            scratch_shapes=[pltpu.VMEM((tok, D), BF16)],
        ),
        out_shape=[
            jax.ShapeDtypeStruct((D, parts * width), BF16),
            jax.ShapeDtypeStruct((D, LANES), BF16),
            jax.ShapeDtypeStruct((span, D), BF16),
            jax.ShapeDtypeStruct((tok, D), BF16),
            jax.ShapeDtypeStruct((span, D), BF16),
            jax.ShapeDtypeStruct((span, D), BF16),
        ],
        compiler_params=vmem(24),
        cost_estimate=cost(2 * span * D * 2 * D, 20 << 20),
        name="project",
    )(blocks_at, columns_at, *chunks, *tokens, cosine, sine)


def head_mask(x, head):
    return jnp.where(lanes_of(x.shape) // HD == head, x, jnp.zeros_like(x))


def both_heads(x):
    return jnp.concatenate([head_mask(x, 0), head_mask(x, 1)], axis=0)


def own_head(x):
    return jnp.concatenate([x[:HD, :QTILE], x[HD:, QTILE:]], axis=0).T


def attend_kernel(q_ref, k_ref, v_ref, bias_ref, o_ref, lse_ref, vt_ref):
    vt_ref[...] = v_ref[...].T
    for t in range(q_ref.shape[0] // QTILE):
        rows = slice(t * QTILE, (t + 1) * QTILE)
        span = slice(t * QTILE, t * QTILE + SPAN)
        s = dot_nt(k_ref[span, :], both_heads(q_ref[rows, :]))
        s += jnp.concatenate([bias_ref[t]] * 2, axis=1)
        top = jnp.max(s, axis=0, keepdims=True)
        e = jnp.exp(s - top)
        total = jnp.sum(e, axis=0, keepdims=True)
        o_ref[rows, :] = own_head(dot(vt_ref[:, span], e.astype(BF16)) / total).astype(BF16)
        lse = top + jnp.log(total)
        for h in range(2):
            lse_ref[0, h : h + 1, rows] = lse[:, h * QTILE : (h + 1) * QTILE]


def attend(q, k, v, bias, first, pairs):
    tok, span = q.shape[0], k.shape[0]
    col = lambda p: (0, first + p)
    return pl.pallas_call(
        attend_kernel,
        grid=(pairs,),
        in_specs=[
            pl.BlockSpec((tok, LANES), col),
            pl.BlockSpec((span, LANES), col),
            pl.BlockSpec((span, LANES), col),
            pl.BlockSpec(bias.shape, lambda p: (0, 0, 0)),
        ],
        out_specs=[
            pl.BlockSpec((tok, LANES), lambda p: (0, p)),
            pl.BlockSpec((1, 8, tok), lambda p: (p, 0, 0)),
        ],
        out_shape=[
            jax.ShapeDtypeStruct((tok, pairs * LANES), BF16),
            jax.ShapeDtypeStruct((pairs, 8, tok), F32),
        ],
        scratch_shapes=[pltpu.VMEM((LANES, span), BF16)],
        compiler_params=vmem(24),
        cost_estimate=cost(16 * tok * SPAN * pairs * LANES, pairs << 20, tok * SPAN * 2 * pairs),
        name="attend",
    )(q, k, v, bias)


def attend_back_kernel(
    q_ref, k_ref, v_ref, o_ref, do_ref, lse_ref, bias_ref, cos_ref, sin_ref,
    dq_ref, dk_ref, dv_ref, kt_ref, dk_sum, dv_sum,
):
    tok = q_ref.shape[0]
    own = k_ref.shape[0] - tok
    kt_ref[...] = k_ref[...].T
    dk_sum[...] = jnp.zeros_like(dk_sum)
    dv_sum[...] = jnp.zeros_like(dv_sum)
    for t in range(tok // QTILE):
        rows = slice(t * QTILE, (t + 1) * QTILE)
        span = slice(t * QTILE, t * QTILE + SPAN)
        keys, values = k_ref[span, :], v_ref[span, :]
        queries, upstream = q_ref[rows, :], do_ref[rows, :]
        product = (upstream.astype(F32) * o_ref[rows, :].astype(F32)).T
        qh, gh = both_heads(queries), both_heads(upstream)
        lse = jnp.concatenate([lse_ref[0, h : h + 1, rows] for h in range(2)], axis=1)
        delta = jnp.concatenate(
            [jnp.sum(product[h * HD : (h + 1) * HD], axis=0, keepdims=True) for h in range(2)],
            axis=1,
        )
        s = dot_nt(keys, qh) + jnp.concatenate([bias_ref[t]] * 2, axis=1)
        p = jnp.exp(s - lse)
        ds = (p * (dot_nt(values, gh) - delta)).astype(BF16)
        dv_sum[span, :] += dot(p.astype(BF16), gh)
        dk_sum[span, :] += dot(ds, qh)
        dq = own_head(dot(kt_ref[:, span], ds))
        there = slice(own + t * QTILE, own + (t + 1) * QTILE)
        dq = rotate_back(dq, cos_ref[there, :], sin_ref[there, :]) * query_scale
        dq_ref[rows, :] = dq.astype(BF16)
    dk_ref[...] = rotate_back(dk_sum[...], cos_ref[...], sin_ref[...]).astype(BF16)
    dv_ref[...] = dv_sum[...].astype(BF16)


def attend_back(q, k, v, o, do, lse, bias, cosine, sine):
    tok, span = q.shape[0], k.shape[0]
    pairs = PAIRS
    col = out = lambda p: (0, p)
    whole = lambda p: (0, 0)
    mine = pl.BlockSpec((tok, LANES), col)
    long = pl.BlockSpec((span, LANES), col)
    return pl.pallas_call(
        attend_back_kernel,
        grid=(pairs,),
        in_specs=[
            mine,
            long,
            long,
            pl.BlockSpec((tok, LANES), col),
            mine,
            pl.BlockSpec((1, 8, tok), lambda p: (p, 0, 0)),
            pl.BlockSpec(bias.shape, lambda p: (0, 0, 0)),
            pl.BlockSpec((span, LANES), whole),
            pl.BlockSpec((span, LANES), whole),
        ],
        out_specs=[
            pl.BlockSpec((tok, LANES), out),
            pl.BlockSpec((span, LANES), out),
            pl.BlockSpec((span, LANES), out),
        ],
        out_shape=[
            pltpu.VMEM((tok, pairs * LANES), BF16),
            pltpu.VMEM((span, pairs * LANES), BF16),
            pltpu.VMEM((span, pairs * LANES), BF16),
        ],
        scratch_shapes=[
            pltpu.VMEM((LANES, span), BF16),
            pltpu.VMEM((span, LANES), F32),
            pltpu.VMEM((span, LANES), F32),
        ],
        compiler_params=vmem(32),
        cost_estimate=cost(40 * tok * SPAN * pairs * LANES, pairs << 21, tok * SPAN * 2 * pairs, weight=LATE),
        name="attend_back",
    )(*in_hbm(q, k, v, o, do), lse, *in_hbm(bias, cosine, sine))


def route_kernel(
    experts, att_a, att_b, col_ref, tok_ref, cot_ref, small_ref, past_ref, routes_ref, slots_ref,
    att_ref, residual_ref, hidden_ref, aux_ref, send_ref,
):
    small = small_ref[...]
    gain = small.astype(F32).T[LANES - 1 : LANES, :]
    att_ref[...] = jnp.concatenate([att_a[...], att_b[...]], axis=1)
    residual = tok_ref[...].astype(F32) + dot(att_ref[...], col_ref[...])
    scale = norm_scale(residual)
    hidden = (residual * scale * gain).astype(BF16)
    residual_ref[...] = residual
    hidden_ref[...] = hidden
    mixed = dot(hidden, small)
    logits = mixed + past_ref[...]
    lane = lanes_of(logits.shape)
    routes = routes_ref[...]
    picked = [
        jnp.sum(jnp.where(lane == routes[:, k : k + 1], logits, 0.0), axis=1, keepdims=True)
        for k in range(2)
    ]
    top = jnp.maximum(picked[0], picked[1])
    raised = [jnp.exp(x - top) for x in picked]
    total = raised[0] + raised[1]
    gates = [x / total for x in raised]
    names = experts + 4
    aux = [gates[0], gates[1]]
    for c in range(2):
        pair = [mixed[:, names + 2 * c + i : names + 2 * c + i + 1] for i in range(2)]
        above = jnp.maximum(pair[0], pair[1])
        up = [jnp.exp(x - above) for x in pair]
        aux += [up[0] / (up[0] + up[1]), up[1] / (up[0] + up[1])]
    aux.append(scale)
    packed = jnp.zeros(logits.shape, F32)
    for i, value in enumerate(aux):
        packed = jnp.where(lane == i, value, packed)
    aux_ref[...] = packed
    cot = cot_ref[...].astype(F32)
    slots = slots_ref[...]
    count, tok = send_ref.shape[0], hidden.shape[0]
    where = lax.broadcasted_iota(jnp.int32, (count, tok), 0)
    hot = [(where == slots[k : k + 1, :]).astype(F32).astype(BF16) for k in range(2)]
    send_ref[:, :D] = dot(hot[0] + hot[1], hidden).astype(BF16)
    grads = dot(hot[0], (gates[0] * cot).astype(BF16)) + dot(hot[1], (gates[1] * cot).astype(BF16))
    send_ref[:, D:] = grads.astype(BF16)


def whole_specs(arrays):
    return [pl.BlockSpec(memory_space=pltpu.VMEM) for _ in arrays]


def route(experts, *args):
    tok = args[0].shape[0]
    outs = [
        jax.ShapeDtypeStruct((tok, D), BF16),
        jax.ShapeDtypeStruct((tok, D), F32),
        jax.ShapeDtypeStruct((tok, D), BF16),
        jax.ShapeDtypeStruct((tok, LANES), F32),
        jax.ShapeDtypeStruct((experts * CAP, 2 * D), BF16),
    ]
    return pl.pallas_call(
        functools.partial(route_kernel, experts),
        in_specs=whole_specs(args),
        out_specs=whole_specs(outs),
        out_shape=outs,
        compiler_params=vmem(56),
        cost_estimate=cost(2 * tok * D * (D + 3 * experts * CAP), 9 << 20),
        name="route",
    )(*args)


def expert_kernel(place, x_ref, *refs):
    count = place.shape[0]
    chunks = refs[: 3 * count]
    out_ref, low_ref, answer, back, gw_ref, uw_ref, dw_ref = refs[3 * count :]
    step = pl.program_id(0)
    height = chunks[0].shape[0]

    @pl.when(step == 0)
    def _():
        answer[...] = jnp.zeros_like(answer)
        back[...] = jnp.zeros_like(back)

    for i in range(count):
        at = pl.ds(pl.multiple_of(place[i] * height, height), height)
        for j, w_ref in enumerate((gw_ref, uw_ref, dw_ref)):
            w_ref[at, :] = chunks[3 * i + j][...]
    rows, grads = x_ref[:, :D], x_ref[:, D:]
    gw, uw, dw = gw_ref[...], uw_ref[...], dw_ref[...]
    pre = dot(rows, gw)
    up = dot(rows, uw)
    grad = dot(grads, dw)
    sigmoid = 1.0 / (1.0 + jnp.exp(-pre))
    active = pre * sigmoid
    hidden = (active * up).astype(BF16)
    gate_low = (grad * up * sigmoid * (1.0 + pre * (1.0 - sigmoid))).astype(BF16)
    up_low = (grad * active).astype(BF16)
    low_ref[0] = gate_low
    low_ref[1] = up_low
    low_ref[2] = hidden
    answer[...] += dot_nt(hidden, dw)
    back[...] += dot_nt(gate_low, gw) + dot_nt(up_low, uw)

    @pl.when(step == pl.num_programs(0) - 1)
    def _():
        out_ref[:, :D] = answer[...].astype(BF16)
        out_ref[:, D:] = back[...].astype(BF16)


def expert_rows(x, place, chunks):
    rows, height = x.shape[0], chunks[0].shape[0]
    tiles = FF // FTILE
    weights, operands = [], []
    for chunk in chunks:
        for j in range(3):
            weights.append(pl.BlockSpec((height, FTILE), lambda s, *_, j=j: (0, j * tiles + s)))
            operands.append(chunk)
    return pl.pallas_call(
        expert_kernel,
        grid_spec=pltpu.PrefetchScalarGridSpec(
            num_scalar_prefetch=1,
            grid=(tiles,),
            in_specs=[pl.BlockSpec((rows, 2 * D), lambda s, *_: (0, 0))] + weights,
            out_specs=[
                pl.BlockSpec((rows, 2 * D), lambda s, *_: (0, 0)),
                pl.BlockSpec((3, rows, FTILE), lambda s, *_: (0, 0, s)),
            ],
            scratch_shapes=[pltpu.VMEM((rows, D), F32)] * 2 + [pltpu.VMEM((D, FTILE), BF16)] * 3,
        ),
        out_shape=[
            jax.ShapeDtypeStruct((rows, 2 * D), BF16),
            pltpu.HBM((3, rows, FF), BF16),
        ],
        compiler_params=vmem(32),
        cost_estimate=cost(12 * rows * D * FF, 20 << 20),
        name="expert_rows",
    )(place, x, *operands)


def expert_sums_kernel(x_ref, low_ref, out_ref, turned):
    step = pl.program_id(0)
    tiles = FF // STILE

    @pl.when(step == 0)
    def _():
        turned[...] = x_ref[:, :D].T

    @pl.when(step == 2 * tiles)
    def _():
        turned[...] = x_ref[:, D:].T

    out_ref[...] = dot(turned[...], low_ref[0]).astype(BF16)


def expert_sums(x, low):
    rows = x.shape[0]
    tiles = FF // STILE
    return pl.pallas_call(
        expert_sums_kernel,
        grid=(3 * tiles,),
        in_specs=[
            pl.BlockSpec((rows, 2 * D), lambda j: (0, 0)),
            pl.BlockSpec((1, rows, STILE), lambda j: (j // tiles, 0, j % tiles)),
        ],
        out_specs=pl.BlockSpec((D, STILE), lambda j: (0, j)),
        out_shape=pltpu.HBM((D, 3 * FF), BF16),
        scratch_shapes=[pltpu.VMEM((D, rows), BF16)],
        compiler_params=vmem(24),
        cost_estimate=cost(6 * rows * D * FF, 20 << 20),
        name="expert_sums",
    )(x, *in_hbm(low))


def combine_kernel(
    experts, fsdp, core_ref, back_ref, residual_ref, hidden_ref, cot_ref, aux_ref, small_ref, col_ref, att_ref,
    past_ref, carry_ref, routes_ref, slots_ref,
    layer_ref, rgrad_ref, agrad_ref, logits_ref, mine_ref, theirs_ref, turned_ref, small_sum,
):
    tok = hidden_ref.shape[0]
    names = experts + 4
    slots, routes = slots_ref[...], routes_ref[...]
    count = back_ref.shape[0]
    where = lax.broadcasted_iota(jnp.int32, (tok, count), 1)
    hot = [(where == slots[:, k : k + 1]).astype(F32).astype(BF16) for k in range(2)]
    answers, returned = back_ref[:, :D], back_ref[:, D:]
    values = [dot(hot[k], answers) for k in range(2)]
    hidden_grad = dot(hot[0] + hot[1], returned)
    hidden_low, cot_low = hidden_ref[...], cot_ref[...]
    hidden, cot = hidden_low.astype(F32), cot_low.astype(F32)
    residual = residual_ref[...]
    small = small_ref[...]
    turned = small.astype(F32).T
    aux = aux_ref[...]
    gates = [aux[:, k : k + 1] for k in range(2)]
    mixing = [[aux[:, 2 + 2 * c + i : 3 + 2 * c + i] for i in range(2)] for c in range(2)]
    scale = aux[:, 6:7]
    both = jnp.sum(hidden * cot, axis=1, keepdims=True)
    against = dot(cot_low, small)
    fixed = [against[:, names + 4 + c : names + 5 + c] for c in range(2)]
    constant = [turned[names + 4 + c : names + 5 + c, :] for c in range(2)]

    def on(k, e):
        return (routes[:, k : k + 1] == e).astype(F32)

    gate_grad = []
    for k in range(2):
        total = jnp.sum(values[k] * cot, axis=1, keepdims=True) + on(k, experts + 1) * both
        for c in range(2):
            total += on(k, experts + 2 + c) * (mixing[c][0] * both + mixing[c][1] * fixed[c])
        gate_grad.append(total)
    mean = gates[0] * gate_grad[0] + gates[1] * gate_grad[1]
    chosen = [gates[k] * (gate_grad[k] - mean) for k in range(2)]
    weight = [sum(on(k, experts + 2 + c) * gates[k] for k in range(2)) for c in range(2)]
    copied = sum(on(k, experts + 1) * gates[k] for k in range(2))
    copied += weight[0] * mixing[0][0] + weight[1] * mixing[1][0]
    lane = lanes_of((tok, LANES))
    logit_grad = jnp.where(lane == routes[:, 0:1], chosen[0], 0.0)
    logit_grad += jnp.where(lane == routes[:, 1:2], chosen[1], 0.0)
    wide = logit_grad
    shares = jnp.zeros((tok, LANES), F32)
    output = residual + gates[0] * values[0] + gates[1] * values[1] + copied * hidden
    for c in range(2):
        parts = [weight[c] * both, weight[c] * fixed[c]]
        middle = mixing[c][0] * parts[0] + mixing[c][1] * parts[1]
        for i in range(2):
            wide = jnp.where(lane == names + 2 * c + i, mixing[c][i] * (parts[i] - middle), wide)
        share = weight[c] * mixing[c][1]
        shares = jnp.where(lane == names + 4 + c, share, shares)
        output += share * constant[c]
    layer_ref[...] = output.astype(BF16)
    logits_ref[...] = lax.dot_general(
        logit_grad, carry_ref[...], NT, precision=lax.Precision.HIGHEST,
        preferred_element_type=F32,
    )
    ride = lax.dot_general(
        past_ref[...], pltpu.roll(logit_grad, names + 6, 1), TN, precision=lax.Precision.HIGHEST,
        preferred_element_type=F32,
    )
    high, low = halves(wide)
    hidden_grad += copied * cot + dot_nt(high, small) + dot_nt(low, small)
    scaled = hidden_grad * turned[LANES - 1 : LANES, :]
    residual_grad = (
        cot
        + scale * scaled
        - residual * (scale * scale * scale) * jnp.mean(scaled * residual, axis=1, keepdims=True)
    )
    rgrad_ref[...] = residual_grad
    residual_low = residual_grad.astype(BF16)
    agrad_ref[...] = dot_nt(residual_low, col_ref[...]).astype(BF16)
    gained = jnp.sum((hidden_grad * residual * scale).reshape(tok // 8, 8, D), axis=0)
    gained = jnp.sum(gained, axis=0, keepdims=True)
    column = lax.broadcasted_iota(jnp.int32, (LANES, D), 0)
    second = jnp.where(column == LANES - 1, gained, 0.0).T
    shares_high, shares_low = halves(shares)
    small_grad = (
        second
        + dot_tn(hidden_low, high)
        + dot_tn(hidden_low, low)
        + dot_tn(cot_low, shares_high)
        + dot_tn(cot_low, shares_low)
    )
    height = D // fsdp
    ride = jnp.concatenate([ride[:16], jnp.zeros((height - 16, LANES), F32)], axis=0)
    small_grad += jnp.concatenate([ride] * fsdp, axis=0)
    turned_ref[...] = att_ref[...].T
    small_sum[...] = small_grad.astype(BF16)
    for c, out_ref in enumerate((mine_ref, theirs_ref)):
        core = (core_ref[0] + c) % 2
        store_pieces(out_ref, dot(rows_of_core(turned_ref, core, fsdp), residual_low).astype(BF16), 0)
        store_pieces(out_ref, rows_of_core(small_sum, core, fsdp), D)


def combine(experts, fsdp, *args):
    tok = args[1].shape[0]
    outs = [
        jax.ShapeDtypeStruct((tok, D), BF16),
        jax.ShapeDtypeStruct((tok, D), F32),
        jax.ShapeDtypeStruct((tok, D), BF16),
        jax.ShapeDtypeStruct((tok, LANES), F32),
    ] + piece_shapes(D + LANES, experts)
    return pl.pallas_call(
        functools.partial(combine_kernel, experts, fsdp),
        in_specs=[pl.BlockSpec(memory_space=pltpu.SMEM)] + whole_specs(args),
        out_specs=whole_specs(outs),
        out_shape=outs,
        scratch_shapes=[pltpu.VMEM((D, tok), BF16), pltpu.VMEM((D, LANES), BF16)],
        compiler_params=vmem(56),
        cost_estimate=cost(2 * tok * D * (2 * D + 3 * experts * CAP), 14 << 20, weight=LATE),
        name="combine",
    )(core_number(), *args)


def normed_grad_kernel(sizes, *refs):
    grads = refs[: 3 * len(sizes)]
    w_ref, *outs = refs[3 * len(sizes) :]
    step = pl.program_id(0)
    last = pl.num_programs(0) - 1

    def part(kind):
        total, at = None, kind * D
        for i, size in enumerate(sizes):
            term = dot_nt(grads[3 * i + kind][...], w_ref[:, at : at + size])
            total = term if total is None else total + term
            at += size
        return total

    grad = part(1) + part(2)

    for i, ref in enumerate(outs[:-1]):

        @pl.when(step == i)
        def _(ref=ref):
            ref[...] = grad.astype(BF16)

    @pl.when(step == last)
    def _():
        outs[-1][...] = grad + part(0)


def normed_grad(parts, weights):
    sizes = [p[0].shape[1] for p in parts]
    tok, span = parts[0][0].shape[0], parts[0][1].shape[0]
    blocks = span // tok
    fixed = lambda s: (0, 0)
    moving = lambda s: (s, 0)
    specs = []
    for size in sizes:
        specs += [pl.BlockSpec((tok, size), fixed)] + [pl.BlockSpec((tok, size), moving)] * 2
    return pl.pallas_call(
        functools.partial(normed_grad_kernel, sizes),
        grid=(blocks,),
        in_specs=specs + [pl.BlockSpec(weights.shape, fixed)],
        out_specs=[pl.BlockSpec((tok, D), fixed)] * blocks,
        out_shape=[jax.ShapeDtypeStruct((tok, D), BF16)] * (blocks - 1)
        + [jax.ShapeDtypeStruct((tok, D), F32)],
        compiler_params=vmem(24),
        cost_estimate=cost(4 * span * D * D, 16 << 20, weight=LATE),
        name="normed_grad",
    )(*in_vmem(*[g for p in parts for g in p]), weights)


def turn_kernel(x_ref, out_ref):
    out_ref[...] = x_ref[...].T


def turn(x):
    return pl.pallas_call(
        turn_kernel,
        in_specs=whole_specs(range(1)),
        out_specs=pl.BlockSpec(memory_space=pltpu.VMEM),
        out_shape=jax.ShapeDtypeStruct(x.shape[::-1], x.dtype),
        compiler_params=vmem(24),
        cost_estimate=cost(0, 8 << 20),
        name="turn",
    )(x)


def project_grad_kernel(count, core_ref, normed_ref, dq_ref, dk_ref, dv_ref, out_ref):
    own = normed_ref.shape[1] - dq_ref.shape[0]
    turned = rows_of_core(normed_ref, core_ref[0], count)
    for kind, ref in enumerate((dq_ref, dk_ref, dv_ref)):
        left = turned[:, own:] if kind == 0 else turned
        store_pieces(out_ref, dot(left, ref[...]).astype(BF16), kind * D)


def project_grad(core, normed_turned, grads, parts, count):
    span = normed_turned.shape[1]
    out = piece_shapes(3 * D, parts)[0]
    return pl.pallas_call(
        functools.partial(project_grad_kernel, count),
        in_specs=[pl.BlockSpec(memory_space=pltpu.SMEM)] + whole_specs(range(4)),
        out_specs=pl.BlockSpec(memory_space=pltpu.VMEM),
        out_shape=out,
        compiler_params=vmem(24),
        cost_estimate=cost(2 * span * D * D, 8 << 20, weight=LATE),
        name="project_grad",
    )(core, normed_turned, *in_vmem(*grads))


def after(x, *others):
    return lax.optimization_barrier((x, others))[0]


class Sequence:
    def __init__(self):
        self.last = ()

    def take(self, *values):
        return lax.optimization_barrier((values, self.last))[0]

    def done(self, *values):
        self.last = values


def folded(count):
    return [0] + list(range(1, count, 2)) + list(range(2, count, 2))[::-1]


def siblings(count):
    return [(i, i ^ 1) for i in range(count)]


def ring_gather(x, count, gates):
    chips = count // 2
    order = folded(chips)
    follow = {order[i]: order[(i + 1) % chips] for i in range(chips)}
    pairs = [(2 * z + c, 2 * follow[z] + c) for z in range(chips) for c in range(2)]
    me = lax.axis_index("fsdp")
    chip, core = me // 2, me % 2
    at = jnp.array([order.index(z) for z in range(chips)], jnp.int32)[chip]
    ring = jnp.array(order, jnp.int32)
    chunks, places = [], []
    current = x
    for k in range(chips):
        source = ring[(at - k) % chips]
        chunks += [current, lax.ppermute(current, "fsdp", siblings(count))]
        places += [2 * source + core, 2 * source + 1 - core]
        if k + 1 < chips:
            if 0 < k <= len(gates) and gates[k - 1]:
                current = after(current, *gates[k - 1])
            current = lax.ppermute(current, "fsdp", pairs)
    return chunks, jnp.stack(places).astype(jnp.int32)


def earlier_rows(x, count, others):
    up = [(i, i + 2) for i in range(count - 2)]
    second = lax.ppermute(x, "fsdp", up)
    core = lax.axis_index("fsdp") % 2
    first = after(jnp.where(core == 0, x, second), *others)
    first = lax.ppermute(first, "fsdp", siblings(count))
    return second, first


def return_send(second, across, count):
    core = lax.axis_index("fsdp") % 2
    across = across.astype(F32)
    total = jnp.where(core == 0, second.astype(F32), second.astype(F32) + across).astype(BF16)
    down = [(i + 2, i) for i in range(count - 2)]
    return lax.ppermute(total, "fsdp", down), jnp.where(core == 0, across, 0.0).astype(BF16), total


def quarter_gather(x, experts, count):
    chips = count // 2
    rows, width = x.shape
    each = width // experts
    me, group = lax.axis_index("fsdp"), lax.axis_index("expert")
    chip, core = me // 2, me % 2
    mine = lax.dynamic_slice_in_dim(x, group * each, each, 1)
    fetched = [mine]
    for k in range(1, chips):
        pairs = [(2 * z + c, 2 * ((z + k) % chips) + c) for z in range(chips) for c in range(2)]
        fetched.append(lax.ppermute(mine, "fsdp", pairs))
    stacked = jnp.stack(fetched)
    terms = plane_all(stacked, experts)
    chunks, columns = [], []
    for k in range(experts):
        here = after(terms[0], terms[-1]) if k == 0 else terms[k]
        chunks += [terms[k], sibling(here, count)]
        columns.append(group ^ k)
    blocks = []
    for k in range(chips):
        source = (chip - k) % chips
        blocks += [2 * source + core, 2 * source + 1 - core]
    places = [jnp.stack(p).astype(jnp.int32) for p in (blocks, columns)]
    return chunks, places, stacked


def sibling(x, count):
    return lax.ppermute(x, "fsdp", siblings(count))


def summed(terms):
    total = terms[0].astype(F32)
    for term in terms[1:]:
        total += term.astype(F32)
    return total.astype(BF16)


def in_plane(x):
    return lax.all_to_all(x, "expert", split_axis=0, concat_axis=0, tiled=True)


def plane_send(mine, other, experts):
    group = lax.axis_index("expert")

    def part(k):
        pair = [lax.dynamic_index_in_dim(x, group ^ k, 0, False) for x in (mine, other)]
        return summed(pair)

    parts = [part(k) for k in range(experts)]
    moved = [
        lax.ppermute(parts[k], "expert", [(i, i ^ k) for i in range(experts)])
        for k in range(1, experts)
    ]
    return parts[:1] + moved, parts


def line_send(pair, count):
    chips = count // 2
    chip = lax.axis_index("fsdp") // 2
    pair = [x.reshape(chips, x.shape[-2] // chips, x.shape[-1]) for x in pair]

    def part(k):
        at = (chip + k) % chips
        return summed([lax.dynamic_index_in_dim(x, at, 0, False) for x in pair])

    parts = [part(k) for k in range(chips)]
    moved = []
    for k in range(1, chips):
        pairs = [(2 * z + c, 2 * ((z + k) % chips) + c) for z in range(chips) for c in range(2)]
        moved.append(lax.ppermute(parts[k], "fsdp", pairs))
    return parts[:1] + moved, parts


def plane_all(x, experts):
    terms = [x]
    for k in range(1, experts):
        terms.append(lax.ppermute(x, "expert", [(i, i ^ k) for i in range(experts)]))
    return terms


def plane_columns(terms):
    experts = len(terms)
    terms = jnp.stack(terms)
    group = lax.axis_index("expert")
    parts = [lax.dynamic_index_in_dim(terms, j ^ group, 0, False) for j in range(experts)]
    return jnp.concatenate(parts, axis=1).astype(F32)


def plane_sum(terms):
    terms = [t.astype(F32) for t in terms]
    while len(terms) > 1:
        terms = [terms[i] + terms[i + 1] for i in range(0, len(terms), 2)]
    return terms[0]


def local(
    tokens,
    past_logits,
    routes,
    lengths,
    projector,
    collector,
    router,
    blender,
    constants,
    first_gain,
    second_gain,
    carryover,
    gating,
    upward,
    downward,
    cotangent,
):
    tok = tokens.shape[0]
    experts = lax.axis_size("expert")
    count = lax.axis_size("fsdp")
    names = experts + 4
    hops = WINDOW // tok
    me = lax.axis_index("fsdp")

    shard = projector.shape[0]
    gap = LANES - names - 8
    small = jnp.concatenate(
        [router, blender, constants, jnp.zeros((shard, gap), BF16)]
        + [first_gain[:, None], second_gain[:, None]],
        axis=1,
    )
    width = 3 * D + LANES
    filler = jnp.zeros((shard, -width % (experts * LANES)), BF16)
    shared = jnp.concatenate([projector, small, filler], axis=1)
    chunks, (blocks_at, columns_at), stacked = quarter_gather(shared, experts, count)
    own = jnp.concatenate([gating[0], upward[0], downward[0]], axis=1)
    second, first = earlier_rows(tokens, count, chunks[0::2])
    collector_all = lax.all_gather(collector, "fsdp", axis=0, tiled=True)

    span = tok + WINDOW
    key_positions = (me - hops) * tok + jnp.arange(span, dtype=jnp.int32)
    cosine, sine = rope_tables(key_positions.astype(F32))
    bounds = jnp.cumsum(lengths[0])
    biases = []
    for t in range(tok // QTILE):
        at = me * tok + t * QTILE + jnp.arange(QTILE, dtype=jnp.int32)
        start = jnp.max(jnp.where(bounds[:, None] <= at[None, :], bounds[:, None], 0), axis=0)
        least = jnp.maximum(at - (WINDOW - 1), start)
        keys_at = key_positions[t * QTILE : t * QTILE + SPAN, None]
        inside = (keys_at >= least[None, :]) & (keys_at <= at[None, :])
        biases.append(jnp.where(inside, 0.0, masked_score).astype(F32))
    bias = jnp.stack(biases)
    onehot = (routes[:, :, None] == jnp.arange(experts, dtype=jnp.int32)).astype(BF16)
    per_token = jnp.sum(onehot, axis=1)
    lower = jnp.tril(jnp.ones((tok, tok), BF16), -1)
    before = jnp.dot(lower, per_token, preferred_element_type=F32)
    position_in = jnp.sum(onehot.astype(F32) * before[:, None, :], axis=2).astype(jnp.int32)
    slots = jnp.where(routes < experts, routes * CAP + position_in, experts * CAP)
    past_part = jnp.dot(
        past_logits, carryover, precision=lax.Precision.HIGHEST, preferred_element_type=F32
    )
    past_part = jnp.pad(past_part, ((0, 0), (0, LANES - names)))
    past_wide = jnp.pad(past_logits, ((0, 0), (0, LANES - names)))
    carry_wide = jnp.pad(carryover, ((0, LANES - names), (0, LANES - names)))

    weights, small_all, normed_all, q, k, v = project(
        blocks_at, columns_at, chunks, [second, first, tokens], cosine, sine
    )
    half = 4
    att_a, lse_a = attend(q, k, v, bias, 0, half)
    att_b, lse_b = attend(q, k, v, bias, half, PAIRS - half)
    lse = jnp.concatenate([lse_a, lse_b], axis=0)
    attended, residual, hidden, aux, send = route(
        experts, att_a, att_b, collector_all, tokens, cotangent, small_all, past_part, routes, slots.T
    )

    def exchange(x):
        x = x.reshape(experts, CAP, 2 * D)
        x = lax.all_to_all(x, "expert", split_axis=0, concat_axis=0, tiled=True)
        return x.reshape(experts * CAP, 2 * D)

    weight_chunks, weight_places = ring_gather(own, count, [[q], [send]])
    arrived = exchange(send)
    answers, low = expert_rows(arrived, weight_places, weight_chunks)
    returned = exchange(answers)
    sums = expert_sums(arrived, low)
    sums = lax.psum_scatter(sums, "fsdp", scatter_dimension=0, tiled=True)

    layer_output, residual_grad, attended_grad, logits_grad, *col_grad = combine(
        experts, count, returned, residual, hidden, cotangent, aux, small_all, collector_all,
        attended, past_wide, carry_wide, routes, slots,
    )
    def back(upstream):
        return attend_back(q, k, v, attended, upstream, lse, bias, cosine, sine)

    normed_turned = turn(after(normed_all, send))
    col_mine, col_theirs = col_grad
    core = core_number()
    seq = Sequence()
    col_other = sibling(col_theirs, count)
    grads = back(attended_grad)
    seq.done(grads)
    (col_other,) = seq.take(col_other)
    col_terms, parts = plane_send(col_mine, col_other, experts)
    seq.done(parts)
    (turned,) = seq.take(normed_turned)
    theirs = project_grad(1 - core, turned, grads, experts, count)
    other = sibling(theirs, count)
    seq.done(theirs)
    (again,) = seq.take(weights)
    *halo_grads, own_grad = normed_grad([grads], again)
    across = sibling(halo_grads[1], count)
    seq.done(own_grad)
    (turned,) = seq.take(normed_turned)
    mine = project_grad(core, turned, grads, experts, count)
    seq.done(mine)
    (other,) = seq.take(other)
    terms, parts = plane_send(mine, other, experts)
    seq.done(parts)
    (across,) = seq.take(across)
    after_rows, across, total = return_send(halo_grads[0], across, count)
    seq.done(total)
    (col_terms,) = seq.take(col_terms)
    col_part = summed(col_terms)
    seq.done(col_part)
    (terms,) = seq.take(terms)
    merged = jnp.concatenate([summed(terms), col_part], axis=1)
    cut = mine.shape[2]
    terms, parts = line_send([merged], count)
    seq.done(parts)
    (sums,) = seq.take(sums)
    sums = sums.astype(F32)
    seq.done(sums)
    (terms,) = seq.take(terms)
    merged = summed(terms)
    terms = plane_all(merged, experts)
    seq.done(merged)
    (after_rows,) = seq.take(after_rows)
    own_grad = own_grad + across.astype(F32) + after_rows.astype(F32)
    tokens_wide = tokens.astype(F32)
    first_scale = norm_scale(tokens_wide)
    scaled = own_grad * small_all[:, LANES - 2].astype(F32)
    gradient_tokens = (
        residual_grad
        + first_scale * scaled
        - tokens_wide
        * (first_scale * first_scale * first_scale)
        * jnp.mean(scaled * tokens_wide, axis=-1, keepdims=True)
    ).astype(BF16)
    seq.done(gradient_tokens)
    (terms,) = seq.take(terms)
    projector_rows = plane_columns([t[:, :cut] for t in terms])[:, : 3 * D]
    col_rows = plane_columns([t[:, cut:] for t in terms])
    first_rows = jnp.sum(projector.astype(F32) * projector_rows, axis=1) / first_gain.astype(F32)

    return (
        layer_output,
        gradient_tokens,
        logits_grad[:, :names],
        projector_rows,
        col_rows[:, :D],
        col_rows[:, D : D + names],
        col_rows[:, D + names : D + names + 4],
        col_rows[:, D + names + 4 : D + names + 6],
        first_rows,
        col_rows[:, D + LANES - 1],
        col_rows[:names, D + names + 6 : D + 2 * names + 6],
        sums[:, :FF][None],
        sums[:, FF : 2 * FF][None],
        sums[:, 2 * FF :][None],
    )


def solution(mesh):
    rows = P(("expert", "fsdp"), None)
    shared = P("fsdp", None)
    expert = P("expert", "fsdp", None)
    return jax.shard_map(
        local,
        mesh=mesh,
        in_specs=(
            rows, rows, rows, P("expert", None), shared, shared, shared, shared, shared,
            P("fsdp"), P("fsdp"), P(), expert, expert, expert, rows,
        ),
        out_specs=(
            rows, rows, rows, shared, shared, shared, shared, shared,
            P("fsdp"), P("fsdp"), P(), expert, expert, expert,
        ),
        check_vma=False,
    )
```
